32 devices in a mesh: group: 8 (over z, y), fold: 4 (over x, core).
Axes of the slice: x: 2, y: 2, z: 4, core: 2. Of those that a mesh axis runs over, the one named last changes fastest.
Arguments:
- right_side: float32 [16, 131072], P(None, ('group', 'fold')), may hold values from -6 to 6
- initial: float32 [16, 131072], P(None, ('group', 'fold')), may hold values from -6 to 6
- counts: int32 [8, 4], P('group'), may hold values from 1 to 4096, 8192 in all within a row
- columns: int32 [512, 5], P('group'), may hold values from 0 to 69, as said below
- blocks: float32 [512, 5, 128, 128], P('group')
Outputs:
- smoothed: float32 [16, 131072], P(None, ('group', 'fold'))
The draws below stay inside these ranges and needn't reach their ends.
Inputs may be any that keep to these rules, and one draw needn't show every extreme that they name: Every row of counts sums to 8192, and its largest entry is 4096. `columns`: index j of row block g * 64 + i names block g * 64 + j - 3; the 5 indices of a row block are distinct and lie within 3 of i + 3.
All inputs are finite; a program needn't handle non-finite values.
Results may differ from the reference program's by a relative error of at most 0.0001.
Values sent between devices are 32-bit elements; how exact they have to be, the bound alone decides.
No kernel may reach another device: no remote copies, remote signals or barrier semaphores. Data moves between devices by JAX's collectives and lax.ppermute only.
A program may use at most 192 MiB of HBM per device.

```python
import math
import jax
import jax.numpy as jnp
import numpy as np
from jax import lax

NV = 16
BLOCK = 128
KB = 5
HB = 3
SWEEPS = 3
DEGREE = 4
OB = 64
OWN = 8192
NB = 512
ROWS = 65536
CAP = 4096
SLOTS = 131072
N_GROUP = 8
N_FOLD = 4


def draw_columns(key, part):
    local_ids = jnp.arange(NB, dtype=jnp.int32) % OB
    nearby = 2 * (HB - 1)
    candidates = jnp.concatenate([jnp.arange(-(HB - 1), 0, dtype=jnp.int32), jnp.arange(1, HB, dtype=jnp.int32)])
    scores = jax.random.randint(key, (NB, nearby), 0, 1 << 20, dtype=jnp.int32) * nearby + jnp.arange(nearby, dtype=jnp.int32)[None, :]
    ordering = jnp.argsort(scores, axis=1, stable=True)
    chosen = candidates[ordering[:, :KB - 3]]
    fixed_part = jnp.stack([jnp.zeros((NB,), jnp.int32), jnp.full((NB,), -HB, jnp.int32), jnp.full((NB,), HB, jnp.int32)], axis=1)
    offsets = jnp.concatenate([fixed_part, chosen.astype(jnp.int32)], axis=1)
    return (local_ids[:, None] + HB + offsets).astype(jnp.int32)


def draw_blocks(key, part):
    noise_key, diag_key = jax.random.split(key)
    shape = (NB, KB, BLOCK, BLOCK)
    scale = 0.45 / (KB * BLOCK) ** 0.5
    noise = jax.random.normal(noise_key, shape, jnp.float32) * scale
    diag_values = jnp.exp(jax.random.uniform(diag_key, (NB, BLOCK), jnp.float32, jnp.log(0.5), jnp.log(4.0)))
    slot_zero = (jnp.arange(KB) == 0)[None, :, None, None]
    on_diagonal = (jnp.arange(BLOCK)[:, None] == jnp.arange(BLOCK)[None, :])[None, None, :, :]
    identity = jnp.logical_and(slot_zero, on_diagonal).astype(jnp.float32)
    return (noise * (1.0 - identity) + identity * diag_values[:, None, :, None]).astype(jnp.float32)


def level_of(own_key, dims, cuts, smallest, largest):
    gain = 1.0
    for position, blocks in cuts:
        heights = jax.random.uniform(jax.random.fold_in(jax.random.fold_in(own_key, 6), position), (blocks,), jnp.float32, smallest / len(cuts), largest / len(cuts))
        gain = gain * jnp.repeat(jnp.exp(heights), dims[position] // blocks).reshape((-1,) + (1,) * (len(dims) - 1 - position))
    return gain


def split_up(count, total, most, slope):
    weights = [(1 << 20) // math.isqrt(rank ** slope) + 1 for rank in range(2, count + 1)]
    surplus, holding = total - most - (count - 1), [1] * (count - 1)
    while surplus > 0:
        movable = [i for i in range(count - 1) if holding[i] < most]
        pool, budget = sum([weights[i] for i in movable]), surplus
        for i in movable:
            extra = min(most - holding[i], max(1, budget * weights[i] // pool), surplus)
            holding[i] = holding[i] + extra
            surplus = surplus - extra
    return np.array([most] + holding)


def ragged_sizes(stream_key, number_of, total, bound, lean):
    if number_of == 2:
        one = jax.random.randint(stream_key, (), max(1, total - bound), min(bound, total - 1) + 1)
        return jnp.stack([one, total - one])
    lengths = jnp.asarray(split_up(number_of, total, bound, lean), jnp.int32)
    twos = (number_of - 1) // 2
    source_of, sink = lengths[1:1 + 2 * twos:2], lengths[2:2 + 2 * twos:2]
    room = jnp.minimum(source_of - 1, bound - sink)
    shifted = jax.random.randint(jax.random.fold_in(stream_key, 1), (twos,), 0, 1 << 20) % (room + 1)
    lengths = lengths.at[1:1 + 2 * twos:2].set(source_of - shifted).at[2:2 + 2 * twos:2].set(sink + shifted)
    return lengths[jax.random.permutation(jax.random.fold_in(stream_key, 2), number_of)]


def scatter_about(key, extent, deviation, most, pieces=(), held_as=jnp.bfloat16):
    values = deviation * jax.random.normal(key, extent, jnp.float32)
    if pieces:
        values = values * level_of(key, extent, pieces, -0.22, 0.18)
    return jnp.clip(values, -most, most).astype(held_as)


def setup_inputs(seed: int = 0) -> dict:
    keys = jax.random.split(jax.random.key(seed), 6)
    right_side = scatter_about(keys[0], (NV, SLOTS), 1.0, 6.0, ((1, 32),), jnp.float32)
    initial = scatter_about(keys[1], (NV, SLOTS), 1.0, 6.0, ((1, 32),), jnp.float32)
    counts = jax.vmap(lambda own: ragged_sizes(own, N_FOLD, OWN, CAP, 2))(jax.random.split(keys[2], N_GROUP)).reshape((N_GROUP, N_FOLD)).astype(jnp.int32)
    columns = draw_columns(jax.random.fold_in(keys[5], 71), 0)
    blocks = draw_blocks(jax.random.fold_in(keys[5], 71), 0)
    return {"right_side": right_side, "initial": initial, "counts": counts, "columns": columns, "blocks": blocks}


upper_bound = 4.5
lower_bound = 1.35


def slot_sources(counts):
    starts = jnp.cumsum(counts, axis=1) - counts
    row_ids = jnp.arange(OWN, dtype=jnp.int32)
    owner_slot = jnp.sum((starts[:, None, :] <= row_ids[None, :, None]).astype(jnp.int32), axis=2) - 1
    row_start = jnp.take_along_axis(starts, owner_slot, axis=1)
    group_ids = jnp.arange(N_GROUP, dtype=jnp.int32)[:, None]
    source = (group_ids * N_FOLD + owner_slot) * CAP + row_ids[None, :] - row_start
    return source.reshape(-1).astype(jnp.int32), starts


def operate(vector, columns, blocks):
    padding = jnp.zeros((NV, HB * BLOCK), jnp.float32)
    extended = jnp.concatenate([padding, vector, padding], axis=1).reshape(NV, NB + 2 * HB, BLOCK)
    base = (jnp.arange(NB, dtype=jnp.int32) // OB * OB).astype(jnp.int32)
    global_ids = (base[:, None] + columns).astype(jnp.int32)
    picked = extended[:, global_ids, :]
    result = jnp.einsum("nikc,ikrc->nir", picked, blocks, precision=lax.Precision.HIGHEST)
    return result.reshape(NV, ROWS)


def reference(right_side, initial, counts, columns, blocks):
    source, starts = slot_sources(counts)
    target = right_side[:, source]
    iterate = initial[:, source]
    theta = (upper_bound + lower_bound) / 2.0
    delta = (upper_bound - lower_bound) / 2.0
    for sweep in range(SWEEPS):
        resid = target - operate(iterate, columns, blocks)
        update = resid / theta
        ratio_now = delta / theta
        for step in range(DEGREE):
            iterate = iterate + update
            if step + 1 < DEGREE:
                resid = resid - operate(update, columns, blocks)
                ratio_next = 1.0 / (2.0 * theta / delta - ratio_now)
                update = ratio_next * ratio_now * update + (2.0 * ratio_next / delta) * resid
                ratio_now = ratio_next
    slot_ids = jnp.arange(SLOTS, dtype=jnp.int32)
    device_ids = slot_ids // CAP
    within = slot_ids % CAP
    group_ids = device_ids // N_FOLD
    fold_ids = device_ids % N_FOLD
    live_counts = counts[group_ids, fold_ids]
    row_start = starts[group_ids, fold_ids]
    clipped = jnp.minimum(within, live_counts - 1)
    target_rows = (group_ids * OWN + row_start + clipped).astype(jnp.int32)
    values = iterate[:, target_rows]
    return jnp.where((within < live_counts)[None, :], values, jnp.float32(0.0))
```

```python
import functools

import jax
import jax.numpy as jnp
from jax import lax
from jax.experimental import pallas as pl
from jax.experimental.pallas import tpu as pltpu
from jax.sharding import PartitionSpec as P

HB = 3
SWEEPS = 3
DEGREE = 4
APPLIES = SWEEPS * DEGREE

upper_bound = 4.5
lower_bound = 1.35

AXES = ("group", "fold")
F32 = jnp.float32
BF16 = jnp.bfloat16
VMEM = pl.BlockSpec(memory_space=pltpu.VMEM)
SMEM = pl.BlockSpec(memory_space=pltpu.SMEM)
ANY = pl.BlockSpec(memory_space=pl.ANY)


def coefficients():
    theta = (upper_bound + lower_bound) / 2.0
    delta = (upper_bound - lower_bound) / 2.0
    pairs = []
    for sweep in range(SWEEPS):
        pairs.append((0.0, 1.0 / theta))
        ratio = delta / theta
        for step in range(1, DEGREE):
            ratio_next = 1.0 / (2.0 * theta / delta - ratio)
            pairs.append((ratio_next * ratio, 2.0 * ratio_next / delta))
            ratio = ratio_next
    return pairs


def params(limit=40):
    return pltpu.CompilerParams(vmem_limit_bytes=limit * 2**20)


def split(value):
    high = value.astype(BF16)
    return high, (value - high.astype(F32)).astype(BF16)


def pick_lanes(window, low, shift):
    lane = lax.broadcasted_iota(jnp.int32, (16, 128), 1)
    turn = (128 - shift) % 128
    first = pltpu.roll(window(low), turn, 1)
    second = pltpu.roll(window(low + 1), turn, 1)
    return jnp.where(lane < 128 - shift, first, second)


def align_kernel(folds, ob, begin, extent, facts, *refs):
    sources, (x_out, u_out, r_out) = refs[:-3], refs[-3:]
    capacity = sources[0].shape[-1]
    lane = lax.broadcasted_iota(jnp.int32, (16, 128), 1)
    base = facts[0] * (ob * 128)
    x_out[...] = jnp.zeros_like(x_out)

    def block(e, carry):
        row = base + e * 128
        totals = [jnp.zeros((16, 128), F32), jnp.zeros((16, 128), F32)]
        for j in range(folds):
            start, count = facts[1 + j], facts[1 + folds + j]
            at = row - start
            low = at >> 7
            shift = at & 127
            index = at + lane
            valid = (index >= 0) & (index < count)
            for a, out in enumerate((1, 0)):

                def window(b, a=a, j=j):
                    b = jnp.clip(b, 0, capacity // 128 - 1)
                    return sources[j][a, :, pl.ds(pl.multiple_of(b * 128, 128), 128)]

                totals[out] = jnp.where(valid, pick_lanes(window, low, shift), totals[out])
        u_out[e] = totals[0]
        r_out[e] = totals[1]
        return carry

    lax.fori_loop(0, ob, block, 0, unroll=2)


def prepare_kernel(rows, halo, facts, blocks, out, raw, sem):
    own = blocks.shape[0]
    first = facts[0] * (rows - 2 * halo) - halo
    depth = raw.shape[0]

    def copy(a, slot):
        i = jnp.clip(first + a, 0, own - 1)
        return pltpu.make_async_copy(blocks.at[i], raw.at[slot], sem.at[slot])

    for a in range(depth - 1):
        copy(a, a).start()

    def row(a, carry):
        slot = a % depth
        copy(a, slot).wait()

        @pl.when(a + depth - 1 < rows)
        def _():
            copy(a + depth - 1, (a + depth - 1) % depth).start()

        for k in range(raw.shape[1]):
            high, low = split(raw[slot, k].T)
            out[a, k * 128 : (k + 1) * 128, :128] = high
            out[a, k * 128 : (k + 1) * 128, 128:] = low
        return carry

    lax.fori_loop(0, rows, row, 0)


def border_kernel(folds, rows, halo, facts, prepared, raw, out):
    del prepared
    fold = facts[0]

    @pl.when((fold == 0) | (fold == folds - 1))
    def _():
        first = jnp.where(fold == 0, 0, rows - halo)

        def row(a, carry):
            for k in range(raw.shape[1]):
                high, low = split(raw[a, k].T)
                out[first + a, k * 128 : (k + 1) * 128, :128] = high
                out[first + a, k * 128 : (k + 1) * 128, 128:] = low
            return carry

        lax.fori_loop(0, halo, row, 0)


def phase_kernel(ob, steps, pairs, last, facts, offsets, operator, x_in, u_in, r_in, got_a, got_b, *refs):
    h = HB * steps
    inner = h - HB
    extent = ob + 2 * h
    rows = ob + 2 * inner
    width = offsets.shape[0] // rows
    if last:
        x_out, u, r, pieces = refs
    else:
        x_out, u_out, r_out, pay_a, pay_b, u, r, pieces = refs
    even = facts[1] == 0
    for got, right in ((got_a, even), (got_b, jnp.logical_not(even))):
        u[pl.ds(jnp.where(right, h + ob, 0), h)] = got[:h]
        if inner:
            r[pl.ds(jnp.where(right, h + ob, HB), inner)] = got[h:]
    u[h : h + ob] = u_in[...]
    r[h : h + ob] = r_in[...]
    high, low = split(u[...])
    pieces[0, :, :16] = high
    pieces[0, :, 16:] = low
    x = x_in[...]
    for t in range(steps):
        x = x + u[h : h + ob]
        now, later = t % 2, (t + 1) % 2
        old, new = pairs[t]
        done = t == steps - 1

        def row(e, carry):
            a = e - HB
            left = jnp.concatenate([pieces[now, e + offsets[a * width + k]] for k in range(width)], axis=1)
            product = jnp.dot(left, operator[a], preferred_element_type=F32)
            product = product[:16] + product[16:]
            resid = r[e] - (product[:, :128] + product[:, 128:])
            r[e] = resid
            update = new * resid if old == 0.0 else old * u[e] + new * resid
            u[e] = update
            if not done:
                first, second = split(update)
                pieces[later, e, :16] = first
                pieces[later, e, 16:] = second
            return carry

        lower, upper = HB * (t + 1), extent - HB * (t + 1)
        lax.fori_loop(lower, upper, row, 0, unroll=True)
    if last:
        x_out[...] = x + u[h : h + ob]
        return
    x_out[...] = x
    u_out[...] = u[h : h + ob]
    r_out[...] = r[h : h + ob]
    for pay, right in ((pay_a, even), (pay_b, jnp.logical_not(even))):
        pay[:h] = u[pl.ds(jnp.where(right, h + ob - h, h), h)]
        if inner:
            pay[h:] = r[pl.ds(jnp.where(right, h + ob - inner, h), inner)]


def finish_kernel(ob, facts, *refs):
    parts, (out, whole) = refs[:-2], refs[-2:]
    total = whole.shape[0]
    for j, part in enumerate(parts):
        whole[pl.ds(facts[2 + j] * ob, ob)] = part[...]
    start, count = facts[0], facts[1]
    lane = lax.broadcasted_iota(jnp.int32, (16, 128), 1)
    low, shift = start >> 7, start & 127

    def block(b, carry):
        piece = pick_lanes(lambda i: whole[jnp.minimum(i, total - 1)], low + b, shift)
        piece = jnp.where(b * 128 + lane < count, piece, 0.0)
        out[:, pl.ds(pl.multiple_of(b * 128, 128), 128)] = piece
        return carry

    lax.fori_loop(0, out.shape[1] // 128, block, 0, unroll=4)


def collect(array, folds):
    held = {(0, 0): array}
    for d in range(1, folds // 2):
        held[d, 0] = lax.ppermute(array, "fold", [((i + 2 * d) % folds, i) for i in range(folds)])
    swap = [(i, i ^ 1) for i in range(folds)]
    for d in range(folds // 2):
        held[d, 1] = lax.ppermute(held[d, 0], "fold", swap)
    return held


def on_device(right_side, initial, counts, columns, blocks):
    groups, folds = lax.axis_size("group"), lax.axis_size("fold")
    vectors, capacity = right_side.shape
    own, width, side = blocks.shape[0], blocks.shape[1], blocks.shape[2]
    ob = own // folds
    steps = 3 if ob >= 9 else 2
    h = HB * steps
    inner = h - HB
    rows = ob + 2 * inner
    pairs = coefficients()
    fold = lax.axis_index("fold")
    me = lax.axis_index("group") * folds + fold
    devices = groups * folds

    last_fold = folds - 1
    border_perm = [(g * folds, (g + 1) * folds) for g in range(groups - 1)]
    border_perm += [((g + 1) * folds + last_fold, g * folds + last_fold) for g in range(groups - 1)]
    to_right = fold == 0
    outward = lax.dynamic_slice_in_dim(blocks, jnp.where(to_right, own - inner, 0), inner, 0)
    relative = columns - (jnp.arange(own, dtype=jnp.int32)[:, None] + HB)
    outward_relative = lax.dynamic_slice_in_dim(relative, jnp.where(to_right, own - inner, 0), inner, 0)
    border = lax.ppermute(outward, AXES, border_perm)
    border_relative = lax.ppermute(outward_relative, AXES, border_perm)

    around = jnp.concatenate([border_relative, relative, border_relative], axis=0)
    offsets = lax.dynamic_slice_in_dim(around, fold * ob, rows, 0).reshape(-1)

    facts = jnp.stack([fold, me % 2]).astype(jnp.int32)
    prepared = pl.pallas_call(
        functools.partial(prepare_kernel, rows, inner),
        out_shape=pltpu.VMEM((rows, width * side, 2 * side), BF16),
        in_specs=[SMEM, ANY],
        out_specs=VMEM,
        scratch_shapes=[pltpu.VMEM((4, width, side, side), F32), pltpu.SemaphoreType.DMA((4,))],
        compiler_params=params(),
        cost_estimate=pl.CostEstimate(flops=10**7, bytes_accessed=rows * width * side * side * 4, transcendentals=0),
    )(facts, blocks)
    operator = pl.pallas_call(
        functools.partial(border_kernel, folds, rows, inner),
        out_shape=pltpu.VMEM((rows, width * side, 2 * side), BF16),
        in_specs=[SMEM, VMEM, VMEM],
        out_specs=VMEM,
        input_output_aliases={1: 0},
        compiler_params=params(),
    )(facts, prepared, border)

    live = counts[0]
    starts = jnp.cumsum(live) - live
    stacked = jnp.stack([right_side, initial])
    held = collect(stacked, folds)
    keys = list(held)
    order = jnp.stack([((fold // 2 + d) % (folds // 2)) * 2 + ((fold % 2) ^ c) for d, c in keys]).astype(jnp.int32)
    align_facts = jnp.concatenate([fold[None].astype(jnp.int32), starts[order], live[order]])
    shape = jax.ShapeDtypeStruct((ob, vectors, side), F32)
    x, u, r = pl.pallas_call(
        functools.partial(align_kernel, folds, ob, 0, ob),
        out_shape=(shape, shape, shape),
        in_specs=[SMEM] + [VMEM] * folds,
        out_specs=(VMEM, VMEM, VMEM),
        compiler_params=params(),
    )(align_facts, *[held[k] for k in keys])

    even = me % 2 == 0

    def payload(right):
        at_u = jnp.where(right, ob - h, 0)
        at_r = jnp.where(right, ob - inner, 0)
        return jnp.concatenate([lax.dynamic_slice_in_dim(u, at_u, h, 0), lax.dynamic_slice_in_dim(r, at_r, inner, 0)])

    pay_a, pay_b = payload(even), payload(jnp.logical_not(even))
    swap_a = [(i, i ^ 1) for i in range(devices)]
    swap_b = [(i, i + 1) for i in range(1, devices - 1, 2)]
    swap_b += [(j, i) for i, j in swap_b]
    pay_shape = jax.ShapeDtypeStruct((2 * h - HB, vectors, side), F32)
    for phase in range(APPLIES // steps):
        got_b = lax.ppermute(pay_b, AXES, swap_b)
        got_a = lax.ppermute(pay_a, AXES, swap_a)
        last = (phase + 1) * steps == APPLIES
        outs = pl.pallas_call(
            functools.partial(phase_kernel, ob, steps, pairs[phase * steps : (phase + 1) * steps], last),
            out_shape=shape if last else (shape, shape, shape, pay_shape, pay_shape),
            in_specs=[SMEM, SMEM] + [VMEM] * 6,
            out_specs=VMEM if last else (VMEM,) * 5,
            scratch_shapes=[
                pltpu.VMEM((ob + 2 * h, vectors, side), F32),
                pltpu.VMEM((ob + 2 * h, vectors, side), F32),
                pltpu.VMEM((2, ob + 2 * h, 2 * vectors, side), BF16),
            ],
            compiler_params=params(),
        )(facts, offsets, pltpu.with_memory_space_constraint(operator, pltpu.VMEM), x, u, r, got_a, got_b)
        if last:
            x = outs
        else:
            x, u, r, pay_a, pay_b = outs

    held = collect(x, folds)
    start = jnp.sum(jnp.where(jnp.arange(folds) == fold, starts, 0))
    count = jnp.sum(jnp.where(jnp.arange(folds) == fold, live, 0))
    finish_facts = jnp.concatenate([jnp.stack([start, count]).astype(jnp.int32), order])
    return pl.pallas_call(
        functools.partial(finish_kernel, ob),
        out_shape=jax.ShapeDtypeStruct((vectors, capacity), F32),
        in_specs=[SMEM] + [VMEM] * folds,
        out_specs=VMEM,
        scratch_shapes=[pltpu.VMEM((own, vectors, side), F32)],
        compiler_params=params(),
    )(finish_facts, *[held[k] for k in keys])


def solution(mesh):
    placed = (
        P(None, AXES),
        P(None, AXES),
        P("group", None),
        P("group", None),
        P("group", None, None, None),
    )
    return jax.shard_map(on_device, mesh=mesh, in_specs=placed, out_specs=P(None, AXES), check_vma=False)
```

```python
import functools

import jax
import jax.numpy as jnp
from jax import lax
from jax.experimental import pallas as pl
from jax.experimental.pallas import tpu as pltpu
from jax.sharding import PartitionSpec as P

HB = 3
SWEEPS = 3
DEGREE = 4
APPLIES = SWEEPS * DEGREE

upper_bound = 4.5
lower_bound = 1.35

AXES = ("group", "fold")
F32 = jnp.float32
BF16 = jnp.bfloat16
VMEM = pl.BlockSpec(memory_space=pltpu.VMEM)
SMEM = pl.BlockSpec(memory_space=pltpu.SMEM)
ANY = pl.BlockSpec(memory_space=pl.ANY)


def coefficients():
    theta = (upper_bound + lower_bound) / 2.0
    delta = (upper_bound - lower_bound) / 2.0
    pairs = []
    for sweep in range(SWEEPS):
        pairs.append((0.0, 1.0 / theta))
        ratio = delta / theta
        for step in range(1, DEGREE):
            ratio_next = 1.0 / (2.0 * theta / delta - ratio)
            pairs.append((ratio_next * ratio, 2.0 * ratio_next / delta))
            ratio = ratio_next
    return pairs


def params(limit=40):
    return pltpu.CompilerParams(vmem_limit_bytes=limit * 2**20)


def split(value):
    high = value.astype(BF16)
    return high, (value - high.astype(F32)).astype(BF16)


def pick_lanes(window, low, shift):
    lane = lax.broadcasted_iota(jnp.int32, (16, 128), 1)
    turn = (128 - shift) % 128
    first = pltpu.roll(window(low), turn, 1)
    second = pltpu.roll(window(low + 1), turn, 1)
    return jnp.where(lane < 128 - shift, first, second)


def put_payloads(ob, steps, even, u, at, r, pay_a, pay_b):
    h = HB * steps
    inner = h - HB
    for pay, right in ((pay_a, even), (pay_b, jnp.logical_not(even))):
        pay[:h] = u[pl.ds(at + jnp.where(right, ob - h, 0), h)]
        if inner:
            pay[h:] = r[pl.ds(at + jnp.where(right, ob - inner, 0), inner)]


def begin_of(counts, j):
    total = 0
    for i in range(counts.shape[1]):
        total = total + jnp.where(i < j, counts[0, i], 0)
    return total


def holder(fold, folds, d, c):
    return jax.lax.rem(fold // 2 + d, folds // 2) * 2 + jnp.where(c, 1 - fold % 2, fold % 2)


def align_kernel(ob, steps, keys, facts, counts, *refs):
    sources, (x_out, u_out, r_out, pay_a, pay_b) = refs[:-5], refs[-5:]
    capacity = sources[0].shape[-1]
    folds = len(keys)
    lane = lax.broadcasted_iota(jnp.int32, (16, 128), 1)
    base = facts[0] * (ob * 128)
    x_out[...] = jnp.zeros_like(x_out)
    spans = []
    for d, c in keys:
        j = holder(facts[0], folds, d, c)
        spans.append((begin_of(counts, j), counts[0, j]))

    def block(e, carry):
        row = base + e * 128
        totals = [jnp.zeros((16, 128), F32), jnp.zeros((16, 128), F32)]
        for j, (start, count) in enumerate(spans):
            at = row - start
            low = at >> 7
            shift = at & 127
            index = at + lane
            valid = (index >= 0) & (index < count)
            for a in range(2):

                def window(b, source=sources[2 * j + a]):
                    b = jnp.clip(b, 0, capacity // 128 - 1)
                    return source[:, pl.ds(pl.multiple_of(b * 128, 128), 128)]

                totals[a] = jnp.where(valid, pick_lanes(window, low, shift), totals[a])
        u_out[e] = totals[0]
        r_out[e] = totals[1]
        return carry

    lax.fori_loop(0, ob, block, 0, unroll=2)
    put_payloads(ob, steps, facts[1] == 0, u_out, 0, r_out, pay_a, pay_b)


def prepare_kernel(ob, halo, facts, blocks, out, token, raw, sem):
    own, width, side = blocks.shape[0], blocks.shape[1], blocks.shape[2]
    rows = ob + 2 * halo
    first = facts[0] * ob - halo

    def copy(a):
        return pltpu.make_async_copy(blocks.at[jnp.clip(first + a, 0, own - 1)], raw.at[a], sem.at[a])

    for a in range(rows):
        copy(a).start()
    group = 4 if rows % 4 == 0 else 2

    def several(g, carry):
        for s in range(group):
            a = g * group + s
            copy(a).wait()
            for k in range(width):
                high, low = split(raw[a, k])
                out[a, k * side : (k + 1) * side, :side] = high.T
                out[a, k * side : (k + 1) * side, side:] = low.T
        return carry

    lax.fori_loop(0, rows // group, several, 0)
    token[...] = jnp.zeros_like(token)


def border_kernel(ob, folds, halo, piece, facts, prepared, raw, out):
    del prepared
    fold = facts[0]
    count, width, side = raw.shape[0], raw.shape[1], raw.shape[2]

    @pl.when((fold == 0) | (fold == folds - 1))
    def _():
        first = jnp.where(fold == 0, halo - count * (piece + 1), halo + ob + count * piece)
        for a in range(count):
            for k in range(width):
                high, low = split(raw[a, k])
                out[first + a, k * side : (k + 1) * side, :side] = high.T
                out[first + a, k * side : (k + 1) * side, side:] = low.T


def phase_kernel(ob, halo, steps, after, pairs, facts, offsets, operator, x_in, u_in, r_in, got_a, got_b, *refs):
    h = HB * steps
    inner = h - HB
    extent = ob + 2 * h
    width = offsets.shape[0] // (ob + 2 * halo)
    if after:
        x_out, u_out, r_out, pay_a, pay_b, u, r, *pieces = refs
    else:
        x_out, u, r, *pieces = refs
    even = facts[1] == 0
    for got, right in ((got_a, even), (got_b, jnp.logical_not(even))):
        u[pl.ds(jnp.where(right, h + ob, 0), h)] = got[:h]
        if inner:
            r[pl.ds(jnp.where(right, h + ob, HB), inner)] = got[h:]
    u[h : h + ob] = u_in[...]
    r[h : h + ob] = r_in[...]
    high, low = split(u[...])
    pieces[0][:, :16] = high
    pieces[0][:, 16:] = low
    x = x_in[...]
    for t in range(steps):
        x = x + u[h : h + ob]
        now, later = pieces[t % 2], pieces[(t + 1) % 2]
        old, new = pairs[t]
        done = t == steps - 1

        def row(e, carry):
            a = e - h + halo
            left = jnp.concatenate([now[e + offsets[a * width + k]] for k in range(width)], axis=1)
            product = jnp.dot(left, operator[a], preferred_element_type=F32)
            product = product[:16] + product[16:]
            resid = r[e] - (product[:, :128] + product[:, 128:])
            r[e] = resid
            update = new * resid if old == 0.0 else old * u[e] + new * resid
            u[e] = update
            if not done:
                first, second = split(update)
                later[e, :16] = first
                later[e, 16:] = second
            return carry

        lower, upper = HB * (t + 1), extent - HB * (t + 1)
        lax.fori_loop(lower, upper, row, 0, unroll=True)
    if not after:
        x_out[...] = x + u[h : h + ob]
        return
    x_out[...] = x
    u_out[...] = u[h : h + ob]
    r_out[...] = r[h : h + ob]
    put_payloads(ob, after, even, u, h, r, pay_a, pay_b)


def finish_kernel(ob, keys, facts, counts, *refs):
    parts, (out, whole) = refs[:-2], refs[-2:]
    total = whole.shape[0]
    for (d, c), part in zip(keys, parts):
        whole[pl.ds(holder(facts[0], len(keys), d, c) * ob, ob)] = part[...]
    start, count = begin_of(counts, facts[0]), counts[0, facts[0]]
    lane = lax.broadcasted_iota(jnp.int32, (16, 128), 1)
    low, shift = start >> 7, start & 127

    def block(b, carry):
        piece = pick_lanes(lambda i: whole[jnp.minimum(i, total - 1)], low + b, shift)
        piece = jnp.where(b * 128 + lane < count, piece, 0.0)
        out[:, pl.ds(pl.multiple_of(b * 128, 128), 128)] = piece
        return carry

    lax.fori_loop(0, out.shape[1] // 128, block, 0, unroll=8)


def over_chips(array, d, folds):
    return lax.ppermute(array, "fold", [((i + 2 * d) % folds, i) for i in range(folds)])


def other_core(array, folds):
    return lax.ppermute(array, "fold", [(i, i ^ 1) for i in range(folds)])


def on_device(right_side, initial, counts, columns, blocks):
    groups, folds = lax.axis_size("group"), lax.axis_size("fold")
    vectors, capacity = right_side.shape
    own, width, side = blocks.shape[0], blocks.shape[1], blocks.shape[2]
    ob = own // folds
    plan = [2, 3, 3, 4] if ob >= 12 else [2] * 6
    halo = HB * (max(plan) - 1)
    rows = ob + 2 * halo
    pairs = coefficients()
    fold = lax.axis_index("fold")
    me = lax.axis_index("group") * folds + fold
    devices = groups * folds
    facts = jnp.stack([fold, me % 2]).astype(jnp.int32)
    state = jax.ShapeDtypeStruct((ob, vectors, side), F32)

    def payload(steps):
        return jax.ShapeDtypeStruct((2 * HB * steps - HB, vectors, side), F32)

    near = (initial, right_side)
    far = [tuple(over_chips(array, d, folds) for array in near) for d in range(1, folds // 2)]

    last_fold = folds - 1
    border_perm = [(g * folds, (g + 1) * folds) for g in range(groups - 1)]
    border_perm += [((g + 1) * folds + last_fold, g * folds + last_fold) for g in range(groups - 1)]
    to_right = fold == 0
    borders = []
    for piece in range(halo // HB):
        at = jnp.where(to_right, own - HB * (piece + 1), HB * piece)
        borders.append(lax.ppermute(lax.dynamic_slice_in_dim(blocks, at, HB, 0), AXES, border_perm))
    relative = columns - (jnp.arange(own, dtype=jnp.int32)[:, None] + HB)
    outward = lax.dynamic_slice_in_dim(relative, jnp.where(to_right, own - halo, 0), halo, 0)
    outward = lax.ppermute(outward, AXES, border_perm)
    around = jnp.concatenate([outward, relative, outward], axis=0)
    offsets = lax.dynamic_slice_in_dim(around, fold * ob, rows, 0).reshape(-1)

    operator, token = pl.pallas_call(
        functools.partial(prepare_kernel, ob, halo),
        out_shape=(pltpu.VMEM((rows, width * side, 2 * side), BF16), jax.ShapeDtypeStruct((8, 128), F32)),
        in_specs=[SMEM, ANY],
        out_specs=(VMEM, VMEM),
        scratch_shapes=[pltpu.VMEM((rows, width, side, side), F32), pltpu.SemaphoreType.DMA((rows,))],
        compiler_params=params(),
        cost_estimate=pl.CostEstimate(flops=10**7, bytes_accessed=2 * rows * width * side * side * 4, transcendentals=0),
    )(facts, blocks)
    far, _ = lax.optimization_barrier((far, token))

    keys, arrays = [], []
    for d, pair in enumerate([near, *far]):
        keys += [(d, False), (d, True)]
        arrays += [*pair, *(other_core(array, folds) for array in pair)]
    x, u, r, pay_a, pay_b = pl.pallas_call(
        functools.partial(align_kernel, ob, plan[0], keys),
        out_shape=(state, state, state, payload(plan[0]), payload(plan[0])),
        in_specs=[SMEM, SMEM] + [VMEM] * (2 * folds),
        out_specs=(VMEM,) * 5,
        compiler_params=params(),
    )(facts, counts, *arrays)

    def with_border(operator, piece):
        return pl.pallas_call(
            functools.partial(border_kernel, ob, folds, halo, piece),
            out_shape=pltpu.VMEM((rows, width * side, 2 * side), BF16),
            in_specs=[SMEM, VMEM, VMEM],
            out_specs=VMEM,
            input_output_aliases={1: 0},
            compiler_params=params(),
        )(facts, pltpu.with_memory_space_constraint(operator, pltpu.VMEM), borders[piece])

    swap_a = [(i, i ^ 1) for i in range(devices)]
    swap_b = [(i, i + 1) for i in range(1, devices - 1, 2)]
    swap_b += [(j, i) for i, j in swap_b]
    there, done = 0, 0
    for phase, steps in enumerate(plan):
        got_b = lax.ppermute(pay_b, AXES, swap_b)
        got_a = lax.ppermute(pay_a, AXES, swap_a)
        while there < steps - 1:
            operator = with_border(operator, there)
            there += 1
        after = plan[phase + 1] if phase + 1 < len(plan) else 0
        outs = pl.pallas_call(
            functools.partial(phase_kernel, ob, halo, steps, after, pairs[done : done + steps]),
            out_shape=(state, state, state, payload(after), payload(after)) if after else state,
            in_specs=[SMEM, SMEM] + [VMEM] * 6,
            out_specs=(VMEM,) * 5 if after else VMEM,
            scratch_shapes=[
                pltpu.VMEM((ob + 2 * HB * steps, vectors, side), F32),
                pltpu.VMEM((ob + 2 * HB * steps, vectors, side), F32),
                pltpu.VMEM((ob + 2 * HB * steps, 2 * vectors, side), BF16),
                pltpu.VMEM((ob + 2 * HB * steps, 2 * vectors, side), BF16),
            ],
            compiler_params=params(),
        )(facts, offsets, pltpu.with_memory_space_constraint(operator, pltpu.VMEM), x, u, r, got_a, got_b)
        done += steps
        if after:
            x, u, r, pay_a, pay_b = outs
        else:
            x = outs

    parts = []
    for d in range(folds // 2):
        part = over_chips(x, d, folds) if d else x
        parts += [part, other_core(part, folds)]
    return pl.pallas_call(
        functools.partial(finish_kernel, ob, keys),
        out_shape=jax.ShapeDtypeStruct((vectors, capacity), F32),
        in_specs=[SMEM, SMEM] + [VMEM] * folds,
        out_specs=VMEM,
        scratch_shapes=[pltpu.VMEM((own, vectors, side), F32)],
        compiler_params=params(),
    )(facts, counts, *parts)


def solution(mesh):
    placed = (
        P(None, AXES),
        P(None, AXES),
        P("group", None),
        P("group", None),
        P("group", None, None, None),
    )
    return jax.shard_map(on_device, mesh=mesh, in_specs=placed, out_specs=P(None, AXES), check_vma=False)
```

```python
import functools

import jax
import jax.numpy as jnp
from jax import lax
from jax.experimental import pallas as pl
from jax.experimental.pallas import tpu as pltpu
from jax.sharding import PartitionSpec as P

HB = 3
SWEEPS = 3
DEGREE = 4
APPLIES = SWEEPS * DEGREE

upper_bound = 4.5
lower_bound = 1.35

AXES = ("group", "fold")
F32 = jnp.float32
BF16 = jnp.bfloat16
VMEM = pl.BlockSpec(memory_space=pltpu.VMEM)
SMEM = pl.BlockSpec(memory_space=pltpu.SMEM)
HBM = pl.BlockSpec(memory_space=pltpu.HBM)


def coefficients():
    theta = (upper_bound + lower_bound) / 2.0
    delta = (upper_bound - lower_bound) / 2.0
    pairs = []
    for sweep in range(SWEEPS):
        pairs.append((0.0, 1.0 / theta))
        ratio = delta / theta
        for step in range(1, DEGREE):
            ratio_next = 1.0 / (2.0 * theta / delta - ratio)
            pairs.append((ratio_next * ratio, 2.0 * ratio_next / delta))
            ratio = ratio_next
    return pairs


def params(limit=16):
    return pltpu.CompilerParams(vmem_limit_bytes=limit * 2**20)


def split(value):
    high = value.astype(BF16)
    return high, (value - high.astype(F32)).astype(BF16)


def pick_lanes(window, low, shift):
    lane = lax.broadcasted_iota(jnp.int32, (16, 128), 1)
    turn = (128 - shift) % 128
    first = pltpu.roll(window(low), turn, 1)
    second = pltpu.roll(window(low + 1), turn, 1)
    return jnp.where(lane < 128 - shift, first, second)


def put_payloads(ob, steps, even, u, at, r, pay_a, pay_b):
    h = HB * steps
    inner = h - HB
    for pay, right in ((pay_a, even), (pay_b, jnp.logical_not(even))):
        pay[:h] = u[pl.ds(at + jnp.where(right, ob - h, 0), h)]
        if inner:
            pay[h:] = r[pl.ds(at + jnp.where(right, ob - inner, 0), inner)]


def begin_of(counts, j):
    total = 0
    for i in range(counts.shape[1]):
        total = total + jnp.where(i < j, counts[0, i], 0)
    return total


def holder(fold, folds, d, c):
    return jax.lax.rem(fold // 2 + d, folds // 2) * 2 + jnp.where(c, 1 - fold % 2, fold % 2)


def align_kernel(ob, steps, keys, facts, counts, *refs):
    n = 2 * len(keys)
    sources, (u_out, r_out, pay_a, pay_b), windows, sem = refs[:n], refs[n : n + 4], refs[n + 4 : 2 * n + 4], refs[-1]
    capacity = sources[0].shape[-1]
    length = windows[0].shape[-1]
    folds = len(keys)
    lane = lax.broadcasted_iota(jnp.int32, (16, 128), 1)
    base = facts[0] * (ob * 128)
    spans, copies = [], []
    for j, (d, c) in enumerate(keys):
        owner = holder(facts[0], folds, d, c)
        start = begin_of(counts, owner)
        first = jnp.clip((base - start) >> 7, 0, (capacity - length) // 128)
        spans.append((start, counts[0, owner], first))
        for i in (2 * j, 2 * j + 1):
            source = sources[i].at[:, pl.ds(pl.multiple_of(first * 128, 128), length)]
            copies.append(pltpu.make_async_copy(source, windows[i], sem.at[i]))
    for copy in copies:
        copy.start()
    for copy in copies:
        copy.wait()

    def block(e, carry):
        row = base + e * 128
        totals = [jnp.zeros((16, 128), F32), jnp.zeros((16, 128), F32)]
        for j, (start, count, first) in enumerate(spans):
            at = row - start
            low = (at >> 7) - first
            shift = at & 127
            index = at + lane
            valid = (index >= 0) & (index < count)
            for a in range(2):

                def window(b, held=windows[2 * j + a]):
                    b = jnp.clip(b, 0, length // 128 - 1)
                    return held[:, pl.ds(pl.multiple_of(b * 128, 128), 128)]

                totals[a] = jnp.where(valid, pick_lanes(window, low, shift), totals[a])
        u_out[e] = totals[0]
        r_out[e] = totals[1]
        return carry

    lax.fori_loop(0, ob, block, 0, unroll=4)
    put_payloads(ob, steps, facts[1] == 0, u_out, 0, r_out, pay_a, pay_b)


def outward_kernel(folds, halo, facts, columns, blocks, *refs):
    *pieces, indices, sem = refs
    own, width = columns.shape
    fold = facts[0]

    def copies():
        for piece, out in enumerate(pieces):
            at = jnp.where(fold == 0, own - HB * (piece + 1), HB * piece)
            yield pltpu.make_async_copy(blocks.at[pl.ds(at, HB)], out, sem.at[piece])

    edge = (fold == 0) | (fold == folds - 1)

    @pl.when(edge)
    def _():
        for copy in copies():
            copy.start()

    for i in range(halo):
        at = jnp.where(fold < folds // 2, own - halo + i, i)
        for k in range(width):
            indices[i * width + k] = columns[at, k]

    @pl.when(edge)
    def _():
        for copy in copies():
            copy.wait()


def gate_kernel(n, *refs):
    del n, refs


def prepare_kernel(ob, halo, facts, columns, blocks, out, token, raw, sem):
    del columns
    own, width, side = blocks.shape[0], blocks.shape[1], blocks.shape[2]
    rows = ob + 2 * halo
    first = facts[0] * ob - halo

    def copy(a):
        return pltpu.make_async_copy(blocks.at[jnp.clip(first + a, 0, own - 1)], raw.at[a], sem.at[a])

    for a in range(rows):
        copy(a).start()
    group = 4 if rows % 4 == 0 else 2

    def several(g, carry):
        for s in range(group):
            a = g * group + s
            copy(a).wait()
            for k in range(width):
                high, low = split(raw[a, k])
                out[a, k * side : (k + 1) * side, :side] = high.T
                out[a, k * side : (k + 1) * side, side:] = low.T
        return carry

    lax.fori_loop(0, rows // group, several, 0)
    token[...] = jnp.zeros_like(token)


def border_kernel(ob, folds, halo, piece, facts, *refs):
    if piece:
        prepared, raw, out = refs
    else:
        columns, indices, prepared, raw, out, offsets = refs
    del prepared
    fold = facts[0]
    count, width, side = raw.shape[0], raw.shape[1], raw.shape[2]

    @pl.when((fold == 0) | (fold == folds - 1))
    def _():
        first = jnp.where(fold == 0, halo - count * (piece + 1), halo + ob + count * piece)
        for a in range(count):
            for k in range(width):
                high, low = split(raw[a, k])
                out[first + a, k * side : (k + 1) * side, :side] = high.T
                out[first + a, k * side : (k + 1) * side, side:] = low.T

    if piece:
        return
    own = columns.shape[0]

    def row(a, carry):
        i = fold * ob - halo + a
        inside = (i >= 0) & (i < own)
        outside = jnp.where(i < 0, i + halo, jnp.clip(i - own, 0, halo - 1))
        local = jnp.where(i < 0, i + own, jnp.where(inside, i, i - own))
        for k in range(width):
            theirs = indices[jnp.clip(outside, 0, halo - 1) * width + k]
            mine = columns[jnp.clip(i, 0, own - 1), k]
            offset = jnp.where(inside, mine, theirs) - HB - local
            offsets[a * width + k] = jnp.clip(offset, -HB, HB)
        return carry

    lax.fori_loop(0, ob + 2 * halo, row, 0, unroll=2)


def phase_kernel(ob, halo, steps, first, after, pairs, facts, offsets, operator, *refs):
    h = HB * steps
    inner = h - HB
    extent = ob + 2 * h
    width = offsets.shape[0] // (ob + 2 * halo)
    if not first:
        x_in, *refs = refs
    u_in, r_in, got_a, got_b, *refs = refs
    if after:
        x_out, u_out, r_out, pay_a, pay_b, u, r, *pieces = refs
    else:
        x_out, u, r, *pieces = refs
    even = facts[1] == 0
    for got, right in ((got_a, even), (got_b, jnp.logical_not(even))):
        u[pl.ds(jnp.where(right, h + ob, 0), h)] = got[:h]
        if inner:
            r[pl.ds(jnp.where(right, h + ob, HB), inner)] = got[h:]
    u[h : h + ob] = u_in[...]
    r[h : h + ob] = r_in[...]
    high, low = split(u[...])
    pieces[0][:, :16] = high
    pieces[0][:, 16:] = low
    x = None if first else x_in[...]
    for t in range(steps):
        x = u[h : h + ob] if x is None else x + u[h : h + ob]
        now, later = pieces[t % 2], pieces[(t + 1) % 2]
        old, new = pairs[t]
        done = t == steps - 1

        def row(e, carry):
            a = e - h + halo
            left = jnp.concatenate([now[e + offsets[a * width + k]] for k in range(width)], axis=1)
            product = jnp.dot(left, operator[a], preferred_element_type=F32)
            product = product[:16] + product[16:]
            resid = r[e] - (product[:, :128] + product[:, 128:])
            r[e] = resid
            update = new * resid if old == 0.0 else old * u[e] + new * resid
            u[e] = update
            if not done:
                big, small = split(update)
                later[e, :16] = big
                later[e, 16:] = small
            return carry

        lower, upper = HB * (t + 1), extent - HB * (t + 1)
        lax.fori_loop(lower, upper, row, 0, unroll=True)
    if not after:
        x_out[...] = x + u[h : h + ob]
        return
    x_out[...] = x
    u_out[...] = u[h : h + ob]
    r_out[...] = r[h : h + ob]
    put_payloads(ob, after, even, u, h, r, pay_a, pay_b)


def finish_kernel(ob, keys, facts, counts, *refs):
    parts, (out, whole) = refs[:-2], refs[-2:]
    total = whole.shape[0]
    for (d, c), part in zip(keys, parts):
        whole[pl.ds(holder(facts[0], len(keys), d, c) * ob, ob)] = part[...]
    start, count = begin_of(counts, facts[0]), counts[0, facts[0]]
    lane = lax.broadcasted_iota(jnp.int32, (16, 128), 1)
    low, shift = start >> 7, start & 127

    def block(b, carry):
        piece = pick_lanes(lambda i: whole[jnp.minimum(i, total - 1)], low + b, shift)
        piece = jnp.where(b * 128 + lane < count, piece, 0.0)
        out[:, pl.ds(pl.multiple_of(b * 128, 128), 128)] = piece
        return carry

    lax.fori_loop(0, out.shape[1] // 128, block, 0, unroll=8)


def over_chips(array, d, folds):
    return lax.ppermute(array, "fold", [((i + 2 * d) % folds, i) for i in range(folds)])


def other_core(array, folds):
    return lax.ppermute(array, "fold", [(i, i ^ 1) for i in range(folds)])


def on_device(right_side, initial, counts, columns, blocks):
    groups, folds = lax.axis_size("group"), lax.axis_size("fold")
    vectors, capacity = right_side.shape
    own, width, side = blocks.shape[0], blocks.shape[1], blocks.shape[2]
    ob = own // folds
    plan = [2, 3, 3, 4] if ob >= 12 else [2] * 6
    halo = HB * (max(plan) - 1)
    rows = ob + 2 * halo
    pairs = coefficients()
    fold = lax.axis_index("fold")
    me = lax.axis_index("group") * folds + fold
    devices = groups * folds
    facts = jnp.stack([fold, me % 2]).astype(jnp.int32)
    state = jax.ShapeDtypeStruct((ob, vectors, side), F32)

    def payload(steps):
        return jax.ShapeDtypeStruct((2 * HB * steps - HB, vectors, side), F32)

    near = (initial, right_side)
    far = [tuple(over_chips(array, d, folds) for array in near) for d in range(1, folds // 2)]

    last_fold = folds - 1
    border_perm = [(g * folds, (g + 1) * folds) for g in range(groups - 1)]
    border_perm += [((g + 1) * folds + last_fold, g * folds + last_fold) for g in range(groups - 1)]
    count = halo // HB
    fixed = pltpu.with_memory_space_constraint(blocks, pltpu.HBM)
    *borders, indices = pl.pallas_call(
        functools.partial(outward_kernel, folds, halo),
        out_shape=(pltpu.VMEM((HB, width, side, side), F32),) * count + (jax.ShapeDtypeStruct((halo * width,), jnp.int32),),
        in_specs=[SMEM, SMEM, HBM],
        out_specs=(VMEM,) * count + (SMEM,),
        scratch_shapes=[pltpu.SemaphoreType.DMA((count,))],
        compiler_params=params(),
    )(facts, columns, fixed)
    borders = [lax.ppermute(piece, AXES, border_perm) for piece in borders]
    index_perm = [(g * folds + 1, (g + 1) * folds) for g in range(groups - 1)]
    index_perm += [((g + 1) * folds + last_fold - 1, g * folds + last_fold) for g in range(groups - 1)]
    indices = lax.ppermute(indices, AXES, index_perm)

    operator, token = pl.pallas_call(
        functools.partial(prepare_kernel, ob, halo),
        out_shape=(pltpu.VMEM((rows, width * side, 2 * side), BF16), jax.ShapeDtypeStruct((8, 128), F32)),
        in_specs=[SMEM, SMEM, HBM],
        out_specs=(VMEM, VMEM),
        scratch_shapes=[pltpu.VMEM((rows, width, side, side), F32), pltpu.SemaphoreType.DMA((rows,))],
        compiler_params=params(32),
        cost_estimate=pl.CostEstimate(flops=10**7, bytes_accessed=2 * rows * width * side * side * 4, transcendentals=0),
    )(facts, columns, fixed)
    flat = [array for pair in far for array in pair]
    flat = pl.pallas_call(
        functools.partial(gate_kernel, len(flat)),
        out_shape=tuple(pltpu.HBM(array.shape, F32) for array in flat),
        in_specs=[HBM] * (len(flat) + 1),
        out_specs=(HBM,) * len(flat),
        input_output_aliases={i: i for i in range(len(flat))},
        compiler_params=params(),
    )(*[pltpu.with_memory_space_constraint(array, pltpu.HBM) for array in flat], token)
    far = [flat[2 * d : 2 * d + 2] for d in range(len(far))]

    keys, arrays = [], []
    for d, pair in enumerate([near, *far]):
        keys += [(d, False), (d, True)]
        arrays += [*pair, *(other_core(array, folds) for array in pair)]
    u, r, pay_a, pay_b = pl.pallas_call(
        functools.partial(align_kernel, ob, plan[0], keys),
        out_shape=(state, state, payload(plan[0]), payload(plan[0])),
        in_specs=[SMEM, SMEM] + [HBM] * (2 * folds),
        out_specs=(VMEM,) * 4,
        scratch_shapes=[pltpu.VMEM((vectors, (ob + 1) * side), F32)] * (2 * folds) + [pltpu.SemaphoreType.DMA((2 * folds,))],
        compiler_params=params(),
    )(facts, counts, *[pltpu.with_memory_space_constraint(array, pltpu.HBM) for array in arrays])

    def with_border(operator, piece):
        whole = pltpu.VMEM((rows, width * side, 2 * side), BF16)
        held = pltpu.with_memory_space_constraint(operator, pltpu.VMEM)
        return pl.pallas_call(
            functools.partial(border_kernel, ob, folds, halo, piece),
            out_shape=whole if piece else (whole, jax.ShapeDtypeStruct((rows * width,), jnp.int32)),
            in_specs=[SMEM, VMEM, VMEM] if piece else [SMEM, SMEM, SMEM, VMEM, VMEM],
            out_specs=VMEM if piece else (VMEM, SMEM),
            input_output_aliases={1: 0} if piece else {3: 0},
            compiler_params=params(),
        )(facts, *([] if piece else [columns, indices]), held, borders[piece])

    swap_a = [(i, i ^ 1) for i in range(devices)]
    swap_b = [(i, i + 1) for i in range(1, devices - 1, 2)]
    swap_b += [(j, i) for i, j in swap_b]
    there, done = 0, 0
    for phase, steps in enumerate(plan):
        got_b = lax.ppermute(pay_b, AXES, swap_b)
        got_a = lax.ppermute(pay_a, AXES, swap_a)
        while there < steps - 1:
            if there:
                operator = with_border(operator, there)
            else:
                operator, offsets = with_border(operator, 0)
            there += 1
        after = plan[phase + 1] if phase + 1 < len(plan) else 0
        outs = pl.pallas_call(
            functools.partial(phase_kernel, ob, halo, steps, phase == 0, after, pairs[done : done + steps]),
            out_shape=(state, state, state, payload(after), payload(after)) if after else state,
            in_specs=[SMEM, SMEM] + [VMEM] * (6 if phase else 5),
            out_specs=(VMEM,) * 5 if after else VMEM,
            scratch_shapes=[
                pltpu.VMEM((ob + 2 * HB * steps, vectors, side), F32),
                pltpu.VMEM((ob + 2 * HB * steps, vectors, side), F32),
                pltpu.VMEM((ob + 2 * HB * steps, 2 * vectors, side), BF16),
                pltpu.VMEM((ob + 2 * HB * steps, 2 * vectors, side), BF16),
            ],
            compiler_params=params(),
        )(facts, offsets, pltpu.with_memory_space_constraint(operator, pltpu.VMEM), *([x] if phase else []), u, r, got_a, got_b)
        done += steps
        if after:
            x, u, r, pay_a, pay_b = outs
        else:
            x = outs

    parts = []
    for d in range(folds // 2):
        part = over_chips(x, d, folds) if d else x
        parts += [part, other_core(part, folds)]
    return pl.pallas_call(
        functools.partial(finish_kernel, ob, keys),
        out_shape=jax.ShapeDtypeStruct((vectors, capacity), F32),
        in_specs=[SMEM, SMEM] + [VMEM] * folds,
        out_specs=VMEM,
        scratch_shapes=[pltpu.VMEM((own, vectors, side), F32)],
        compiler_params=params(),
    )(facts, counts, *parts)


def solution(mesh):
    placed = (
        P(None, AXES),
        P(None, AXES),
        P("group", None),
        P("group", None),
        P("group", None, None, None),
    )
    return jax.shard_map(on_device, mesh=mesh, in_specs=placed, out_specs=P(None, AXES), check_vma=False)
```

```python
import functools

import jax
import jax.numpy as jnp
from jax import lax
from jax.experimental import pallas as pl
from jax.experimental.pallas import tpu as pltpu
from jax.sharding import PartitionSpec as P

HB = 3
SWEEPS = 3
DEGREE = 4
APPLIES = SWEEPS * DEGREE

upper_bound = 4.5
lower_bound = 1.35

AXES = ("group", "fold")
F32 = jnp.float32
BF16 = jnp.bfloat16
VMEM = pl.BlockSpec(memory_space=pltpu.VMEM)
SMEM = pl.BlockSpec(memory_space=pltpu.SMEM)
HBM = pl.BlockSpec(memory_space=pltpu.HBM)


def coefficients():
    theta = (upper_bound + lower_bound) / 2.0
    delta = (upper_bound - lower_bound) / 2.0
    pairs = []
    for sweep in range(SWEEPS):
        pairs.append((0.0, 1.0 / theta))
        ratio = delta / theta
        for step in range(1, DEGREE):
            ratio_next = 1.0 / (2.0 * theta / delta - ratio)
            pairs.append((ratio_next * ratio, 2.0 * ratio_next / delta))
            ratio = ratio_next
    return pairs


def params(limit=16):
    return pltpu.CompilerParams(vmem_limit_bytes=limit * 2**20)


def split(value):
    high = value.astype(BF16)
    return high, (value - high.astype(F32)).astype(BF16)


def pick_lanes(window, low, shift):
    lane = lax.broadcasted_iota(jnp.int32, (16, 128), 1)
    turn = (128 - shift) % 128
    first = pltpu.roll(window(low), turn, 1)
    second = pltpu.roll(window(low + 1), turn, 1)
    return jnp.where(lane < 128 - shift, first, second)


def put_payloads(ob, steps, even, u, at, r, pay_a, pay_b):
    h = HB * steps
    inner = h - HB
    for pay, right in ((pay_a, even), (pay_b, jnp.logical_not(even))):
        pay[:h] = u[pl.ds(at + jnp.where(right, ob - h, 0), h)]
        if inner:
            pay[h:] = r[pl.ds(at + jnp.where(right, ob - inner, 0), inner)]


def begin_of(counts, j):
    total = 0
    for i in range(counts.shape[1]):
        total = total + jnp.where(i < j, counts[0, i], 0)
    return total


def holder(fold, folds, d, c):
    return lax.rem(fold // 2 + d, folds // 2) * 2 + jnp.where(c, 1 - fold % 2, fold % 2)


def part_of(fold, folds, backwards):
    return jnp.where(backwards == 1, folds - 1 - fold, fold)


def align_kernel(ob, steps, keys, facts, counts, *refs):
    folds = len(keys)
    sources, (u_out, r_out, pay_a, pay_b), windows, sem = refs[: folds + 1], refs[folds + 1 : folds + 5], refs[-2], refs[-1]
    capacity = sources[0].shape[-1]
    length = windows.shape[-1]
    lane = lax.broadcasted_iota(jnp.int32, (16, 128), 1)
    base = facts[0] * (ob * 128)
    spans, copies = [], []
    for j, (d, c) in enumerate(keys):
        owner = holder(facts[2], folds, d, c)
        start = begin_of(counts, owner)
        first = jnp.clip((base - start) >> 7, 0, (capacity - length) // 128)
        spans.append((start, counts[0, owner], first))
        for i in range(2):
            source = sources[i] if j == 0 else sources[j + 1].at[i]
            source = source.at[:, pl.ds(pl.multiple_of(first * 128, 128), length)]
            copies.append(pltpu.make_async_copy(source, windows.at[2 * j + i], sem.at[2 * j + i]))
    for copy in copies:
        copy.start()
    for copy in copies:
        copy.wait()

    def block(e, carry):
        row = base + e * 128
        totals = [jnp.zeros((16, 128), F32), jnp.zeros((16, 128), F32)]
        for j, (start, count, first) in enumerate(spans):
            at = row - start
            low = (at >> 7) - first
            shift = at & 127
            index = at + lane
            valid = (index >= 0) & (index < count)
            for a in range(2):

                def window(b, held=windows.at[2 * j + a]):
                    b = jnp.clip(b, 0, length // 128 - 1)
                    return held[:, pl.ds(pl.multiple_of(b * 128, 128), 128)]

                totals[a] = jnp.where(valid, pick_lanes(window, low, shift), totals[a])
        u_out[e] = totals[0]
        r_out[e] = totals[1]
        return carry

    lax.fori_loop(0, ob, block, 0, unroll=4)
    put_payloads(ob, steps, facts[1] == 0, u_out, 0, r_out, pay_a, pay_b)


def outward_kernel(folds, halo, width, facts, columns, initial, right_side, blocks, stacked, border, sem):
    own = columns.shape[1]
    size = blocks.shape[0] // own
    part = facts[0]
    pair = [pltpu.make_async_copy(array, stacked.at[i], sem.at[i]) for i, array in enumerate((initial, right_side))]
    for copy in pair:
        copy.start()
    first = jnp.where(part == 0, 0, own - halo)

    @pl.when((part == 0) | (part == folds - 1))
    def _():
        rows = blocks.at[pl.ds(pl.multiple_of(first * size, size), halo * size)]
        copy = pltpu.make_async_copy(rows, border.at[: halo * size], sem.at[2])
        copy.start()
        lane = lax.broadcasted_iota(jnp.int32, (8, 128), 1)
        indices = jnp.zeros((8, 128), jnp.int32)
        for i in range(halo):
            for k in range(width):
                indices = jnp.where(lane == i * width + k, columns[k, first + i], indices)
        border[halo * size :] = indices.astype(F32)
        copy.wait()

    for copy in pair:
        copy.wait()


def gate_kernel(n, *refs):
    del n, refs


def put_row(out, a, raw):
    side = raw.shape[-1]
    for k in range(out.shape[1] // side):
        high, low = split(raw[k * side : (k + 1) * side])
        out[a, k * side : (k + 1) * side, :side] = high.T
        out[a, k * side : (k + 1) * side, side:] = low.T


def prepare_kernel(ob, halo, width, facts, columns, blocks, out, token, offsets, raw, sem):
    rows, size = raw.shape[0], raw.shape[1]
    own = blocks.shape[0] // size
    first = facts[0] * ob - halo

    def copy(a):
        i = pl.multiple_of(jnp.clip(first + a, 0, own - 1) * size, size)
        return pltpu.make_async_copy(blocks.at[pl.ds(i, size)], raw.at[a], sem.at[a])

    for a in range(rows):
        copy(a).start()

    def indices(a, carry):
        i = first + a
        for k in range(width):
            offsets[a * width + k] = columns[k, jnp.clip(i, 0, own - 1)] - HB - i
        return carry

    lax.fori_loop(0, rows, indices, 0)
    token[...] = jnp.zeros_like(token)
    group = 4 if rows % 4 == 0 else 2

    def several(g, carry):
        for s in range(group):
            a = g * group + s
            copy(a).wait()
            put_row(out, a, raw.at[a])
        return carry

    lax.fori_loop(0, rows // group, several, 0)


def border_kernel(ob, folds, halo, width, facts, known, prepared, raw, out, offsets, vector, scalars, sem):
    del prepared
    part = facts[0]
    size = out.shape[1]

    def keep(n, carry):
        offsets[n] = known[n]
        return carry

    lax.fori_loop(0, known.shape[0], keep, 0, unroll=10)

    @pl.when((part == 0) | (part == folds - 1))
    def _():
        vector[...] = raw[halo * size :].astype(jnp.int32)
        copy = pltpu.make_async_copy(vector, scalars, sem)
        copy.start()
        first = jnp.where(part == 0, 0, halo + ob)
        for a in range(halo):
            put_row(out, first + a, raw.at[a * size : (a + 1) * size])
        copy.wait()
        own = ob * folds
        for i in range(halo):
            local = jnp.where(part == 0, own - halo + i, i)
            for k in range(width):
                offset = jnp.clip(scalars[0, i * width + k] - HB - local, -HB, HB)
                offsets[(first + i) * width + k] = offset


def phase_kernel(ob, halo, steps, first, after, pairs, facts, offsets, operator, *refs):
    h = HB * steps
    inner = h - HB
    extent = ob + 2 * h
    width = offsets.shape[0] // (ob + 2 * halo)
    if not first:
        x_in, *refs = refs
    u_in, r_in, got_a, got_b, *refs = refs
    if after:
        x_out, u_out, r_out, pay_a, pay_b, u, r, *pieces = refs
    else:
        x_out, u, r, *pieces = refs
    even = facts[1] == 0
    for got, right in ((got_a, even), (got_b, jnp.logical_not(even))):
        u[pl.ds(jnp.where(right, h + ob, 0), h)] = got[:h]
        if inner:
            r[pl.ds(jnp.where(right, h + ob, HB), inner)] = got[h:]
    u[h : h + ob] = u_in[...]
    r[h : h + ob] = r_in[...]
    high, low = split(u[...])
    pieces[0][:, :16] = high
    pieces[0][:, 16:] = low
    x = None if first else x_in[...]
    for t in range(steps):
        x = u[h : h + ob] if x is None else x + u[h : h + ob]
        now, later = pieces[t % 2], pieces[(t + 1) % 2]
        old, new = pairs[t]
        done = t == steps - 1

        def row(e, carry):
            a = e - h + halo
            left = jnp.concatenate([now[e + offsets[a * width + k]] for k in range(width)], axis=1)
            product = jnp.dot(left, operator[a], preferred_element_type=F32)
            product = product[:16] + product[16:]
            resid = r[e] - (product[:, :128] + product[:, 128:])
            r[e] = resid
            update = new * resid if old == 0.0 else old * u[e] + new * resid
            u[e] = update
            if not done:
                big, small = split(update)
                later[e, :16] = big
                later[e, 16:] = small
            return carry

        lower, upper = HB * (t + 1), extent - HB * (t + 1)
        lax.fori_loop(lower, upper, row, 0, unroll=True)
    if not after:
        x_out[...] = x + u[h : h + ob]
        return
    x_out[...] = x
    u_out[...] = u[h : h + ob]
    r_out[...] = r[h : h + ob]
    put_payloads(ob, after, even, u, h, r, pay_a, pay_b)


def finish_kernel(ob, keys, facts, counts, *refs):
    parts, (out, whole) = refs[:-2], refs[-2:]
    total = whole.shape[0]
    for (d, c), part in zip(keys, parts):
        theirs = part_of(holder(facts[2], len(keys), d, c), len(keys), facts[3])
        whole[pl.ds(theirs * ob, ob)] = part[...]
    start, count = begin_of(counts, facts[2]), counts[0, facts[2]]
    lane = lax.broadcasted_iota(jnp.int32, (16, 128), 1)
    low, shift = start >> 7, start & 127

    def block(b, carry):
        piece = pick_lanes(lambda i: whole[jnp.minimum(i, total - 1)], low + b, shift)
        piece = jnp.where(b * 128 + lane < count, piece, 0.0)
        out[:, pl.ds(pl.multiple_of(b * 128, 128), 128)] = piece
        return carry

    lax.fori_loop(0, out.shape[1] // 128, block, 0, unroll=8)


def over_chips(array, d, folds):
    return lax.ppermute(array, "fold", [((i + 2 * d) % folds, i) for i in range(folds)])


def other_core(array, folds):
    return lax.ppermute(array, "fold", [(i, i ^ 1) for i in range(folds)])


def on_device(right_side, initial, counts, columns, blocks):
    groups, folds = lax.axis_size("group"), lax.axis_size("fold")
    vectors, capacity = right_side.shape
    own, width, side = blocks.shape[0], blocks.shape[1], blocks.shape[2]
    size = width * side
    ob = own // folds
    steps = 3 if ob >= 9 else 2
    halo = HB * (steps - 1)
    rows = ob + 2 * halo
    pairs = coefficients()
    fold = lax.axis_index("fold")
    backwards = lax.axis_index("group") % 2
    part = part_of(fold, folds, backwards)
    devices = groups * folds
    facts = jnp.stack([part, part % 2, fold, backwards]).astype(jnp.int32)
    state = jax.ShapeDtypeStruct((ob, vectors, side), F32)
    operator_shape = pltpu.VMEM((rows, size, 2 * side), BF16)

    payload = jax.ShapeDtypeStruct((2 * HB * steps - HB, vectors, side), F32)

    line = [g * folds + (folds - 1 - p if g % 2 else p) for g in range(groups) for p in range(folds)]

    def swap(first, distance):
        ends = [(line[i], line[i + 1]) for i in range(first, devices - 1, distance)]
        return ends + [(j, i) for i, j in ends]

    swap_a, swap_b, swap_border = swap(0, 2), swap(1, 2), swap(folds - 1, folds)

    turned = columns.T
    flat = pltpu.with_memory_space_constraint(blocks.reshape(own * size, side), pltpu.HBM)
    near = [pltpu.with_memory_space_constraint(array, pltpu.HBM) for array in (initial, right_side)]
    stacked, border = pl.pallas_call(
        functools.partial(outward_kernel, folds, halo, width),
        out_shape=(pltpu.VMEM((2, vectors, capacity), F32), pltpu.VMEM((halo * size + 8, side), F32)),
        in_specs=[SMEM, SMEM, HBM, HBM, HBM],
        out_specs=(VMEM, VMEM),
        scratch_shapes=[pltpu.SemaphoreType.DMA((3,))],
        compiler_params=params(),
    )(facts, turned, *near, flat)
    far = [over_chips(stacked, d, folds) for d in range(1, folds // 2)]
    border = lax.ppermute(border, AXES, swap_border)

    operator, token, offsets = pl.pallas_call(
        functools.partial(prepare_kernel, ob, halo, width),
        out_shape=(operator_shape, jax.ShapeDtypeStruct((8, 128), F32), jax.ShapeDtypeStruct((rows * width,), jnp.int32)),
        in_specs=[SMEM, SMEM, HBM],
        out_specs=(VMEM, VMEM, SMEM),
        scratch_shapes=[
            pltpu.VMEM((rows, size, side), F32),
            pltpu.SemaphoreType.DMA((rows,)),
        ],
        compiler_params=params(),
        cost_estimate=pl.CostEstimate(flops=10**7, bytes_accessed=2 * rows * size * side * 4, transcendentals=0),
    )(facts, turned, flat)

    def gate(arrays, spaces, token):
        return pl.pallas_call(
            functools.partial(gate_kernel, len(arrays)),
            out_shape=tuple(space(array.shape, F32) for array, space in zip(arrays, spaces)),
            in_specs=[pl.BlockSpec(memory_space=space) for space in spaces] + [pl.BlockSpec(memory_space=pl.ANY)],
            out_specs=tuple(pl.BlockSpec(memory_space=space) for space in spaces),
            input_output_aliases={i: i for i in range(len(arrays))},
            compiler_params=params(),
        )(*[pltpu.with_memory_space_constraint(array, space) for array, space in zip(arrays, spaces)], token)

    far = gate(far, [pltpu.HBM] * len(far), token)

    keys, arrays = [], []
    for d, array in enumerate([stacked, *far]):
        keys += [(d, False), (d, True)]
        arrays += ([array] if d else []) + [other_core(array, folds)]
    u, r, pay_a, pay_b = pl.pallas_call(
        functools.partial(align_kernel, ob, steps, keys),
        out_shape=(state, state, payload, payload),
        in_specs=[SMEM, SMEM] + [HBM] * (folds + 1),
        out_specs=(VMEM,) * 4,
        scratch_shapes=[
            pltpu.VMEM((2 * folds, vectors, (ob + 1) * side), F32),
            pltpu.SemaphoreType.DMA((2 * folds,)),
        ],
        compiler_params=params(),
    )(facts, counts, *near, *[pltpu.with_memory_space_constraint(array, pltpu.HBM) for array in arrays])

    operator, offsets = pl.pallas_call(
        functools.partial(border_kernel, ob, folds, halo, width),
        out_shape=(operator_shape, jax.ShapeDtypeStruct((rows * width,), jnp.int32)),
        in_specs=[SMEM, SMEM, VMEM, VMEM],
        out_specs=(VMEM, SMEM),
        input_output_aliases={2: 0},
        scratch_shapes=[
            pltpu.VMEM((8, 128), jnp.int32),
            pltpu.SMEM((8, 128), jnp.int32),
            pltpu.SemaphoreType.DMA(()),
        ],
        compiler_params=params(),
    )(facts, offsets, pltpu.with_memory_space_constraint(operator, pltpu.VMEM), border)
    operator = pltpu.with_memory_space_constraint(operator, pltpu.VMEM)

    x = None
    extent = ob + 2 * HB * steps
    for done in range(0, APPLIES, steps):
        got_a = lax.ppermute(pay_a, AXES, swap_a)
        got_b = lax.ppermute(pay_b, AXES, swap_b)
        first, last = done == 0, done + steps == APPLIES
        outs = pl.pallas_call(
            functools.partial(phase_kernel, ob, halo, steps, first, 0 if last else steps, pairs[done : done + steps]),
            out_shape=state if last else (state, state, state, payload, payload),
            in_specs=[SMEM, SMEM] + [VMEM] * (5 if first else 6),
            out_specs=VMEM if last else (VMEM,) * 5,
            scratch_shapes=[pltpu.VMEM((extent, vectors, side), F32)] * 2
            + [pltpu.VMEM((extent, 2 * vectors, side), BF16)] * 2,
            compiler_params=params(),
        )(facts, offsets, operator, *([] if first else [x]), u, r, got_a, got_b)
        if last:
            x = outs
        else:
            x, u, r, pay_a, pay_b = outs

    parts = []
    for d in range(folds // 2):
        piece = over_chips(x, d, folds) if d else x
        parts += [piece, other_core(piece, folds)]
    return pl.pallas_call(
        functools.partial(finish_kernel, ob, keys),
        out_shape=jax.ShapeDtypeStruct((vectors, capacity), F32),
        in_specs=[SMEM, SMEM] + [VMEM] * folds,
        out_specs=VMEM,
        scratch_shapes=[pltpu.VMEM((own, vectors, side), F32)],
        compiler_params=params(),
    )(facts, counts, *parts)


def solution(mesh):
    placed = (
        P(None, AXES),
        P(None, AXES),
        P("group", None),
        P("group", None),
        P("group", None, None, None),
    )
    return jax.shard_map(on_device, mesh=mesh, in_specs=placed, out_specs=P(None, AXES), check_vma=False)
```

```python
import functools

import jax
import jax.numpy as jnp
from jax import lax
from jax.experimental import pallas as pl
from jax.experimental.pallas import tpu as pltpu
from jax.sharding import PartitionSpec as P

HB = 3
SWEEPS = 3
DEGREE = 4
APPLIES = SWEEPS * DEGREE

upper_bound = 4.5
lower_bound = 1.35

AXES = ("group", "fold")
F32 = jnp.float32
BF16 = jnp.bfloat16
VMEM = pl.BlockSpec(memory_space=pltpu.VMEM)
SMEM = pl.BlockSpec(memory_space=pltpu.SMEM)
HBM = pl.BlockSpec(memory_space=pltpu.HBM)


def coefficients():
    theta = (upper_bound + lower_bound) / 2.0
    delta = (upper_bound - lower_bound) / 2.0
    pairs = []
    for sweep in range(SWEEPS):
        pairs.append((0.0, 1.0 / theta))
        ratio = delta / theta
        for step in range(1, DEGREE):
            ratio_next = 1.0 / (2.0 * theta / delta - ratio)
            pairs.append((ratio_next * ratio, 2.0 * ratio_next / delta))
            ratio = ratio_next
    return pairs


def params(limit=16):
    return pltpu.CompilerParams(vmem_limit_bytes=limit * 2**20)


def split(value):
    high = value.astype(BF16)
    return high, (value - high.astype(F32)).astype(BF16)


def pick_lanes(window, low, shift):
    lane = lax.broadcasted_iota(jnp.int32, (16, 128), 1)
    turn = (128 - shift) % 128
    first = pltpu.roll(window(low), turn, 1)
    second = pltpu.roll(window(low + 1), turn, 1)
    return jnp.where(lane < 128 - shift, first, second)


def sides(even, right_is_a):
    return even if right_is_a else jnp.logical_not(even)


def put_payload(ob, steps, right, u, r, pay):
    h = HB * steps
    inner = h - HB
    pay[:h] = u[pl.ds(h + jnp.where(right, ob - h, 0), h)]
    if inner:
        pay[h:] = r[pl.ds(h + jnp.where(right, ob - inner, 0), inner)]


def take_payload(ob, steps, right, got, u, r, now):
    h = HB * steps
    inner = h - HB
    at = jnp.where(right, h + ob, 0)
    u[pl.ds(at, h)] = got[:h]
    if inner:
        r[pl.ds(jnp.where(right, h + ob, HB), inner)] = got[h:]
    high, low = split(got[:h])
    now[pl.ds(at, h), :16] = high
    now[pl.ds(at, h), 16:] = low


def begin_of(counts, j):
    total = 0
    for i in range(counts.shape[1]):
        total = total + jnp.where(i < j, counts[0, i], 0)
    return total


def holder(fold, folds, d, c):
    return lax.rem(fold // 2 + d, folds // 2) * 2 + jnp.where(c, 1 - fold % 2, fold % 2)


def part_of(fold, folds, backwards):
    return jnp.where(backwards == 1, folds - 1 - fold, fold)


def align_kernel(ob, steps, keys, facts, counts, *refs):
    folds = len(keys)
    sources, (x, u, r, now, later, pay_a, pay_b) = refs[:folds], refs[folds:]
    del x, later
    h = HB * steps
    capacity = sources[0].shape[-1]
    lane = lax.broadcasted_iota(jnp.int32, (16, 128), 1)
    base = facts[0] * (ob * 128)
    spans = []
    for d, c in keys:
        owner = holder(facts[2], folds, d, c)
        spans.append((begin_of(counts, owner), counts[0, owner]))

    def block(e, carry):
        row = base + e * 128
        totals = [jnp.zeros((16, 128), F32), jnp.zeros((16, 128), F32)]
        for source, (start, count) in zip(sources, spans):
            at = row - start
            low = at >> 7
            shift = at & 127
            index = at + lane
            valid = (index >= 0) & (index < count)
            for a in range(2):

                def window(b, a=a, source=source):
                    b = jnp.clip(b, 0, capacity // 128 - 1)
                    return source[a, :, pl.ds(pl.multiple_of(b * 128, 128), 128)]

                totals[a] = jnp.where(valid, pick_lanes(window, low, shift), totals[a])
        u[h + e] = totals[0]
        r[h + e] = totals[1]
        high, low = split(totals[0])
        now[h + e, :16] = high
        now[h + e, 16:] = low
        return carry

    lax.fori_loop(0, ob, block, 0, unroll=4)
    even = facts[1] == 0
    put_payload(ob, steps, sides(even, True), u, r, pay_a)
    put_payload(ob, steps, sides(even, False), u, r, pay_b)


def stack_kernel(initial, right_side, stacked, sem):
    pair = [pltpu.make_async_copy(array, stacked.at[i], sem.at[i]) for i, array in enumerate((initial, right_side))]
    for copy in pair:
        copy.start()
    for copy in pair:
        copy.wait()


def outward_kernel(folds, halo, width, facts, columns, blocks, border, sem):
    own = columns.shape[1]
    size = blocks.shape[0] // own
    part = facts[0]
    first = jnp.where(part == 0, 0, own - halo)

    @pl.when((part == 0) | (part == folds - 1))
    def _():
        rows = blocks.at[pl.ds(pl.multiple_of(first * size, size), halo * size)]
        copy = pltpu.make_async_copy(rows, border.at[: halo * size], sem)
        copy.start()
        lane = lax.broadcasted_iota(jnp.int32, (8, 128), 1)
        indices = jnp.zeros((8, 128), jnp.int32)
        for i in range(halo):
            for k in range(width):
                indices = jnp.where(lane == i * width + k, columns[k, first + i], indices)
        border[halo * size :] = indices.astype(F32)
        copy.wait()


def gate_kernel(n, *refs):
    del n, refs


def put_row(out, a, raw):
    side = raw.shape[-1]
    for k in range(out.shape[1] // side):
        high, low = split(raw[k * side : (k + 1) * side])
        out[a, k * side : (k + 1) * side, :side] = high.T
        out[a, k * side : (k + 1) * side, side:] = low.T


def prepare_kernel(ob, halo, width, facts, columns, blocks, out, token, offsets, raw, sem):
    rows, size = raw.shape[0], raw.shape[1]
    own = blocks.shape[0] // size
    first = facts[0] * ob - halo

    def copy(a):
        i = pl.multiple_of(jnp.clip(first + a, 0, own - 1) * size, size)
        return pltpu.make_async_copy(blocks.at[pl.ds(i, size)], raw.at[a], sem.at[a])

    for a in range(rows):
        copy(a).start()

    def indices(a, carry):
        i = first + a
        for k in range(width):
            offsets[a * width + k] = columns[k, jnp.clip(i, 0, own - 1)] - HB - i
        return carry

    lax.fori_loop(0, rows, indices, 0)
    token[...] = jnp.zeros_like(token)
    group = 4 if rows % 4 == 0 else 2

    def several(g, carry):
        for s in range(group):
            a = g * group + s
            copy(a).wait()
            put_row(out, a, raw.at[a])
        return carry

    lax.fori_loop(0, rows // group, several, 0)


def border_kernel(ob, folds, halo, width, facts, prepared, raw, before, out, offsets, vector, scalars, sem):
    del prepared, before
    part = facts[0]
    size = out.shape[1]

    @pl.when((part == 0) | (part == folds - 1))
    def _():
        vector[...] = raw[halo * size :].astype(jnp.int32)
        copy = pltpu.make_async_copy(vector, scalars, sem)
        copy.start()
        first = jnp.where(part == 0, 0, halo + ob)
        for a in range(halo):
            put_row(out, first + a, raw.at[a * size : (a + 1) * size])
        copy.wait()
        for i in range(halo):
            local = jnp.where(part == 0, ob * folds - halo + i, i)
            for k in range(width):
                offsets[i * width + k] = jnp.clip(scalars[0, i * width + k] - HB - local, -HB, HB)


def apply_rows(t, steps, starts, count, first, last, pair, offset, operator, x, u, r, pieces):
    now, later = pieces[t % 2], pieces[(t + 1) % 2]
    width = operator.shape[1] // 128
    old, new = pair
    final = last and t == steps - 1

    def row(n, carry):
        e = starts + n
        a = e - HB
        left = jnp.concatenate([now[e + offset(a, k)] for k in range(width)], axis=1)
        product = jnp.dot(left, operator[a], preferred_element_type=F32)
        product = product[:16] + product[16:]
        resid = r[e] - (product[:, :128] + product[:, 128:])
        before = u[e]
        update = new * resid if old == 0.0 else old * before + new * resid
        total = before if first and t == 0 else x[e] + before
        x[e] = total + update if final else total
        if not final:
            r[e] = resid
            u[e] = update
            high, low = split(update)
            later[e, :16] = high
            later[e, 16:] = low
        return carry

    lax.fori_loop(0, count, row, 0, unroll=True)


def inner_kernel(ob, folds, steps, first, last, pairs, facts, offsets, operator, *refs):
    got_a, (x, u, r, *pieces) = refs[5], refs[6:]
    h = HB * steps
    width = operator.shape[1] // 128
    even = facts[1] == 0
    take_payload(ob, steps, sides(even, True), got_a, u, r, pieces[0])

    def offset(a, k):
        return offsets[a * width + k]

    for t in range(steps):
        starts = jnp.where(even, h + HB + HB * t, HB + HB * t)
        count = ob + h - 2 * HB - 2 * HB * t
        apply_rows(t, steps, starts, count, first, last, pairs[t], offset, operator, x, u, r, pieces)


def outer_kernel(ob, folds, steps, first, last, pairs, facts, offsets, lent, operator, *refs):
    got_b, (x, u, r, *pieces), outs = refs[5], refs[6:11], refs[11:]
    h = HB * steps
    inner = h - HB
    width = operator.shape[1] // 128
    even = facts[1] == 0
    edge = (facts[0] == 0) | (facts[0] == folds - 1)
    take_payload(ob, steps, sides(even, False), got_b, u, r, pieces[0])

    def offset(a, k):
        i = jnp.where(even, a, a - inner - ob)
        outside = edge & (i >= 0) & (i < inner)
        return jnp.where(outside, lent[jnp.clip(i, 0, inner - 1) * width + k], offsets[a * width + k])

    for t in range(steps):
        starts = jnp.where(even, HB + HB * t, h + ob - HB - HB * t)
        apply_rows(t, steps, starts, h, first, last, pairs[t], offset, operator, x, u, r, pieces)
    if last:
        outs[0][...] = x[h : h + ob]
    else:
        put_payload(ob, steps, sides(even, True), u, r, outs[0])
        put_payload(ob, steps, sides(even, False), u, r, outs[1])


def finish_kernel(ob, keys, facts, counts, *refs):
    parts, (out, whole) = refs[:-2], refs[-2:]
    total = whole.shape[0]
    for (d, c), part in zip(keys, parts):
        theirs = part_of(holder(facts[2], len(keys), d, c), len(keys), facts[3])
        whole[pl.ds(theirs * ob, ob)] = part[...]
    start, count = begin_of(counts, facts[2]), counts[0, facts[2]]
    lane = lax.broadcasted_iota(jnp.int32, (16, 128), 1)
    low, shift = start >> 7, start & 127

    def block(b, carry):
        piece = pick_lanes(lambda i: whole[jnp.minimum(i, total - 1)], low + b, shift)
        piece = jnp.where(b * 128 + lane < count, piece, 0.0)
        out[:, pl.ds(pl.multiple_of(b * 128, 128), 128)] = piece
        return carry

    lax.fori_loop(0, out.shape[1] // 128, block, 0, unroll=8)


def over_chips(array, d, folds):
    return lax.ppermute(array, "fold", [((i + 2 * d) % folds, i) for i in range(folds)])


def other_core(array, folds):
    return lax.ppermute(array, "fold", [(i, i ^ 1) for i in range(folds)])


def on_device(right_side, initial, counts, columns, blocks):
    groups, folds = lax.axis_size("group"), lax.axis_size("fold")
    vectors, capacity = right_side.shape
    own, width, side = blocks.shape[0], blocks.shape[1], blocks.shape[2]
    size = width * side
    ob = own // folds
    steps = 3 if ob >= 9 else 2
    halo = HB * (steps - 1)
    rows = ob + 2 * halo
    pairs = coefficients()
    fold = lax.axis_index("fold")
    backwards = lax.axis_index("group") % 2
    part = part_of(fold, folds, backwards)
    devices = groups * folds
    facts = jnp.stack([part, part % 2, fold, backwards]).astype(jnp.int32)
    operator_shape = pltpu.VMEM((rows, size, 2 * side), BF16)

    payload = jax.ShapeDtypeStruct((2 * HB * steps - HB, vectors, side), F32)

    line = [g * folds + (folds - 1 - p if g % 2 else p) for g in range(groups) for p in range(folds)]

    def swap(first, distance):
        ends = [(line[i], line[i + 1]) for i in range(first, devices - 1, distance)]
        return ends + [(j, i) for i, j in ends]

    swap_a, swap_b, swap_border = swap(0, 2), swap(1, 2), swap(folds - 1, folds)

    near = [pltpu.with_memory_space_constraint(array, pltpu.HBM) for array in (initial, right_side)]
    stacked = pl.pallas_call(
        stack_kernel,
        out_shape=pltpu.VMEM((2, vectors, capacity), F32),
        in_specs=[HBM, HBM],
        out_specs=VMEM,
        scratch_shapes=[pltpu.SemaphoreType.DMA((2,))],
        compiler_params=params(),
    )(*near)
    far = [over_chips(stacked, d, folds) for d in range(1, folds // 2)]
    turned = columns.T
    flat = pltpu.with_memory_space_constraint(blocks.reshape(own * size, side), pltpu.HBM)
    border = pl.pallas_call(
        functools.partial(outward_kernel, folds, halo, width),
        out_shape=pltpu.VMEM((halo * size + 8, side), F32),
        in_specs=[SMEM, SMEM, HBM],
        out_specs=VMEM,
        scratch_shapes=[pltpu.SemaphoreType.DMA(())],
        compiler_params=params(),
    )(facts, turned, flat)
    border = lax.ppermute(border, AXES, swap_border)

    operator, token, offsets = pl.pallas_call(
        functools.partial(prepare_kernel, ob, halo, width),
        out_shape=(operator_shape, jax.ShapeDtypeStruct((8, 128), F32), jax.ShapeDtypeStruct((rows * width,), jnp.int32)),
        in_specs=[SMEM, SMEM, HBM],
        out_specs=(VMEM, VMEM, SMEM),
        scratch_shapes=[
            pltpu.VMEM((rows, size, side), F32),
            pltpu.SemaphoreType.DMA((rows,)),
        ],
        compiler_params=params(),
        cost_estimate=pl.CostEstimate(flops=10**7, bytes_accessed=2 * rows * size * side * 4, transcendentals=0),
    )(facts, turned, flat)

    def gate(arrays, spaces, token):
        return pl.pallas_call(
            functools.partial(gate_kernel, len(arrays)),
            out_shape=tuple(space(array.shape, F32) for array, space in zip(arrays, spaces)),
            in_specs=[pl.BlockSpec(memory_space=space) for space in spaces] + [pl.BlockSpec(memory_space=pl.ANY)],
            out_specs=tuple(pl.BlockSpec(memory_space=space) for space in spaces),
            input_output_aliases={i: i for i in range(len(arrays))},
            compiler_params=params(),
        )(*[pltpu.with_memory_space_constraint(array, space) for array, space in zip(arrays, spaces)], token)

    far = gate(far, [pltpu.VMEM] * len(far), token)

    keys, arrays = [], []
    for d, array in enumerate([stacked, *far]):
        keys += [(d, False), (d, True)]
        arrays += [array, other_core(array, folds)]
    extent = ob + 2 * HB * steps
    state = (pltpu.VMEM((extent, vectors, side), F32),) * 3 + (pltpu.VMEM((extent, 2 * vectors, side), BF16),) * 2
    *held, pay_a, pay_b = pl.pallas_call(
        functools.partial(align_kernel, ob, steps, keys),
        out_shape=(*state, payload, payload),
        in_specs=[SMEM, SMEM] + [VMEM] * folds,
        out_specs=(VMEM,) * 7,
        compiler_params=params(),
    )(facts, counts, *[pltpu.with_memory_space_constraint(array, pltpu.VMEM) for array in arrays])

    def part_of_phase(kernel, operator, indices, held, got, outs):
        held = [pltpu.with_memory_space_constraint(array, pltpu.VMEM) for array in held]
        n = len(indices)
        results = pl.pallas_call(
            functools.partial(kernel, ob, folds, steps, done == 0, done + steps == APPLIES, pairs[done : done + steps]),
            out_shape=(*state, *outs),
            in_specs=[SMEM] * (1 + n) + [VMEM] * 7,
            out_specs=(VMEM,) * (5 + len(outs)),
            input_output_aliases={2 + n + i: i for i in range(5)},
            compiler_params=params(),
        )(facts, *indices, pltpu.with_memory_space_constraint(operator, pltpu.VMEM), *held, got)
        return results[:5], results[5:]

    for done in range(0, APPLIES, steps):
        got_b = lax.ppermute(pay_b, AXES, swap_b)
        got_a = lax.ppermute(pay_a, AXES, swap_a)
        held, _ = part_of_phase(inner_kernel, operator, [offsets], held, got_a, ())
        if done == 0:
            operator, lent = pl.pallas_call(
                functools.partial(border_kernel, ob, folds, halo, width),
                out_shape=(operator_shape, jax.ShapeDtypeStruct((halo * width,), jnp.int32)),
                in_specs=[SMEM, VMEM, VMEM, pl.BlockSpec(memory_space=pl.ANY)],
                out_specs=(VMEM, SMEM),
                input_output_aliases={1: 0},
                scratch_shapes=[
                    pltpu.VMEM((8, 128), jnp.int32),
                    pltpu.SMEM((8, 128), jnp.int32),
                    pltpu.SemaphoreType.DMA(()),
                ],
                compiler_params=params(),
            )(facts, pltpu.with_memory_space_constraint(operator, pltpu.VMEM), border, held[0])
        if done + steps < APPLIES:
            held, (pay_a, pay_b) = part_of_phase(
                outer_kernel, operator, [offsets, lent], held, got_b, (payload, payload)
            )
        else:
            result = jax.ShapeDtypeStruct((ob, vectors, side), F32)
            held, (x,) = part_of_phase(outer_kernel, operator, [offsets, lent], held, got_b, (result,))
        if steps % 2:
            held = [*held[:3], held[4], held[3]]

    parts = []
    for d in range(folds // 2):
        piece = over_chips(x, d, folds) if d else x
        parts += [piece, other_core(piece, folds)]
    return pl.pallas_call(
        functools.partial(finish_kernel, ob, keys),
        out_shape=jax.ShapeDtypeStruct((vectors, capacity), F32),
        in_specs=[SMEM, SMEM] + [VMEM] * folds,
        out_specs=VMEM,
        scratch_shapes=[pltpu.VMEM((own, vectors, side), F32)],
        compiler_params=params(),
    )(facts, counts, *parts)


def solution(mesh):
    placed = (
        P(None, AXES),
        P(None, AXES),
        P("group", None),
        P("group", None),
        P("group", None, None, None),
    )
    return jax.shard_map(on_device, mesh=mesh, in_specs=placed, out_specs=P(None, AXES), check_vma=False)
```

```python
import functools

import jax
import jax.numpy as jnp
from jax import lax
from jax.experimental import pallas as pl
from jax.experimental.pallas import tpu as pltpu
from jax.sharding import PartitionSpec as P

HB = 3
SWEEPS = 3
DEGREE = 4
APPLIES = SWEEPS * DEGREE

upper_bound = 4.5
lower_bound = 1.35

AXES = ("group", "fold")
F32 = jnp.float32
BF16 = jnp.bfloat16
VMEM = pl.BlockSpec(memory_space=pltpu.VMEM)
SMEM = pl.BlockSpec(memory_space=pltpu.SMEM)
HBM = pl.BlockSpec(memory_space=pltpu.HBM)


def coefficients():
    theta = (upper_bound + lower_bound) / 2.0
    delta = (upper_bound - lower_bound) / 2.0
    pairs = []
    for sweep in range(SWEEPS):
        pairs.append((0.0, 1.0 / theta))
        ratio = delta / theta
        for step in range(1, DEGREE):
            ratio_next = 1.0 / (2.0 * theta / delta - ratio)
            pairs.append((ratio_next * ratio, 2.0 * ratio_next / delta))
            ratio = ratio_next
    return pairs


def params(limit=16):
    return pltpu.CompilerParams(vmem_limit_bytes=limit * 2**20)


def split(value):
    high = value.astype(BF16)
    return high, (value - high.astype(F32)).astype(BF16)


def pick_lanes(window, low, shift):
    lane = lax.broadcasted_iota(jnp.int32, (16, 128), 1)
    turn = (128 - shift) % 128
    first = pltpu.roll(window(low), turn, 1)
    second = pltpu.roll(window(low + 1), turn, 1)
    return jnp.where(lane < 128 - shift, first, second)


def sides(even, right_is_a):
    return even if right_is_a else jnp.logical_not(even)


def put_payload(ob, steps, right, u, r, pay):
    h = HB * steps
    inner = h - HB
    pay[:h] = u[pl.ds(h + jnp.where(right, ob - h, 0), h)]
    if inner:
        pay[h:] = r[pl.ds(h + jnp.where(right, ob - inner, 0), inner)]


def take_payload(ob, steps, right, got, u, r, now):
    h = HB * steps
    inner = h - HB
    at = jnp.where(right, h + ob, 0)
    u[pl.ds(at, h)] = got[:h]
    if inner:
        r[pl.ds(jnp.where(right, h + ob, HB), inner)] = got[h:]
    high, low = split(got[:h])
    now[pl.ds(at, h), :16] = high
    now[pl.ds(at, h), 16:] = low


COUNTS = 4


def begin_of(facts, folds, j):
    total = 0
    for i in range(folds):
        total = total + jnp.where(i < j, facts[COUNTS + i], 0)
    return total


def holder(fold, folds, d, c):
    return lax.rem(fold // 2 + d, folds // 2) * 2 + jnp.where(c, 1 - fold % 2, fold % 2)


def part_of(fold, folds, backwards):
    return jnp.where(backwards == 1, folds - 1 - fold, fold)


def align_kernel(ob, steps, keys, facts, *refs):
    folds = len(keys)
    sources, (x, u, r, now, later, pay_a, pay_b) = refs[:folds], refs[folds:]
    del x, later
    h = HB * steps
    capacity = sources[0].shape[-1]
    lane = lax.broadcasted_iota(jnp.int32, (16, 128), 1)
    base = facts[0] * (ob * 128)
    spans = []
    for d, c in keys:
        owner = holder(facts[2], folds, d, c)
        spans.append((begin_of(facts, folds, owner), facts[COUNTS + owner]))

    def block(e, carry):
        row = base + e * 128
        totals = [jnp.zeros((16, 128), F32), jnp.zeros((16, 128), F32)]
        for source, (start, count) in zip(sources, spans):
            at = row - start
            low = at >> 7
            shift = at & 127
            index = at + lane
            valid = (index >= 0) & (index < count)
            for a in range(2):

                def window(b, a=a, source=source):
                    b = jnp.clip(b, 0, capacity // 128 - 1)
                    return source[a, :, pl.ds(pl.multiple_of(b * 128, 128), 128)]

                totals[a] = jnp.where(valid, pick_lanes(window, low, shift), totals[a])
        u[h + e] = totals[0]
        r[h + e] = totals[1]
        high, low = split(totals[0])
        now[h + e, :16] = high
        now[h + e, 16:] = low
        return carry

    lax.fori_loop(0, ob, block, 0, unroll=4)
    even = facts[1] == 0
    put_payload(ob, steps, sides(even, True), u, r, pay_a)
    put_payload(ob, steps, sides(even, False), u, r, pay_b)


def first_kernel(folds, halo, width, counts, columns, initial, right_side, blocks, facts, held, stacked, border, live, sem):
    own = columns.shape[1]
    size = blocks.shape[0] // own
    fold = lax.axis_index("fold")
    backwards = lax.rem(lax.axis_index("group"), 2)
    part = part_of(fold, folds, backwards)
    edge = (part == 0) | (part == folds - 1)
    first = jnp.where(part == 0, 0, own - halo)
    small = [pltpu.make_async_copy(columns, held, sem.at[0]), pltpu.make_async_copy(counts, live, sem.at[1])]
    pair = [pltpu.make_async_copy(array, stacked.at[i], sem.at[2 + i]) for i, array in enumerate((initial, right_side))]
    rows = []
    for i in range(halo):
        row = blocks.at[pl.ds(pl.multiple_of((first + i) * size, size), size)]
        rows.append(pltpu.make_async_copy(row, border.at[i * size : (i + 1) * size], sem.at[4 + i]))
    for copy in small:
        copy.start()

    @pl.when(edge)
    def _():
        for copy in rows:
            copy.start()

    for copy in pair:
        copy.start()
    for copy in small:
        copy.wait()
    for i, fact in enumerate((part, lax.rem(part, 2), fold, backwards)):
        facts[i] = fact
    for i in range(folds):
        facts[COUNTS + i] = live[0, i]

    @pl.when(edge)
    def _():
        lane = lax.broadcasted_iota(jnp.int32, (8, 128), 1)
        indices = jnp.zeros((8, 128), jnp.int32)
        for i in range(halo):
            for k in range(width):
                indices = jnp.where(lane == i * width + k, held[k, first + i], indices)
        border[halo * size :] = indices.astype(F32)
        for copy in rows:
            copy.wait()

    for copy in pair:
        copy.wait()


def gate_kernel(n, *refs):
    del n, refs


def put_row(out, a, raw):
    side = raw.shape[-1]
    for k in range(out.shape[1] // side):
        high, low = split(raw[k * side : (k + 1) * side])
        out[a, k * side : (k + 1) * side, :side] = high.T
        out[a, k * side : (k + 1) * side, side:] = low.T


def prepare_kernel(ob, halo, width, facts, columns, blocks, out, token, offsets, raw, sem):
    rows, size = raw.shape[0], raw.shape[1]
    own = blocks.shape[0] // size
    first = facts[0] * ob - halo

    def copy(a):
        i = pl.multiple_of(jnp.clip(first + a, 0, own - 1) * size, size)
        return pltpu.make_async_copy(blocks.at[pl.ds(i, size)], raw.at[a], sem.at[a])

    for a in range(rows):
        copy(a).start()

    def indices(a, carry):
        i = first + a
        for k in range(width):
            offsets[a * width + k] = columns[k, jnp.clip(i, 0, own - 1)] - HB - i
        return carry

    lax.fori_loop(0, rows, indices, 0)
    token[...] = jnp.zeros_like(token)
    group = 4 if rows % 4 == 0 else 2

    def several(g, carry):
        for s in range(group):
            a = g * group + s
            copy(a).wait()
            put_row(out, a, raw.at[a])
        return carry

    lax.fori_loop(0, rows // group, several, 0)


def border_kernel(ob, folds, halo, width, facts, prepared, raw, before, out, offsets, vector, scalars, sem):
    del prepared, before
    part = facts[0]
    size = out.shape[1]

    @pl.when((part == 0) | (part == folds - 1))
    def _():
        vector[...] = raw[halo * size :].astype(jnp.int32)
        copy = pltpu.make_async_copy(vector, scalars, sem)
        copy.start()
        first = jnp.where(part == 0, 0, halo + ob)
        for a in range(halo):
            put_row(out, first + a, raw.at[a * size : (a + 1) * size])
        copy.wait()
        for i in range(halo):
            local = jnp.where(part == 0, ob * folds - halo + i, i)
            for k in range(width):
                offsets[i * width + k] = jnp.clip(scalars[0, i * width + k] - HB - local, -HB, HB)


def apply_rows(t, steps, starts, count, first, last, pair, offset, operator, x, u, r, pieces):
    now, later = pieces[t % 2], pieces[(t + 1) % 2]
    width = operator.shape[1] // 128
    old, new = pair
    final = last and t == steps - 1

    def row(n, carry):
        e = starts + n
        a = e - HB
        left = jnp.concatenate([now[e + offset(a, k)] for k in range(width)], axis=1)
        product = jnp.dot(left, operator[a], preferred_element_type=F32)
        product = product[:16] + product[16:]
        resid = r[e] - (product[:, :128] + product[:, 128:])
        before = u[e]
        update = new * resid if old == 0.0 else old * before + new * resid
        total = before if first and t == 0 else x[e] + before
        x[e] = total + update if final else total
        if not final:
            r[e] = resid
            u[e] = update
            high, low = split(update)
            later[e, :16] = high
            later[e, 16:] = low
        return carry

    lax.fori_loop(0, count, row, 0, unroll=True)


def inner_kernel(ob, folds, steps, first, last, pairs, facts, offsets, operator, *refs):
    got_a, (x, u, r, *pieces) = refs[5], refs[6:]
    h = HB * steps
    width = operator.shape[1] // 128
    even = facts[1] == 0
    take_payload(ob, steps, sides(even, True), got_a, u, r, pieces[0])

    def offset(a, k):
        return offsets[a * width + k]

    for t in range(steps):
        starts = jnp.where(even, h + HB + HB * t, HB + HB * t)
        count = ob + h - 2 * HB - 2 * HB * t
        apply_rows(t, steps, starts, count, first, last, pairs[t], offset, operator, x, u, r, pieces)


def outer_kernel(ob, folds, steps, first, last, pairs, facts, offsets, lent, operator, *refs):
    got_b, (x, u, r, *pieces), outs = refs[5], refs[6:11], refs[11:]
    h = HB * steps
    inner = h - HB
    width = operator.shape[1] // 128
    even = facts[1] == 0
    edge = (facts[0] == 0) | (facts[0] == folds - 1)
    take_payload(ob, steps, sides(even, False), got_b, u, r, pieces[0])

    def offset(a, k):
        i = jnp.where(even, a, a - inner - ob)
        outside = edge & (i >= 0) & (i < inner)
        return jnp.where(outside, lent[jnp.clip(i, 0, inner - 1) * width + k], offsets[a * width + k])

    for t in range(steps):
        starts = jnp.where(even, HB + HB * t, h + ob - HB - HB * t)
        apply_rows(t, steps, starts, h, first, last, pairs[t], offset, operator, x, u, r, pieces)
    if last:
        outs[0][...] = x[h : h + ob]
    else:
        put_payload(ob, steps, sides(even, True), u, r, outs[0])
        put_payload(ob, steps, sides(even, False), u, r, outs[1])


def finish_kernel(ob, keys, facts, *refs):
    parts, (out, whole) = refs[:-2], refs[-2:]
    total = whole.shape[0]
    for (d, c), part in zip(keys, parts):
        theirs = part_of(holder(facts[2], len(keys), d, c), len(keys), facts[3])
        whole[pl.ds(theirs * ob, ob)] = part[...]
    start, count = begin_of(facts, len(keys), facts[2]), facts[COUNTS + facts[2]]
    lane = lax.broadcasted_iota(jnp.int32, (16, 128), 1)
    low, shift = start >> 7, start & 127

    def block(b, carry):
        piece = pick_lanes(lambda i: whole[jnp.minimum(i, total - 1)], low + b, shift)
        piece = jnp.where(b * 128 + lane < count, piece, 0.0)
        out[:, pl.ds(pl.multiple_of(b * 128, 128), 128)] = piece
        return carry

    lax.fori_loop(0, out.shape[1] // 128, block, 0, unroll=8)


def over_chips(array, d, folds):
    return lax.ppermute(array, "fold", [((i + 2 * d) % folds, i) for i in range(folds)])


def other_core(array, folds):
    return lax.ppermute(array, "fold", [(i, i ^ 1) for i in range(folds)])


def on_device(right_side, initial, counts, columns, blocks):
    groups, folds = lax.axis_size("group"), lax.axis_size("fold")
    vectors, capacity = right_side.shape
    own, width, side = blocks.shape[0], blocks.shape[1], blocks.shape[2]
    size = width * side
    ob = own // folds
    steps = 3 if ob >= 9 else 2
    halo = HB * (steps - 1)
    rows = ob + 2 * halo
    pairs = coefficients()
    devices = groups * folds
    operator_shape = pltpu.VMEM((rows, size, 2 * side), BF16)

    payload = jax.ShapeDtypeStruct((2 * HB * steps - HB, vectors, side), F32)

    line = [g * folds + (folds - 1 - p if g % 2 else p) for g in range(groups) for p in range(folds)]

    def swap(first, distance):
        ends = [(line[i], line[i + 1]) for i in range(first, devices - 1, distance)]
        return ends + [(j, i) for i, j in ends]

    swap_a, swap_b, swap_border = swap(0, 2), swap(1, 2), swap(folds - 1, folds)

    def fixed(array, space=pltpu.HBM):
        return pltpu.with_memory_space_constraint(array, space)

    flat = fixed(blocks.reshape(own * size, side))
    facts, indices, stacked, border = pl.pallas_call(
        functools.partial(first_kernel, folds, halo, width),
        out_shape=(
            pltpu.SMEM((COUNTS + folds,), jnp.int32),
            pltpu.SMEM((width, own), jnp.int32),
            pltpu.VMEM((2, vectors, capacity), F32),
            pltpu.VMEM((halo * size + 8, side), F32),
        ),
        in_specs=[HBM] * 5,
        out_specs=(SMEM, SMEM, VMEM, VMEM),
        scratch_shapes=[pltpu.SMEM((1, folds), jnp.int32), pltpu.SemaphoreType.DMA((4 + halo,))],
        compiler_params=params(),
    )(fixed(counts), fixed(columns.T), fixed(initial), fixed(right_side), flat)
    facts, indices = fixed(facts, pltpu.SMEM), fixed(indices, pltpu.SMEM)
    border = lax.ppermute(border, AXES, swap_border)
    far = [over_chips(stacked, d, folds) for d in range(1, folds // 2)]

    operator, token, offsets = pl.pallas_call(
        functools.partial(prepare_kernel, ob, halo, width),
        out_shape=(operator_shape, jax.ShapeDtypeStruct((8, 128), F32), pltpu.SMEM((rows * width,), jnp.int32)),
        in_specs=[SMEM, SMEM, HBM],
        out_specs=(VMEM, VMEM, SMEM),
        scratch_shapes=[
            pltpu.VMEM((rows, size, side), F32),
            pltpu.SemaphoreType.DMA((rows,)),
        ],
        compiler_params=params(),
        cost_estimate=pl.CostEstimate(flops=10**7, bytes_accessed=2 * rows * size * side * 4, transcendentals=0),
    )(facts, indices, flat)
    offsets = fixed(offsets, pltpu.SMEM)

    def gate(arrays, spaces, token):
        return pl.pallas_call(
            functools.partial(gate_kernel, len(arrays)),
            out_shape=tuple(space(array.shape, F32) for array, space in zip(arrays, spaces)),
            in_specs=[pl.BlockSpec(memory_space=space) for space in spaces] + [pl.BlockSpec(memory_space=pl.ANY)],
            out_specs=tuple(pl.BlockSpec(memory_space=space) for space in spaces),
            input_output_aliases={i: i for i in range(len(arrays))},
            compiler_params=params(),
        )(*[pltpu.with_memory_space_constraint(array, space) for array, space in zip(arrays, spaces)], token)

    far = gate(far, [pltpu.VMEM] * len(far), token)

    keys, arrays = [], []
    for d, array in enumerate([stacked, *far]):
        keys += [(d, False), (d, True)]
        arrays += [array, other_core(array, folds)]
    extent = ob + 2 * HB * steps
    state = (pltpu.VMEM((extent, vectors, side), F32),) * 3 + (pltpu.VMEM((extent, 2 * vectors, side), BF16),) * 2
    *held, pay_a, pay_b = pl.pallas_call(
        functools.partial(align_kernel, ob, steps, keys),
        out_shape=(*state, payload, payload),
        in_specs=[SMEM] + [VMEM] * folds,
        out_specs=(VMEM,) * 7,
        compiler_params=params(),
    )(facts, *[fixed(array, pltpu.VMEM) for array in arrays])

    def part_of_phase(kernel, operator, indices, held, got, outs):
        held = [pltpu.with_memory_space_constraint(array, pltpu.VMEM) for array in held]
        n = len(indices)
        results = pl.pallas_call(
            functools.partial(kernel, ob, folds, steps, done == 0, done + steps == APPLIES, pairs[done : done + steps]),
            out_shape=(*state, *outs),
            in_specs=[SMEM] * (1 + n) + [VMEM] * 7,
            out_specs=(VMEM,) * (5 + len(outs)),
            input_output_aliases={2 + n + i: i for i in range(5)},
            compiler_params=params(),
        )(facts, *indices, pltpu.with_memory_space_constraint(operator, pltpu.VMEM), *held, got)
        return results[:5], results[5:]

    for done in range(0, APPLIES, steps):
        got_b = lax.ppermute(pay_b, AXES, swap_b)
        got_a = lax.ppermute(pay_a, AXES, swap_a)
        held, _ = part_of_phase(inner_kernel, operator, [offsets], held, got_a, ())
        if done == 0:
            operator, lent = pl.pallas_call(
                functools.partial(border_kernel, ob, folds, halo, width),
                out_shape=(operator_shape, pltpu.SMEM((halo * width,), jnp.int32)),
                in_specs=[SMEM, VMEM, VMEM, pl.BlockSpec(memory_space=pl.ANY)],
                out_specs=(VMEM, SMEM),
                input_output_aliases={1: 0},
                scratch_shapes=[
                    pltpu.VMEM((8, 128), jnp.int32),
                    pltpu.SMEM((8, 128), jnp.int32),
                    pltpu.SemaphoreType.DMA(()),
                ],
                compiler_params=params(),
            )(facts, pltpu.with_memory_space_constraint(operator, pltpu.VMEM), border, held[0])
            lent = fixed(lent, pltpu.SMEM)
        if done + steps < APPLIES:
            held, (pay_a, pay_b) = part_of_phase(
                outer_kernel, operator, [offsets, lent], held, got_b, (payload, payload)
            )
        else:
            result = jax.ShapeDtypeStruct((ob, vectors, side), F32)
            held, (x,) = part_of_phase(outer_kernel, operator, [offsets, lent], held, got_b, (result,))
        if steps % 2:
            held = [*held[:3], held[4], held[3]]

    parts = []
    for d in range(folds // 2):
        piece = over_chips(x, d, folds) if d else x
        parts += [piece, other_core(piece, folds)]
    return pl.pallas_call(
        functools.partial(finish_kernel, ob, keys),
        out_shape=jax.ShapeDtypeStruct((vectors, capacity), F32),
        in_specs=[SMEM] + [VMEM] * folds,
        out_specs=VMEM,
        scratch_shapes=[pltpu.VMEM((own, vectors, side), F32)],
        compiler_params=params(),
    )(facts, *parts)


def solution(mesh):
    placed = (
        P(None, AXES),
        P(None, AXES),
        P("group", None),
        P("group", None),
        P("group", None, None, None),
    )
    return jax.shard_map(on_device, mesh=mesh, in_specs=placed, out_specs=P(None, AXES), check_vma=False)
```

```python
import functools

import jax
import jax.numpy as jnp
from jax import lax
from jax.experimental import pallas as pl
from jax.experimental.pallas import tpu as pltpu
from jax.sharding import PartitionSpec as P

HB = 3
SWEEPS = 3
DEGREE = 4
APPLIES = SWEEPS * DEGREE

upper_bound = 4.5
lower_bound = 1.35
THETA = (upper_bound + lower_bound) / 2.0

AXES = ("group", "fold")
F32 = jnp.float32
BF16 = jnp.bfloat16
VMEM = pl.BlockSpec(memory_space=pltpu.VMEM)
SMEM = pl.BlockSpec(memory_space=pltpu.SMEM)
HBM = pl.BlockSpec(memory_space=pltpu.HBM)


def coefficients():
    theta = THETA
    delta = (upper_bound - lower_bound) / 2.0
    pairs = []
    for sweep in range(SWEEPS):
        pairs.append((0.0, 1.0 / theta))
        ratio = delta / theta
        for step in range(1, DEGREE):
            ratio_next = 1.0 / (2.0 * theta / delta - ratio)
            pairs.append((ratio_next * ratio, 2.0 * ratio_next / delta))
            ratio = ratio_next
    return pairs


def params(limit=16):
    return pltpu.CompilerParams(vmem_limit_bytes=limit * 2**20)


def split(value):
    high = value.astype(BF16)
    return high, (value - high.astype(F32)).astype(BF16)


def pick_lanes(window, low, shift):
    lane = lax.broadcasted_iota(jnp.int32, (16, 128), 1)
    turn = (128 - shift) % 128
    first = pltpu.roll(window(low), turn, 1)
    second = pltpu.roll(window(low + 1), turn, 1)
    return jnp.where(lane < 128 - shift, first, second)


def put_near(ob, steps, even, u, r, pay):
    h = HB * steps
    inner = h - HB
    pay[:h] = u[pl.ds(jnp.where(even, ob, h), h)]
    if inner:
        pay[h:] = r[pl.ds(jnp.where(even, h + ob - inner, h), inner)]


def take_near(ob, steps, even, got, u, r, now):
    h = HB * steps
    inner = h - HB
    at = jnp.where(even, h + ob, 0)
    u[pl.ds(at, h)] = got[:h]
    if inner:
        r[pl.ds(jnp.where(even, h + ob, HB), inner)] = got[h:]
    high, low = split(got[:h])
    now[pl.ds(at, h), :16] = high
    now[pl.ds(at, h), 16:] = low


def sent_blocks(steps):
    return HB * (steps - 2)


def put_far(ob, steps, even, u, r, pay):
    h = HB * steps
    pay[: 2 * HB] = u[pl.ds(jnp.where(even, h, h + ob - 2 * HB), 2 * HB)]
    pay[2 * HB : 3 * HB] = r[pl.ds(jnp.where(even, h, h + ob - HB), HB)]


def put_far_ahead(ob, steps, even, u, pay):
    h, n = HB * steps, sent_blocks(steps)
    pay[3 * HB :] = u[pl.ds(jnp.where(even, h + HB, h + ob - HB - n), n)]


def take_far(ob, steps, even, got, u, r, now, later):
    h, n = HB * steps, sent_blocks(steps)
    high, low = split(got[: 2 * HB])
    at = jnp.where(even, h - 2 * HB, h + ob)
    now[pl.ds(at, 2 * HB), :16] = high
    now[pl.ds(at, 2 * HB), 16:] = low
    at = jnp.where(even, h - HB, h + ob)
    u[pl.ds(at, HB)] = got[pl.ds(jnp.where(even, HB, 0), HB)]
    r[pl.ds(at, HB)] = got[2 * HB : 3 * HB]
    if n:
        ahead = got[3 * HB :]
        at = jnp.where(even, h - HB - n, h + ob + HB)
        u[pl.ds(at, n)] = ahead
        r[pl.ds(at, n)] = ahead * THETA
        high, low = split(ahead)
        later[pl.ds(at, n), :16] = high
        later[pl.ds(at, n), 16:] = low


COUNTS = 4


def begin_of(facts, folds, j):
    total = 0
    for i in range(folds):
        total = total + jnp.where(i < j, facts[COUNTS + i], 0)
    return total


def holder(fold, folds, d, c):
    return lax.rem(fold // 2 + d, folds // 2) * 2 + jnp.where(c, 1 - fold % 2, fold % 2)


def part_of(fold, folds, backwards):
    return jnp.where(backwards == 1, folds - 1 - fold, fold)


def align_kernel(ob, steps, keys, facts, *refs):
    folds = len(keys)
    sources, (x, u, r, now, later, pay_a) = refs[:folds], refs[folds:]
    del x, later
    h = HB * steps
    capacity = sources[0].shape[-1]
    lane = lax.broadcasted_iota(jnp.int32, (16, 128), 1)
    base = facts[0] * (ob * 128)
    spans = []
    for d, c in keys:
        owner = holder(facts[2], folds, d, c)
        spans.append((begin_of(facts, folds, owner), facts[COUNTS + owner]))

    def block(e, carry):
        row = base + e * 128
        totals = [jnp.zeros((16, 128), F32), jnp.zeros((16, 128), F32)]
        for source, (start, count) in zip(sources, spans):
            at = row - start
            low = at >> 7
            shift = at & 127
            index = at + lane
            valid = (index >= 0) & (index < count)
            for a in range(2):

                def window(b, a=a, source=source):
                    b = jnp.clip(b, 0, capacity // 128 - 1)
                    return source[a, :, pl.ds(pl.multiple_of(b * 128, 128), 128)]

                totals[a] = jnp.where(valid, pick_lanes(window, low, shift), totals[a])
        u[h + e] = totals[0]
        r[h + e] = totals[1]
        high, low = split(totals[0])
        now[h + e, :16] = high
        now[h + e, 16:] = low
        return carry

    lax.fori_loop(0, ob, block, 0, unroll=4)
    put_near(ob, steps, facts[1] == 0, u, r, pay_a)


def first_kernel(folds, lend, width, counts, columns, initial, right_side, blocks, facts, held, stacked, border, live, sem):
    own = columns.shape[1]
    size = blocks.shape[0] // own
    fold = lax.axis_index("fold")
    backwards = lax.rem(lax.axis_index("group"), 2)
    part = part_of(fold, folds, backwards)
    edge = (part == 0) | (part == folds - 1)
    first = jnp.where(part == 0, 0, own - lend)
    small = [pltpu.make_async_copy(columns, held, sem.at[0]), pltpu.make_async_copy(counts, live, sem.at[1])]
    pair = [pltpu.make_async_copy(array, stacked.at[i], sem.at[2 + i]) for i, array in enumerate((initial, right_side))]
    rows = []
    for i in range(lend):
        row = blocks.at[pl.ds(pl.multiple_of((first + i) * size, size), size)]
        rows.append(pltpu.make_async_copy(row, border.at[i * size : (i + 1) * size], sem.at[4 + i]))
    for copy in small:
        copy.start()

    @pl.when(edge)
    def _():
        for copy in rows:
            copy.start()

    for copy in pair:
        copy.start()
    for copy in small:
        copy.wait()
    for i, fact in enumerate((part, lax.rem(part, 2), fold, backwards)):
        facts[i] = fact
    for i in range(folds):
        facts[COUNTS + i] = live[0, i]

    @pl.when(edge)
    def _():
        lane = lax.broadcasted_iota(jnp.int32, (8, 128), 1)
        indices = jnp.zeros((8, 128), jnp.int32)
        for i in range(lend):
            for k in range(width):
                indices = jnp.where(lane == i * width + k, held[k, first + i], indices)
        border[lend * size :] = indices.astype(F32)
        for copy in rows:
            copy.wait()

    for copy in pair:
        copy.wait()


def gate_kernel(n, *refs):
    del n, refs


def put_row(out, a, raw):
    side = raw.shape[-1]
    for k in range(out.shape[1] // side):
        high, low = split(raw[k * side : (k + 1) * side])
        out[a, k * side : (k + 1) * side, :side] = high.T
        out[a, k * side : (k + 1) * side, side:] = low.T


def prepare_kernel(ob, halo, width, facts, columns, blocks, out, token, offsets, raw, sem):
    rows, size = raw.shape[0], raw.shape[1]
    own = blocks.shape[0] // size
    first = facts[0] * ob - halo

    def copy(a):
        i = pl.multiple_of(jnp.clip(first + a, 0, own - 1) * size, size)
        return pltpu.make_async_copy(blocks.at[pl.ds(i, size)], raw.at[a], sem.at[a])

    for a in range(rows):
        copy(a).start()

    def indices(a, carry):
        i = first + a
        for k in range(width):
            offsets[a * width + k] = columns[k, jnp.clip(i, 0, own - 1)] - HB - i
        return carry

    lax.fori_loop(0, rows, indices, 0)
    token[...] = jnp.zeros_like(token)
    group = 4 if rows % 4 == 0 else 2

    def several(g, carry):
        for s in range(group):
            a = g * group + s
            copy(a).wait()
            put_row(out, a, raw.at[a])
        return carry

    lax.fori_loop(0, rows // group, several, 0)


def border_kernel(ob, folds, halo, lend, width, facts, prepared, raw, before, out, offsets, vector, scalars, sem):
    del prepared, before
    part = facts[0]
    size = out.shape[1]

    @pl.when((part == 0) | (part == folds - 1))
    def _():
        vector[...] = raw[lend * size :].astype(jnp.int32)
        copy = pltpu.make_async_copy(vector, scalars, sem)
        copy.start()
        first = jnp.where(part == 0, halo - lend, halo + ob)
        for a in range(lend):
            put_row(out, first + a, raw.at[a * size : (a + 1) * size])
        copy.wait()
        for i in range(lend):
            local = jnp.where(part == 0, ob * folds - lend + i, i)
            for k in range(width):
                offsets[i * width + k] = jnp.clip(scalars[0, i * width + k] - HB - local, -HB, HB)


def apply_rows(t, steps, starts, count, first, last, pair, offset, operator, x, u, r, pieces):
    now, later = pieces[t % 2], pieces[(t + 1) % 2]
    width = operator.shape[1] // 128
    old, new = pair
    final = last and t == steps - 1

    def row(n, carry):
        e = starts + n
        a = e - HB
        left = jnp.concatenate([now[e + offset(a, k)] for k in range(width)], axis=1)
        product = jnp.dot(left, operator[a], preferred_element_type=F32)
        product = product[:16] + product[16:]
        resid = r[e] - (product[:, :128] + product[:, 128:])
        before = u[e]
        update = new * resid if old == 0.0 else old * before + new * resid
        total = before if first and t == 0 else x[e] + before
        x[e] = total + update if final else total
        if not final:
            r[e] = resid
            u[e] = update
            high, low = split(update)
            later[e, :16] = high
            later[e, 16:] = low
        return carry

    lax.fori_loop(0, count, row, 0, unroll=True)


def look_up(offsets, width):
    return lambda a, k: offsets[a * width + k]


def ahead(ob, steps, even, first, pair, offset, operator, x, u, r, pieces):
    h, n = HB * steps, sent_blocks(steps)
    starts = jnp.where(even, h + HB, h + ob - HB - n)
    apply_rows(0, steps, starts, n, first, False, pair, offset, operator, x, u, r, pieces)


def begin_kernel(ob, steps, pair, facts, offsets, operator, *refs):
    (x, u, r, *pieces), pay_b = refs[5:10], refs[10]
    even = facts[1] == 0
    put_far(ob, steps, even, u, r, pay_b)
    if sent_blocks(steps):
        ahead(ob, steps, even, True, pair, look_up(offsets, operator.shape[1] // 128), operator, x, u, r, pieces)
        put_far_ahead(ob, steps, even, u, pay_b)


def inner_kernel(ob, folds, steps, first, last, pairs, facts, offsets, operator, *refs):
    got_a, (x, u, r, *pieces) = refs[5], refs[6:]
    h = HB * steps
    even = facts[1] == 0
    offset = look_up(offsets, operator.shape[1] // 128)
    take_near(ob, steps, even, got_a, u, r, pieces[0])
    for t in range(steps):
        done = HB + (HB * t if t else sent_blocks(steps))
        starts = jnp.where(even, h + done, HB + HB * t)
        count = ob + h - HB - HB * t - done
        apply_rows(t, steps, starts, count, first, last, pairs[t], offset, operator, x, u, r, pieces)


def outer_kernel(ob, folds, steps, first, last, pairs, facts, offsets, lent, operator, *refs):
    got_b, (x, u, r, *pieces), outs = refs[5], refs[6:11], refs[11:]
    h = HB * steps
    inner = h - HB
    width = operator.shape[1] // 128
    lend = lent.shape[0] // width
    even = facts[1] == 0
    edge = (facts[0] == 0) | (facts[0] == folds - 1)
    take_far(ob, steps, even, got_b, u, r, *pieces)

    def offset(a, k):
        i = a - jnp.where(even, inner - lend, inner + ob)
        outside = edge & (i >= 0) & (i < lend)
        return jnp.where(outside, lent[jnp.clip(i, 0, lend - 1) * width + k], offsets[a * width + k])

    for t in range(steps):
        count = h if t else 2 * HB
        starts = jnp.where(even, HB + HB * t + h - count if not t else HB + HB * t, h + ob - HB - HB * t)
        apply_rows(t, steps, starts, count, first, last, pairs[t], offset, operator, x, u, r, pieces)
    if last:
        outs[0][...] = x[h : h + ob]
        return
    put_near(ob, steps, even, u, r, outs[0])
    put_far(ob, steps, even, u, r, outs[1])
    if sent_blocks(steps):
        pieces = pieces[::-1] if steps % 2 else pieces
        ahead(ob, steps, even, False, pairs[steps], look_up(offsets, width), operator, x, u, r, pieces)
        put_far_ahead(ob, steps, even, u, outs[1])


def finish_kernel(ob, keys, facts, *refs):
    parts, (out, whole) = refs[:-2], refs[-2:]
    total = whole.shape[0]
    for (d, c), part in zip(keys, parts):
        theirs = part_of(holder(facts[2], len(keys), d, c), len(keys), facts[3])
        whole[pl.ds(theirs * ob, ob)] = part[...]
    start, count = begin_of(facts, len(keys), facts[2]), facts[COUNTS + facts[2]]
    lane = lax.broadcasted_iota(jnp.int32, (16, 128), 1)
    low, shift = start >> 7, start & 127

    def block(b, carry):
        piece = pick_lanes(lambda i: whole[jnp.minimum(i, total - 1)], low + b, shift)
        piece = jnp.where(b * 128 + lane < count, piece, 0.0)
        out[:, pl.ds(pl.multiple_of(b * 128, 128), 128)] = piece
        return carry

    lax.fori_loop(0, out.shape[1] // 128, block, 0, unroll=8)


def over_chips(array, d, folds):
    return lax.ppermute(array, "fold", [((i + 2 * d) % folds, i) for i in range(folds)])


def other_core(array, folds):
    return lax.ppermute(array, "fold", [(i, i ^ 1) for i in range(folds)])


def on_device(right_side, initial, counts, columns, blocks):
    groups, folds = lax.axis_size("group"), lax.axis_size("fold")
    vectors, capacity = right_side.shape
    own, width, side = blocks.shape[0], blocks.shape[1], blocks.shape[2]
    size = width * side
    ob = own // folds
    steps = 4 if ob >= 12 else 2
    halo = HB * (steps - 1)
    lend = max(HB, sent_blocks(steps))
    rows = ob + 2 * halo
    pairs = coefficients()
    devices = groups * folds
    operator_shape = pltpu.VMEM((rows, size, 2 * side), BF16)


    payload_a = jax.ShapeDtypeStruct((2 * HB * steps - HB, vectors, side), F32)
    payload_b = jax.ShapeDtypeStruct((3 * HB + sent_blocks(steps), vectors, side), F32)

    line = [g * folds + (folds - 1 - p if g % 2 else p) for g in range(groups) for p in range(folds)]

    def swap(first, distance):
        ends = [(line[i], line[i + 1]) for i in range(first, devices - 1, distance)]
        return ends + [(j, i) for i, j in ends]

    swap_a, swap_b, swap_border = swap(0, 2), swap(1, 2), swap(folds - 1, folds)

    def fixed(array, space=pltpu.HBM):
        return pltpu.with_memory_space_constraint(array, space)

    flat = fixed(blocks.reshape(own * size, side))
    facts, indices, stacked, border = pl.pallas_call(
        functools.partial(first_kernel, folds, lend, width),
        out_shape=(
            pltpu.SMEM((COUNTS + folds,), jnp.int32),
            pltpu.SMEM((width, own), jnp.int32),
            pltpu.VMEM((2, vectors, capacity), F32),
            pltpu.VMEM((lend * size + 8, side), F32),
        ),
        in_specs=[HBM] * 5,
        out_specs=(SMEM, SMEM, VMEM, VMEM),
        scratch_shapes=[pltpu.SMEM((1, folds), jnp.int32), pltpu.SemaphoreType.DMA((4 + lend,))],
        compiler_params=params(),
    )(fixed(counts), fixed(columns.T), fixed(initial), fixed(right_side), flat)
    facts, indices = fixed(facts, pltpu.SMEM), fixed(indices, pltpu.SMEM)
    border = lax.ppermute(border, AXES, swap_border)
    far = [over_chips(stacked, d, folds) for d in range(1, folds // 2)]

    operator, token, offsets = pl.pallas_call(
        functools.partial(prepare_kernel, ob, halo, width),
        out_shape=(operator_shape, jax.ShapeDtypeStruct((8, 128), F32), pltpu.SMEM((rows * width,), jnp.int32)),
        in_specs=[SMEM, SMEM, HBM],
        out_specs=(VMEM, VMEM, SMEM),
        scratch_shapes=[
            pltpu.VMEM((rows, size, side), F32),
            pltpu.SemaphoreType.DMA((rows,)),
        ],
        compiler_params=params(),
        cost_estimate=pl.CostEstimate(flops=10**7, bytes_accessed=2 * rows * size * side * 4, transcendentals=0),
    )(facts, indices, flat)
    offsets = fixed(offsets, pltpu.SMEM)

    def gate(arrays, spaces, token):
        return pl.pallas_call(
            functools.partial(gate_kernel, len(arrays)),
            out_shape=tuple(space(array.shape, F32) for array, space in zip(arrays, spaces)),
            in_specs=[pl.BlockSpec(memory_space=space) for space in spaces] + [pl.BlockSpec(memory_space=pl.ANY)],
            out_specs=tuple(pl.BlockSpec(memory_space=space) for space in spaces),
            input_output_aliases={i: i for i in range(len(arrays))},
            compiler_params=params(),
        )(*[pltpu.with_memory_space_constraint(array, space) for array, space in zip(arrays, spaces)], token)

    far = gate(far, [pltpu.VMEM] * len(far), token)

    keys, arrays = [], []
    for d, array in enumerate([stacked, *far]):
        keys += [(d, False), (d, True)]
        arrays += [array, other_core(array, folds)]
    extent = ob + 2 * HB * steps
    state = (pltpu.VMEM((extent, vectors, side), F32),) * 3 + (pltpu.VMEM((extent, 2 * vectors, side), BF16),) * 2
    *held, pay_a = pl.pallas_call(
        functools.partial(align_kernel, ob, steps, keys),
        out_shape=(*state, payload_a),
        in_specs=[SMEM] + [VMEM] * folds,
        out_specs=(VMEM,) * 6,
        compiler_params=params(),
    )(facts, *[fixed(array, pltpu.VMEM) for array in arrays])

    *held, pay_b = pl.pallas_call(
        functools.partial(begin_kernel, ob, steps, pairs[0]),
        out_shape=(*state, payload_b),
        in_specs=[SMEM, SMEM] + [VMEM] * 6,
        out_specs=(VMEM,) * 6,
        input_output_aliases={3 + i: i for i in range(5)},
        compiler_params=params(),
    )(facts, offsets, fixed(operator, pltpu.VMEM), *[fixed(array, pltpu.VMEM) for array in held])

    def part_of_phase(kernel, operator, indices, held, got, outs):
        held = [pltpu.with_memory_space_constraint(array, pltpu.VMEM) for array in held]
        n = len(indices)
        results = pl.pallas_call(
            functools.partial(kernel, ob, folds, steps, done == 0, done + steps == APPLIES, pairs[done : done + steps + 1]),
            out_shape=(*state, *outs),
            in_specs=[SMEM] * (1 + n) + [VMEM] * 7,
            out_specs=(VMEM,) * (5 + len(outs)),
            input_output_aliases={2 + n + i: i for i in range(5)},
            compiler_params=params(),
        )(facts, *indices, pltpu.with_memory_space_constraint(operator, pltpu.VMEM), *held, got)
        return results[:5], results[5:]

    for done in range(0, APPLIES, steps):
        got_b = lax.ppermute(pay_b, AXES, swap_b)
        got_a = lax.ppermute(pay_a, AXES, swap_a)
        held, _ = part_of_phase(inner_kernel, operator, [offsets], held, got_a, ())
        if done == 0:
            operator, lent = pl.pallas_call(
                functools.partial(border_kernel, ob, folds, halo, lend, width),
                out_shape=(operator_shape, pltpu.SMEM((lend * width,), jnp.int32)),
                in_specs=[SMEM, VMEM, VMEM, pl.BlockSpec(memory_space=pl.ANY)],
                out_specs=(VMEM, SMEM),
                input_output_aliases={1: 0},
                scratch_shapes=[
                    pltpu.VMEM((8, 128), jnp.int32),
                    pltpu.SMEM((8, 128), jnp.int32),
                    pltpu.SemaphoreType.DMA(()),
                ],
                compiler_params=params(),
            )(facts, pltpu.with_memory_space_constraint(operator, pltpu.VMEM), border, held[0])
            lent = fixed(lent, pltpu.SMEM)
        if done + steps < APPLIES:
            held, (pay_a, pay_b) = part_of_phase(
                outer_kernel, operator, [offsets, lent], held, got_b, (payload_a, payload_b)
            )
        else:
            result = jax.ShapeDtypeStruct((ob, vectors, side), F32)
            held, (x,) = part_of_phase(outer_kernel, operator, [offsets, lent], held, got_b, (result,))
        if steps % 2:
            held = [*held[:3], held[4], held[3]]

    parts = []
    for d in range(folds // 2):
        piece = over_chips(x, d, folds) if d else x
        parts += [piece, other_core(piece, folds)]
    return pl.pallas_call(
        functools.partial(finish_kernel, ob, keys),
        out_shape=jax.ShapeDtypeStruct((vectors, capacity), F32),
        in_specs=[SMEM] + [VMEM] * folds,
        out_specs=VMEM,
        scratch_shapes=[pltpu.VMEM((own, vectors, side), F32)],
        compiler_params=params(),
    )(facts, *parts)


def solution(mesh):
    placed = (
        P(None, AXES),
        P(None, AXES),
        P("group", None),
        P("group", None),
        P("group", None, None, None),
    )
    return jax.shard_map(on_device, mesh=mesh, in_specs=placed, out_specs=P(None, AXES), check_vma=False)
```

```python
import functools

import jax
import jax.numpy as jnp
from jax import lax
from jax.experimental import pallas as pl
from jax.experimental.pallas import tpu as pltpu
from jax.sharding import PartitionSpec as P

HB = 3
SWEEPS = 3
DEGREE = 4
APPLIES = SWEEPS * DEGREE

upper_bound = 4.5
lower_bound = 1.35
THETA = (upper_bound + lower_bound) / 2.0

AXES = ("group", "fold")
F32 = jnp.float32
BF16 = jnp.bfloat16
VMEM = pl.BlockSpec(memory_space=pltpu.VMEM)
SMEM = pl.BlockSpec(memory_space=pltpu.SMEM)
HBM = pl.BlockSpec(memory_space=pltpu.HBM)


def coefficients():
    theta = THETA
    delta = (upper_bound - lower_bound) / 2.0
    pairs = []
    for sweep in range(SWEEPS):
        pairs.append((0.0, 1.0 / theta))
        ratio = delta / theta
        for step in range(1, DEGREE):
            ratio_next = 1.0 / (2.0 * theta / delta - ratio)
            pairs.append((ratio_next * ratio, 2.0 * ratio_next / delta))
            ratio = ratio_next
    return pairs


def params(limit=16):
    return pltpu.CompilerParams(vmem_limit_bytes=limit * 2**20)


def split(value):
    high = value.astype(BF16)
    return high, (value - high.astype(F32)).astype(BF16)


def pick_lanes(window, low, shift):
    lane = lax.broadcasted_iota(jnp.int32, (16, 128), 1)
    turn = (128 - shift) % 128
    first = pltpu.roll(window(low), turn, 1)
    second = pltpu.roll(window(low + 1), turn, 1)
    return jnp.where(lane < 128 - shift, first, second)


def put_near(ob, steps, even, u, r, pay):
    h = HB * steps
    inner = h - HB
    pay[:h] = u[pl.ds(jnp.where(even, ob, h), h)]
    if inner:
        pay[h:] = r[pl.ds(jnp.where(even, h + ob - inner, h), inner)]


def take_near(ob, steps, even, got, u, r, now):
    h = HB * steps
    inner = h - HB
    at = jnp.where(even, h + ob, 0)
    u[pl.ds(at, h)] = got[:h]
    if inner:
        r[pl.ds(jnp.where(even, h + ob, HB), inner)] = got[h:]
    high, low = split(got[:h])
    now[pl.ds(at, h), :16] = high
    now[pl.ds(at, h), 16:] = low


def sent_blocks(steps):
    return HB * (steps - 2)


def put_far(ob, steps, even, u, r, pay):
    h = HB * steps
    pay[: 2 * HB] = u[pl.ds(jnp.where(even, h, h + ob - 2 * HB), 2 * HB)]
    pay[2 * HB : 3 * HB] = r[pl.ds(jnp.where(even, h, h + ob - HB), HB)]


def put_far_ahead(ob, steps, even, u, pay):
    h, n = HB * steps, sent_blocks(steps)
    pay[3 * HB :] = u[pl.ds(jnp.where(even, h + HB, h + ob - HB - n), n)]


def take_far(ob, steps, even, got, u, r, now, later):
    h, n = HB * steps, sent_blocks(steps)
    high, low = split(got[: 2 * HB])
    at = jnp.where(even, h - 2 * HB, h + ob)
    now[pl.ds(at, 2 * HB), :16] = high
    now[pl.ds(at, 2 * HB), 16:] = low
    at = jnp.where(even, h - HB, h + ob)
    u[pl.ds(at, HB)] = got[pl.ds(jnp.where(even, HB, 0), HB)]
    r[pl.ds(at, HB)] = got[2 * HB : 3 * HB]
    if n:
        ahead = got[3 * HB :]
        at = jnp.where(even, h - HB - n, h + ob + HB)
        u[pl.ds(at, n)] = ahead
        r[pl.ds(at, n)] = ahead * THETA
        high, low = split(ahead)
        later[pl.ds(at, n), :16] = high
        later[pl.ds(at, n), 16:] = low


COUNTS = 4


def begin_of(facts, folds, j):
    total = 0
    for i in range(folds):
        total = total + jnp.where(i < j, facts[COUNTS + i], 0)
    return total


def holder(fold, folds, d, c):
    return lax.rem(fold // 2 + d, folds // 2) * 2 + jnp.where(c, 1 - fold % 2, fold % 2)


def part_of(fold, folds, backwards):
    return jnp.where(backwards == 1, folds - 1 - fold, fold)


def align_kernel(ob, folds, facts, *refs):
    sources, outs = refs[:2], refs[2:]
    capacity = sources[0].shape[-1]
    lane = lax.broadcasted_iota(jnp.int32, (16, 128), 1)
    spans = []
    for c in (False, True):
        owner = holder(facts[2], folds, 0, c)
        spans.append((begin_of(facts, folds, owner), facts[COUNTS + owner]))
    for d, out in enumerate(outs):
        base = part_of(holder(facts[2], folds, d, False), folds, facts[3]) * (ob * 128)

        def block(e, carry, out=out, base=base):
            row = base + e * 128
            totals = [jnp.zeros((16, 128), F32), jnp.zeros((16, 128), F32)]
            for source, (start, count) in zip(sources, spans):
                at = row - start
                low = at >> 7
                shift = at & 127
                index = at + lane
                valid = (index >= 0) & (index < count)
                for a in range(2):

                    def window(b, a=a, source=source):
                        b = jnp.clip(b, 0, capacity // 128 - 1)
                        return source[a, :, pl.ds(pl.multiple_of(b * 128, 128), 128)]

                    totals[a] = jnp.where(valid, pick_lanes(window, low, shift), totals[a])
            out[0, e] = totals[0]
            out[1, e] = totals[1]
            return carry

        lax.fori_loop(0, ob, block, 0, unroll=4)


def first_kernel(folds, lend, width, counts, columns, initial, right_side, blocks, facts, held, stacked, border, live, sem):
    own = columns.shape[1]
    size = blocks.shape[0] // own
    fold = lax.axis_index("fold")
    backwards = lax.rem(lax.axis_index("group"), 2)
    part = part_of(fold, folds, backwards)
    edge = (part == 0) | (part == folds - 1)
    first = jnp.where(part == 0, 0, own - lend)
    small = [pltpu.make_async_copy(columns, held, sem.at[0]), pltpu.make_async_copy(counts, live, sem.at[1])]
    pair = [pltpu.make_async_copy(array, stacked.at[i], sem.at[2 + i]) for i, array in enumerate((initial, right_side))]
    rows = []
    for i in range(lend):
        row = blocks.at[pl.ds(pl.multiple_of((first + i) * size, size), size)]
        rows.append(pltpu.make_async_copy(row, border.at[i * size : (i + 1) * size], sem.at[4 + i]))
    for copy in small:
        copy.start()

    @pl.when(edge)
    def _():
        for copy in rows:
            copy.start()

    for copy in pair:
        copy.start()
    for copy in small:
        copy.wait()
    for i, fact in enumerate((part, lax.rem(part, 2), fold, backwards)):
        facts[i] = fact
    for i in range(folds):
        facts[COUNTS + i] = live[0, i]

    @pl.when(edge)
    def _():
        lane = lax.broadcasted_iota(jnp.int32, (8, 128), 1)
        indices = jnp.zeros((8, 128), jnp.int32)
        for i in range(lend):
            for k in range(width):
                indices = jnp.where(lane == i * width + k, held[k, first + i], indices)
        border[lend * size :] = indices.astype(F32)
        for copy in rows:
            copy.wait()

    for copy in pair:
        copy.wait()


def put_row(out, a, raw):
    side = raw.shape[-1]
    for k in range(out.shape[1] // side):
        high, low = split(raw[k * side : (k + 1) * side])
        out[a, k * side : (k + 1) * side, :side] = high.T
        out[a, k * side : (k + 1) * side, side:] = low.T


def prepare_kernel(ob, halo, width, facts, columns, blocks, token, out, offsets, raw, sem):
    del token
    rows, size = raw.shape[0], raw.shape[1]
    own = blocks.shape[0] // size
    first = facts[0] * ob - halo

    def copy(a):
        i = pl.multiple_of(jnp.clip(first + a, 0, own - 1) * size, size)
        return pltpu.make_async_copy(blocks.at[pl.ds(i, size)], raw.at[a], sem.at[a])

    for a in range(rows):
        copy(a).start()

    def indices(a, carry):
        i = first + a
        for k in range(width):
            offsets[a * width + k] = columns[k, jnp.clip(i, 0, own - 1)] - HB - i
        return carry

    lax.fori_loop(0, rows, indices, 0)
    group = 4 if rows % 4 == 0 else 2

    def several(g, carry):
        for s in range(group):
            a = g * group + s
            copy(a).wait()
            put_row(out, a, raw.at[a])
        return carry

    lax.fori_loop(0, rows // group, several, 0)


def border_kernel(ob, folds, halo, lend, width, facts, prepared, raw, before, out, offsets, vector, scalars, sem):
    del prepared, before
    part = facts[0]
    size = out.shape[1]

    @pl.when((part == 0) | (part == folds - 1))
    def _():
        vector[...] = raw[lend * size :].astype(jnp.int32)
        copy = pltpu.make_async_copy(vector, scalars, sem)
        copy.start()
        first = jnp.where(part == 0, halo - lend, halo + ob)
        for a in range(lend):
            put_row(out, first + a, raw.at[a * size : (a + 1) * size])
        copy.wait()
        for i in range(lend):
            local = jnp.where(part == 0, ob * folds - lend + i, i)
            for k in range(width):
                offsets[i * width + k] = jnp.clip(scalars[0, i * width + k] - HB - local, -HB, HB)


def apply_rows(t, steps, starts, count, first, last, pair, offset, operator, x, u, r, pieces):
    now, later = pieces[t % 2], pieces[(t + 1) % 2]
    width = operator.shape[1] // 128
    old, new = pair
    final = last and t == steps - 1

    def row(n, carry):
        e = starts + n
        a = e - HB
        left = jnp.concatenate([now[e + offset(a, k)] for k in range(width)], axis=1)
        product = jnp.dot(left, operator[a], preferred_element_type=F32)
        product = product[:16] + product[16:]
        resid = r[e] - (product[:, :128] + product[:, 128:])
        before = u[e]
        update = new * resid if old == 0.0 else old * before + new * resid
        total = before if first and t == 0 else x[e] + before
        x[e] = total + update if final else total
        if not final:
            r[e] = resid
            u[e] = update
            high, low = split(update)
            later[e, :16] = high
            later[e, 16:] = low
        return carry

    lax.fori_loop(0, count, row, 0, unroll=True)


def look_up(offsets, width):
    return lambda a, k: offsets[a * width + k]


def ahead(ob, steps, even, first, pair, offset, operator, x, u, r, pieces):
    h, n = HB * steps, sent_blocks(steps)
    starts = jnp.where(even, h + HB, h + ob - HB - n)
    apply_rows(0, steps, starts, n, first, False, pair, offset, operator, x, u, r, pieces)


def begin_kernel(ob, steps, pair, facts, offsets, operator, *refs):
    partial, (x, u, r, *pieces), (pay_a, pay_b) = refs[:-7], refs[-7:-2], refs[-2:]
    h = HB * steps
    total = partial[0][...]
    for other in partial[1:]:
        total = total + other[...]
    u[h : h + ob] = total[0]
    r[h : h + ob] = total[1]
    high, low = split(total[0])
    pieces[0][h : h + ob, :16] = high
    pieces[0][h : h + ob, 16:] = low
    even = facts[1] == 0
    put_near(ob, steps, even, u, r, pay_a)
    put_far(ob, steps, even, u, r, pay_b)
    if sent_blocks(steps):
        ahead(ob, steps, even, True, pair, look_up(offsets, operator.shape[1] // 128), operator, x, u, r, pieces)
        put_far_ahead(ob, steps, even, u, pay_b)


def inner_kernel(ob, folds, steps, first, last, pairs, facts, offsets, operator, *refs):
    got_a, (x, u, r, *pieces) = refs[5], refs[6:]
    h = HB * steps
    even = facts[1] == 0
    offset = look_up(offsets, operator.shape[1] // 128)
    take_near(ob, steps, even, got_a, u, r, pieces[0])
    for t in range(steps):
        done = HB + (HB * t if t else sent_blocks(steps))
        starts = jnp.where(even, h + done, HB + HB * t)
        count = ob + h - HB - HB * t - done
        apply_rows(t, steps, starts, count, first, last, pairs[t], offset, operator, x, u, r, pieces)


def outer_kernel(ob, folds, steps, first, last, pairs, facts, offsets, lent, operator, *refs):
    got_b, (x, u, r, *pieces), outs = refs[5], refs[6:11], refs[11:]
    h = HB * steps
    inner = h - HB
    width = operator.shape[1] // 128
    lend = lent.shape[0] // width
    even = facts[1] == 0
    edge = (facts[0] == 0) | (facts[0] == folds - 1)
    take_far(ob, steps, even, got_b, u, r, *pieces)

    def offset(a, k):
        i = a - jnp.where(even, inner - lend, inner + ob)
        outside = edge & (i >= 0) & (i < lend)
        return jnp.where(outside, lent[jnp.clip(i, 0, lend - 1) * width + k], offsets[a * width + k])

    for t in range(steps):
        count = h if t else 2 * HB
        starts = jnp.where(even, HB + HB * t + h - count if not t else HB + HB * t, h + ob - HB - HB * t)
        apply_rows(t, steps, starts, count, first, last, pairs[t], offset, operator, x, u, r, pieces)
    if last:
        outs[0][...] = x[h : h + ob]
        return
    put_near(ob, steps, even, u, r, outs[0])
    put_far(ob, steps, even, u, r, outs[1])
    if sent_blocks(steps):
        pieces = pieces[::-1] if steps % 2 else pieces
        ahead(ob, steps, even, False, pairs[steps], look_up(offsets, width), operator, x, u, r, pieces)
        put_far_ahead(ob, steps, even, u, outs[1])


def finish_kernel(ob, keys, facts, *refs):
    parts, (out, whole) = refs[:-2], refs[-2:]
    total = whole.shape[0]
    for (d, c), part in zip(keys, parts):
        theirs = part_of(holder(facts[2], len(keys), d, c), len(keys), facts[3])
        whole[pl.ds(theirs * ob, ob)] = part[...]
    start, count = begin_of(facts, len(keys), facts[2]), facts[COUNTS + facts[2]]
    lane = lax.broadcasted_iota(jnp.int32, (16, 128), 1)
    low, shift = start >> 7, start & 127

    def block(b, carry):
        piece = pick_lanes(lambda i: whole[jnp.minimum(i, total - 1)], low + b, shift)
        piece = jnp.where(b * 128 + lane < count, piece, 0.0)
        out[:, pl.ds(pl.multiple_of(b * 128, 128), 128)] = piece
        return carry

    lax.fori_loop(0, out.shape[1] // 128, block, 0, unroll=8)


def over_chips(array, d, folds):
    return lax.ppermute(array, "fold", [((i + 2 * d) % folds, i) for i in range(folds)])


def other_core(array, folds):
    return lax.ppermute(array, "fold", [(i, i ^ 1) for i in range(folds)])


def on_device(right_side, initial, counts, columns, blocks):
    groups, folds = lax.axis_size("group"), lax.axis_size("fold")
    vectors, capacity = right_side.shape
    own, width, side = blocks.shape[0], blocks.shape[1], blocks.shape[2]
    size = width * side
    ob = own // folds
    steps = 3 if ob >= 9 else 2
    halo = HB * (steps - 1)
    lend = max(HB, sent_blocks(steps))
    rows = ob + 2 * halo
    pairs = coefficients()
    devices = groups * folds
    operator_shape = pltpu.VMEM((rows, size, 2 * side), BF16)


    payload_a = jax.ShapeDtypeStruct((2 * HB * steps - HB, vectors, side), F32)
    payload_b = jax.ShapeDtypeStruct((3 * HB + sent_blocks(steps), vectors, side), F32)

    line = [g * folds + (folds - 1 - p if g % 2 else p) for g in range(groups) for p in range(folds)]

    def swap(first, distance):
        ends = [(line[i], line[i + 1]) for i in range(first, devices - 1, distance)]
        return ends + [(j, i) for i, j in ends]

    swap_a, swap_b, swap_border = swap(0, 2), swap(1, 2), swap(folds - 1, folds)

    def fixed(array, space=pltpu.HBM):
        return pltpu.with_memory_space_constraint(array, space)

    flat = fixed(blocks.reshape(own * size, side))
    facts, indices, stacked, border = pl.pallas_call(
        functools.partial(first_kernel, folds, lend, width),
        out_shape=(
            pltpu.SMEM((COUNTS + folds,), jnp.int32),
            pltpu.SMEM((width, own), jnp.int32),
            pltpu.VMEM((2, vectors, capacity), F32),
            pltpu.VMEM((lend * size + 8, side), F32),
        ),
        in_specs=[HBM] * 5,
        out_specs=(SMEM, SMEM, VMEM, VMEM),
        scratch_shapes=[pltpu.SMEM((1, folds), jnp.int32), pltpu.SemaphoreType.DMA((4 + lend,))],
        compiler_params=params(),
    )(fixed(counts), fixed(columns.T), fixed(initial), fixed(right_side), flat)
    facts, indices = fixed(facts, pltpu.SMEM), fixed(indices, pltpu.SMEM)
    border = lax.ppermute(border, AXES, swap_border)
    mate = other_core(stacked, folds)
    rows_of = jax.ShapeDtypeStruct((2, ob, vectors, side), F32)
    partial = pl.pallas_call(
        functools.partial(align_kernel, ob, folds),
        out_shape=(rows_of,) * (folds // 2),
        in_specs=[SMEM, VMEM, VMEM],
        out_specs=(VMEM,) * (folds // 2),
        compiler_params=params(),
    )(facts, fixed(stacked, pltpu.VMEM), fixed(mate, pltpu.VMEM))
    sent = [over_chips(partial[d], folds // 2 - d, folds) for d in range(1, folds // 2)]

    operator, offsets = pl.pallas_call(
        functools.partial(prepare_kernel, ob, halo, width),
        out_shape=(operator_shape, pltpu.SMEM((rows * width,), jnp.int32)),
        in_specs=[SMEM, SMEM, HBM, pl.BlockSpec(memory_space=pl.ANY)],
        out_specs=(VMEM, SMEM),
        scratch_shapes=[pltpu.VMEM((rows, size, side), F32), pltpu.SemaphoreType.DMA((rows,))],
        compiler_params=params(32),
        cost_estimate=pl.CostEstimate(flops=10**7, bytes_accessed=2 * rows * size * side * 4, transcendentals=0),
    )(facts, indices, flat, partial[0])
    offsets = fixed(offsets, pltpu.SMEM)

    extent = ob + 2 * HB * steps
    state = (pltpu.VMEM((extent, vectors, side), F32),) * 3 + (pltpu.VMEM((extent, 2 * vectors, side), BF16),) * 2
    *held, pay_a, pay_b = pl.pallas_call(
        functools.partial(begin_kernel, ob, steps, pairs[0]),
        out_shape=(*state, payload_a, payload_b),
        in_specs=[SMEM, SMEM] + [VMEM] * (1 + folds // 2),
        out_specs=(VMEM,) * 7,
        compiler_params=params(),
    )(facts, offsets, fixed(operator, pltpu.VMEM), partial[0], *sent)

    def part_of_phase(kernel, operator, indices, held, got, outs):
        held = [pltpu.with_memory_space_constraint(array, pltpu.VMEM) for array in held]
        n = len(indices)
        results = pl.pallas_call(
            functools.partial(kernel, ob, folds, steps, done == 0, done + steps == APPLIES, pairs[done : done + steps + 1]),
            out_shape=(*state, *outs),
            in_specs=[SMEM] * (1 + n) + [VMEM] * 7,
            out_specs=(VMEM,) * (5 + len(outs)),
            input_output_aliases={2 + n + i: i for i in range(5)},
            compiler_params=params(),
        )(facts, *indices, pltpu.with_memory_space_constraint(operator, pltpu.VMEM), *held, got)
        return results[:5], results[5:]

    for done in range(0, APPLIES, steps):
        got_b = lax.ppermute(pay_b, AXES, swap_b)
        got_a = lax.ppermute(pay_a, AXES, swap_a)
        held, _ = part_of_phase(inner_kernel, operator, [offsets], held, got_a, ())
        if done == 0:
            operator, lent = pl.pallas_call(
                functools.partial(border_kernel, ob, folds, halo, lend, width),
                out_shape=(operator_shape, pltpu.SMEM((lend * width,), jnp.int32)),
                in_specs=[SMEM, VMEM, VMEM, pl.BlockSpec(memory_space=pl.ANY)],
                out_specs=(VMEM, SMEM),
                input_output_aliases={1: 0},
                scratch_shapes=[
                    pltpu.VMEM((8, 128), jnp.int32),
                    pltpu.SMEM((8, 128), jnp.int32),
                    pltpu.SemaphoreType.DMA(()),
                ],
                compiler_params=params(),
            )(facts, pltpu.with_memory_space_constraint(operator, pltpu.VMEM), border, held[0])
            lent = fixed(lent, pltpu.SMEM)
        if done + steps < APPLIES:
            held, (pay_a, pay_b) = part_of_phase(
                outer_kernel, operator, [offsets, lent], held, got_b, (payload_a, payload_b)
            )
        else:
            result = jax.ShapeDtypeStruct((ob, vectors, side), F32)
            held, (x,) = part_of_phase(outer_kernel, operator, [offsets, lent], held, got_b, (result,))
        if steps % 2:
            held = [*held[:3], held[4], held[3]]

    parts = []
    keys = [(d, c) for d in range(folds // 2) for c in (False, True)]
    for d in range(folds // 2):
        piece = over_chips(x, d, folds) if d else x
        parts += [piece, other_core(piece, folds)]
    return pl.pallas_call(
        functools.partial(finish_kernel, ob, keys),
        out_shape=jax.ShapeDtypeStruct((vectors, capacity), F32),
        in_specs=[SMEM] + [VMEM] * folds,
        out_specs=VMEM,
        scratch_shapes=[pltpu.VMEM((own, vectors, side), F32)],
        compiler_params=params(),
    )(facts, *parts)


def solution(mesh):
    placed = (
        P(None, AXES),
        P(None, AXES),
        P("group", None),
        P("group", None),
        P("group", None, None, None),
    )
    return jax.shard_map(on_device, mesh=mesh, in_specs=placed, out_specs=P(None, AXES), check_vma=False)
```

```python
import functools

import jax
import jax.numpy as jnp
from jax import lax
from jax.experimental import pallas as pl
from jax.experimental.pallas import tpu as pltpu
from jax.sharding import PartitionSpec as P

HB = 3
SWEEPS = 3
DEGREE = 4
APPLIES = SWEEPS * DEGREE

upper_bound = 4.5
lower_bound = 1.35
THETA = (upper_bound + lower_bound) / 2.0

AXES = ("group", "fold")
F32 = jnp.float32
BF16 = jnp.bfloat16
VMEM = pl.BlockSpec(memory_space=pltpu.VMEM)
SMEM = pl.BlockSpec(memory_space=pltpu.SMEM)
HBM = pl.BlockSpec(memory_space=pltpu.HBM)


def coefficients():
    theta = THETA
    delta = (upper_bound - lower_bound) / 2.0
    pairs = []
    for sweep in range(SWEEPS):
        pairs.append((0.0, 1.0 / theta))
        ratio = delta / theta
        for step in range(1, DEGREE):
            ratio_next = 1.0 / (2.0 * theta / delta - ratio)
            pairs.append((ratio_next * ratio, 2.0 * ratio_next / delta))
            ratio = ratio_next
    return pairs


def params(limit=16):
    return pltpu.CompilerParams(vmem_limit_bytes=limit * 2**20)


def split(value):
    high = value.astype(BF16)
    return high, (value - high.astype(F32)).astype(BF16)


def pick_lanes(window, low, shift):
    lane = lax.broadcasted_iota(jnp.int32, (16, 128), 1)
    turn = (128 - shift) % 128
    first = pltpu.roll(window(low), turn, 1)
    second = pltpu.roll(window(low + 1), turn, 1)
    return jnp.where(lane < 128 - shift, first, second)


def put_near(ob, steps, even, u, r, pay):
    h = HB * steps
    inner = h - HB
    pay[:h] = u[pl.ds(jnp.where(even, ob, h), h)]
    if inner:
        pay[h:] = r[pl.ds(jnp.where(even, h + ob - inner, h), inner)]


def take_near(ob, steps, even, got, u, r, now):
    h = HB * steps
    inner = h - HB
    at = jnp.where(even, h + ob, 0)
    u[pl.ds(at, h)] = got[:h]
    if inner:
        r[pl.ds(jnp.where(even, h + ob, HB), inner)] = got[h:]
    high, low = split(got[:h])
    now[pl.ds(at, h), :16] = high
    now[pl.ds(at, h), 16:] = low


def sent_blocks(steps):
    return HB * (steps - 2)


def put_far(ob, steps, even, u, r, pay):
    h = HB * steps
    pay[: 2 * HB] = u[pl.ds(jnp.where(even, h, h + ob - 2 * HB), 2 * HB)]
    pay[2 * HB : 3 * HB] = r[pl.ds(jnp.where(even, h, h + ob - HB), HB)]


def put_far_ahead(ob, steps, even, u, pay):
    h, n = HB * steps, sent_blocks(steps)
    pay[3 * HB :] = u[pl.ds(jnp.where(even, h + HB, h + ob - HB - n), n)]


def take_far(ob, steps, even, got, u, r, now, later):
    h, n = HB * steps, sent_blocks(steps)
    high, low = split(got[: 2 * HB])
    at = jnp.where(even, h - 2 * HB, h + ob)
    now[pl.ds(at, 2 * HB), :16] = high
    now[pl.ds(at, 2 * HB), 16:] = low
    at = jnp.where(even, h - HB, h + ob)
    u[pl.ds(at, HB)] = got[pl.ds(jnp.where(even, HB, 0), HB)]
    r[pl.ds(at, HB)] = got[2 * HB : 3 * HB]
    if n:
        ahead = got[3 * HB :]
        at = jnp.where(even, h - HB - n, h + ob + HB)
        u[pl.ds(at, n)] = ahead
        r[pl.ds(at, n)] = ahead * THETA
        high, low = split(ahead)
        later[pl.ds(at, n), :16] = high
        later[pl.ds(at, n), 16:] = low


COUNTS = 4


def begin_of(facts, folds, j):
    total = 0
    for i in range(folds):
        total = total + jnp.where(i < j, facts[COUNTS + i], 0)
    return total


def holder(fold, folds, d, c):
    return lax.rem(fold // 2 + d, folds // 2) * 2 + jnp.where(c, 1 - fold % 2, fold % 2)


def part_of(fold, folds, backwards):
    return jnp.where(backwards == 1, folds - 1 - fold, fold)


def align_kernel(ob, folds, facts, *refs):
    sources, outs = refs[:2], refs[2:]
    capacity = sources[0].shape[-1]
    lane = lax.broadcasted_iota(jnp.int32, (16, 128), 1)
    spans = []
    for c in (False, True):
        owner = holder(facts[2], folds, 0, c)
        spans.append((begin_of(facts, folds, owner), facts[COUNTS + owner]))
    for d, out in enumerate(outs):
        base = part_of(holder(facts[2], folds, d, False), folds, facts[3]) * (ob * 128)

        def block(e, carry, out=out, base=base):
            row = base + e * 128
            totals = [jnp.zeros((16, 128), F32), jnp.zeros((16, 128), F32)]
            for source, (start, count) in zip(sources, spans):
                at = row - start
                low = at >> 7
                shift = at & 127
                index = at + lane
                valid = (index >= 0) & (index < count)
                for a in range(2):

                    def window(b, a=a, source=source):
                        b = jnp.clip(b, 0, capacity // 128 - 1)
                        return source[a, :, pl.ds(pl.multiple_of(b * 128, 128), 128)]

                    totals[a] = jnp.where(valid, pick_lanes(window, low, shift), totals[a])
            out[0, e] = totals[0]
            out[1, e] = totals[1]
            return carry

        lax.fori_loop(0, ob, block, 0, unroll=4)


def first_kernel(folds, lend, width, counts, columns, initial, right_side, blocks, facts, held, stacked, border, live, sem):
    own = columns.shape[1]
    size = blocks.shape[0] // own
    fold = lax.axis_index("fold")
    backwards = lax.rem(lax.axis_index("group"), 2)
    part = part_of(fold, folds, backwards)
    edge = (part == 0) | (part == folds - 1)
    first = jnp.where(part == 0, 0, own - lend)
    small = [pltpu.make_async_copy(columns, held, sem.at[0]), pltpu.make_async_copy(counts, live, sem.at[1])]
    pair = [pltpu.make_async_copy(array, stacked.at[i], sem.at[2 + i]) for i, array in enumerate((initial, right_side))]
    rows = []
    for i in range(lend):
        row = blocks.at[pl.ds(pl.multiple_of((first + i) * size, size), size)]
        rows.append(pltpu.make_async_copy(row, border.at[i * size : (i + 1) * size], sem.at[4 + i]))
    for copy in small:
        copy.start()

    @pl.when(edge)
    def _():
        for copy in rows:
            copy.start()

    for copy in pair:
        copy.start()
    for copy in small:
        copy.wait()
    for i, fact in enumerate((part, lax.rem(part, 2), fold, backwards)):
        facts[i] = fact
    for i in range(folds):
        facts[COUNTS + i] = live[0, i]

    @pl.when(edge)
    def _():
        lane = lax.broadcasted_iota(jnp.int32, (8, 128), 1)
        indices = jnp.zeros((8, 128), jnp.int32)
        for i in range(lend):
            for k in range(width):
                indices = jnp.where(lane == i * width + k, held[k, first + i], indices)
        border[lend * size :] = indices.astype(F32)
        for copy in rows:
            copy.wait()

    for copy in pair:
        copy.wait()


def gate_kernel(*refs):
    del refs


def put_row(out, a, raw):
    side = raw.shape[-1]
    for k in range(out.shape[1] // side):
        high, low = split(raw[k * side : (k + 1) * side])
        out[a, k * side : (k + 1) * side, :side] = high.T
        out[a, k * side : (k + 1) * side, side:] = low.T


def prepare_kernel(ob, halo, width, facts, columns, blocks, token, out, offsets, raw, sem):
    del token
    rows, size = raw.shape[0], raw.shape[1]
    own = blocks.shape[0] // size
    first = facts[0] * ob - halo

    def copy(a):
        i = pl.multiple_of(jnp.clip(first + a, 0, own - 1) * size, size)
        return pltpu.make_async_copy(blocks.at[pl.ds(i, size)], raw.at[a], sem.at[a])

    for a in range(rows):
        copy(a).start()

    def indices(a, carry):
        i = first + a
        for k in range(width):
            offsets[a * width + k] = columns[k, jnp.clip(i, 0, own - 1)] - HB - i
        return carry

    lax.fori_loop(0, rows, indices, 0)
    group = 4 if rows % 4 == 0 else 2

    def several(g, carry):
        for s in range(group):
            a = g * group + s
            copy(a).wait()
            put_row(out, a, raw.at[a])
        return carry

    lax.fori_loop(0, rows // group, several, 0)


def border_kernel(ob, folds, halo, lend, width, facts, prepared, raw, before, out, offsets, vector, scalars, sem):
    del prepared, before
    part = facts[0]
    size = out.shape[1]

    @pl.when((part == 0) | (part == folds - 1))
    def _():
        vector[...] = raw[lend * size :].astype(jnp.int32)
        copy = pltpu.make_async_copy(vector, scalars, sem)
        copy.start()
        first = jnp.where(part == 0, halo - lend, halo + ob)
        for a in range(lend):
            put_row(out, first + a, raw.at[a * size : (a + 1) * size])
        copy.wait()
        for i in range(lend):
            local = jnp.where(part == 0, ob * folds - lend + i, i)
            for k in range(width):
                offsets[i * width + k] = jnp.clip(scalars[0, i * width + k] - HB - local, -HB, HB)


def apply_rows(t, steps, starts, count, first, last, pair, offset, operator, x, u, r, pieces):
    now, later = pieces[t % 2], pieces[(t + 1) % 2]
    width = operator.shape[1] // 128
    old, new = pair
    final = last and t == steps - 1

    def row(n, carry):
        e = starts + n
        a = e - HB
        left = jnp.concatenate([now[e + offset(a, k)] for k in range(width)], axis=1)
        product = jnp.dot(left, operator[a], preferred_element_type=F32)
        product = product[:16] + product[16:]
        resid = r[e] - (product[:, :128] + product[:, 128:])
        before = u[e]
        update = new * resid if old == 0.0 else old * before + new * resid
        total = before if first and t == 0 else x[e] + before
        x[e] = total + update if final else total
        if not final:
            r[e] = resid
            u[e] = update
            high, low = split(update)
            later[e, :16] = high
            later[e, 16:] = low
        return carry

    lax.fori_loop(0, count, row, 0, unroll=True)


def look_up(offsets, width):
    return lambda a, k: offsets[a * width + k]


def ahead(ob, steps, even, first, pair, offset, operator, x, u, r, pieces):
    h, n = HB * steps, sent_blocks(steps)
    starts = jnp.where(even, h + HB, h + ob - HB - n)
    apply_rows(0, steps, starts, n, first, False, pair, offset, operator, x, u, r, pieces)


def begin_kernel(ob, steps, pair, facts, offsets, operator, *refs):
    partial, (x, u, r, *pieces), (pay_a, pay_b) = refs[:-7], refs[-7:-2], refs[-2:]
    h = HB * steps
    total = partial[0][...]
    for other in partial[1:]:
        total = total + other[...]
    u[h : h + ob] = total[0]
    r[h : h + ob] = total[1]
    high, low = split(total[0])
    pieces[0][h : h + ob, :16] = high
    pieces[0][h : h + ob, 16:] = low
    even = facts[1] == 0
    put_near(ob, steps, even, u, r, pay_a)
    put_far(ob, steps, even, u, r, pay_b)
    if sent_blocks(steps):
        ahead(ob, steps, even, True, pair, look_up(offsets, operator.shape[1] // 128), operator, x, u, r, pieces)
        put_far_ahead(ob, steps, even, u, pay_b)


def inner_kernel(ob, folds, steps, first, last, pairs, facts, offsets, operator, *refs):
    got_a, (x, u, r, *pieces) = refs[5], refs[6:]
    h = HB * steps
    even = facts[1] == 0
    offset = look_up(offsets, operator.shape[1] // 128)
    take_near(ob, steps, even, got_a, u, r, pieces[0])
    for t in range(steps):
        done = HB + (HB * t if t else sent_blocks(steps))
        starts = jnp.where(even, h + done, HB + HB * t)
        count = ob + h - HB - HB * t - done
        apply_rows(t, steps, starts, count, first, last, pairs[t], offset, operator, x, u, r, pieces)


def outer_kernel(ob, folds, steps, first, last, pairs, facts, offsets, lent, operator, *refs):
    got_b, (x, u, r, *pieces), outs = refs[5], refs[6:11], refs[11:]
    h = HB * steps
    inner = h - HB
    width = operator.shape[1] // 128
    lend = lent.shape[0] // width
    even = facts[1] == 0
    edge = (facts[0] == 0) | (facts[0] == folds - 1)
    take_far(ob, steps, even, got_b, u, r, *pieces)

    def offset(a, k):
        i = a - jnp.where(even, inner - lend, inner + ob)
        outside = edge & (i >= 0) & (i < lend)
        return jnp.where(outside, lent[jnp.clip(i, 0, lend - 1) * width + k], offsets[a * width + k])

    for t in range(steps):
        count = h if t else 2 * HB
        starts = jnp.where(even, HB + HB * t + h - count if not t else HB + HB * t, h + ob - HB - HB * t)
        apply_rows(t, steps, starts, count, first, last, pairs[t], offset, operator, x, u, r, pieces)
    if last:
        outs[0][...] = x[h : h + ob]
        return
    put_near(ob, steps, even, u, r, outs[0])
    put_far(ob, steps, even, u, r, outs[1])
    if sent_blocks(steps):
        pieces = pieces[::-1] if steps % 2 else pieces
        ahead(ob, steps, even, False, pairs[steps], look_up(offsets, width), operator, x, u, r, pieces)
        put_far_ahead(ob, steps, even, u, outs[1])


def finish_kernel(ob, keys, facts, *refs):
    parts, (out, whole) = refs[:-2], refs[-2:]
    total = whole.shape[0]
    for (d, c), part in zip(keys, parts):
        theirs = part_of(holder(facts[2], len(keys), d, c), len(keys), facts[3])
        whole[pl.ds(theirs * ob, ob)] = part[...]
    start, count = begin_of(facts, len(keys), facts[2]), facts[COUNTS + facts[2]]
    lane = lax.broadcasted_iota(jnp.int32, (16, 128), 1)
    low, shift = start >> 7, start & 127

    def block(b, carry):
        piece = pick_lanes(lambda i: whole[jnp.minimum(i, total - 1)], low + b, shift)
        piece = jnp.where(b * 128 + lane < count, piece, 0.0)
        out[:, pl.ds(pl.multiple_of(b * 128, 128), 128)] = piece
        return carry

    lax.fori_loop(0, out.shape[1] // 128, block, 0, unroll=8)


def over_chips(array, d, folds):
    return lax.ppermute(array, "fold", [((i + 2 * d) % folds, i) for i in range(folds)])


def other_core(array, folds):
    return lax.ppermute(array, "fold", [(i, i ^ 1) for i in range(folds)])


def on_device(right_side, initial, counts, columns, blocks):
    groups, folds = lax.axis_size("group"), lax.axis_size("fold")
    vectors, capacity = right_side.shape
    own, width, side = blocks.shape[0], blocks.shape[1], blocks.shape[2]
    size = width * side
    ob = own // folds
    steps = 3 if ob >= 9 else 2
    halo = HB * (steps - 1)
    lend = max(HB, sent_blocks(steps))
    rows = ob + 2 * halo
    pairs = coefficients()
    devices = groups * folds
    operator_shape = pltpu.VMEM((rows, size, 2 * side), BF16)


    payload_a = jax.ShapeDtypeStruct((2 * HB * steps - HB, vectors, side), F32)
    payload_b = jax.ShapeDtypeStruct((3 * HB + sent_blocks(steps), vectors, side), F32)

    line = [g * folds + (folds - 1 - p if g % 2 else p) for g in range(groups) for p in range(folds)]

    def swap(first, distance):
        ends = [(line[i], line[i + 1]) for i in range(first, devices - 1, distance)]
        return ends + [(j, i) for i, j in ends]

    swap_a, swap_b, swap_border = swap(0, 2), swap(1, 2), swap(folds - 1, folds)

    def fixed(array, space=pltpu.HBM):
        return pltpu.with_memory_space_constraint(array, space)

    flat = fixed(blocks.reshape(own * size, side))
    facts, indices, stacked, border = pl.pallas_call(
        functools.partial(first_kernel, folds, lend, width),
        out_shape=(
            pltpu.SMEM((COUNTS + folds,), jnp.int32),
            pltpu.SMEM((width, own), jnp.int32),
            pltpu.VMEM((2, vectors, capacity), F32),
            pltpu.VMEM((lend * size + 8, side), F32),
        ),
        in_specs=[HBM] * 5,
        out_specs=(SMEM, SMEM, VMEM, VMEM),
        scratch_shapes=[pltpu.SMEM((1, folds), jnp.int32), pltpu.SemaphoreType.DMA((4 + lend,))],
        compiler_params=params(),
    )(fixed(counts), fixed(columns.T), fixed(initial), fixed(right_side), flat)
    facts, indices = fixed(facts, pltpu.SMEM), fixed(indices, pltpu.SMEM)
    mate = other_core(stacked, folds)
    rows_of = jax.ShapeDtypeStruct((2, ob, vectors, side), F32)
    partial = pl.pallas_call(
        functools.partial(align_kernel, ob, folds),
        out_shape=(rows_of,) * (folds // 2),
        in_specs=[SMEM, VMEM, VMEM],
        out_specs=(VMEM,) * (folds // 2),
        compiler_params=params(),
    )(facts, fixed(stacked, pltpu.VMEM), fixed(mate, pltpu.VMEM))
    sent = [over_chips(partial[d], folds // 2 - d, folds) for d in range(1, folds // 2)]
    border = pl.pallas_call(
        gate_kernel,
        out_shape=pltpu.VMEM(border.shape, F32),
        in_specs=[VMEM, pl.BlockSpec(memory_space=pl.ANY)],
        out_specs=VMEM,
        input_output_aliases={0: 0},
        compiler_params=params(),
    )(fixed(border, pltpu.VMEM), partial[0])
    border = lax.ppermute(border, AXES, swap_border)

    operator, offsets = pl.pallas_call(
        functools.partial(prepare_kernel, ob, halo, width),
        out_shape=(operator_shape, pltpu.SMEM((rows * width,), jnp.int32)),
        in_specs=[SMEM, SMEM, HBM, pl.BlockSpec(memory_space=pl.ANY)],
        out_specs=(VMEM, SMEM),
        scratch_shapes=[pltpu.VMEM((rows, size, side), F32), pltpu.SemaphoreType.DMA((rows,))],
        compiler_params=params(32),
        cost_estimate=pl.CostEstimate(flops=10**7, bytes_accessed=2 * rows * size * side * 4, transcendentals=0),
    )(facts, indices, flat, partial[0])
    offsets = fixed(offsets, pltpu.SMEM)

    extent = ob + 2 * HB * steps
    state = (pltpu.VMEM((extent, vectors, side), F32),) * 3 + (pltpu.VMEM((extent, 2 * vectors, side), BF16),) * 2
    *held, pay_a, pay_b = pl.pallas_call(
        functools.partial(begin_kernel, ob, steps, pairs[0]),
        out_shape=(*state, payload_a, payload_b),
        in_specs=[SMEM, SMEM] + [VMEM] * (1 + folds // 2),
        out_specs=(VMEM,) * 7,
        compiler_params=params(),
    )(facts, offsets, fixed(operator, pltpu.VMEM), partial[0], *sent)

    def part_of_phase(kernel, operator, indices, held, got, outs):
        held = [pltpu.with_memory_space_constraint(array, pltpu.VMEM) for array in held]
        n = len(indices)
        results = pl.pallas_call(
            functools.partial(kernel, ob, folds, steps, done == 0, done + steps == APPLIES, pairs[done : done + steps + 1]),
            out_shape=(*state, *outs),
            in_specs=[SMEM] * (1 + n) + [VMEM] * 7,
            out_specs=(VMEM,) * (5 + len(outs)),
            input_output_aliases={2 + n + i: i for i in range(5)},
            compiler_params=params(),
        )(facts, *indices, pltpu.with_memory_space_constraint(operator, pltpu.VMEM), *held, got)
        return results[:5], results[5:]

    for done in range(0, APPLIES, steps):
        got_b = lax.ppermute(pay_b, AXES, swap_b)
        got_a = lax.ppermute(pay_a, AXES, swap_a)
        held, _ = part_of_phase(inner_kernel, operator, [offsets], held, got_a, ())
        if done == 0:
            operator, lent = pl.pallas_call(
                functools.partial(border_kernel, ob, folds, halo, lend, width),
                out_shape=(operator_shape, pltpu.SMEM((lend * width,), jnp.int32)),
                in_specs=[SMEM, VMEM, VMEM, pl.BlockSpec(memory_space=pl.ANY)],
                out_specs=(VMEM, SMEM),
                input_output_aliases={1: 0},
                scratch_shapes=[
                    pltpu.VMEM((8, 128), jnp.int32),
                    pltpu.SMEM((8, 128), jnp.int32),
                    pltpu.SemaphoreType.DMA(()),
                ],
                compiler_params=params(),
            )(facts, pltpu.with_memory_space_constraint(operator, pltpu.VMEM), border, held[0])
            lent = fixed(lent, pltpu.SMEM)
        if done + steps < APPLIES:
            held, (pay_a, pay_b) = part_of_phase(
                outer_kernel, operator, [offsets, lent], held, got_b, (payload_a, payload_b)
            )
        else:
            result = jax.ShapeDtypeStruct((ob, vectors, side), F32)
            held, (x,) = part_of_phase(outer_kernel, operator, [offsets, lent], held, got_b, (result,))
        if steps % 2:
            held = [*held[:3], held[4], held[3]]

    parts = []
    keys = [(d, c) for d in range(folds // 2) for c in (False, True)]
    for d in range(folds // 2):
        piece = over_chips(x, d, folds) if d else x
        parts += [piece, other_core(piece, folds)]
    return pl.pallas_call(
        functools.partial(finish_kernel, ob, keys),
        out_shape=jax.ShapeDtypeStruct((vectors, capacity), F32),
        in_specs=[SMEM] + [VMEM] * folds,
        out_specs=VMEM,
        scratch_shapes=[pltpu.VMEM((own, vectors, side), F32)],
        compiler_params=params(),
    )(facts, *parts)


def solution(mesh):
    placed = (
        P(None, AXES),
        P(None, AXES),
        P("group", None),
        P("group", None),
        P("group", None, None, None),
    )
    return jax.shard_map(on_device, mesh=mesh, in_specs=placed, out_specs=P(None, AXES), check_vma=False)
```

```python
import functools

import jax
import jax.numpy as jnp
from jax import lax
from jax.experimental import pallas as pl
from jax.experimental.pallas import tpu as pltpu
from jax.sharding import PartitionSpec as P

HB = 3
SWEEPS = 3
DEGREE = 4
APPLIES = SWEEPS * DEGREE

upper_bound = 4.5
lower_bound = 1.35
THETA = (upper_bound + lower_bound) / 2.0

AXES = ("group", "fold")
F32 = jnp.float32
BF16 = jnp.bfloat16
VMEM = pl.BlockSpec(memory_space=pltpu.VMEM)
SMEM = pl.BlockSpec(memory_space=pltpu.SMEM)
HBM = pl.BlockSpec(memory_space=pltpu.HBM)


def coefficients():
    theta = THETA
    delta = (upper_bound - lower_bound) / 2.0
    pairs = []
    for sweep in range(SWEEPS):
        pairs.append((0.0, 1.0 / theta))
        ratio = delta / theta
        for step in range(1, DEGREE):
            ratio_next = 1.0 / (2.0 * theta / delta - ratio)
            pairs.append((ratio_next * ratio, 2.0 * ratio_next / delta))
            ratio = ratio_next
    return pairs


def params(limit=16):
    return pltpu.CompilerParams(vmem_limit_bytes=limit * 2**20)


def split(value):
    high = value.astype(BF16)
    return high, (value - high.astype(F32)).astype(BF16)


def pick_lanes(window, low, shift):
    lane = lax.broadcasted_iota(jnp.int32, (16, 128), 1)
    turn = (128 - shift) % 128
    first = pltpu.roll(window(low), turn, 1)
    second = pltpu.roll(window(low + 1), turn, 1)
    return jnp.where(lane < 128 - shift, first, second)


def put_near(ob, steps, even, u, r, pay):
    h = HB * steps
    inner = h - HB
    pay[:h] = u[pl.ds(jnp.where(even, ob, h), h)]
    if inner:
        pay[h:] = r[pl.ds(jnp.where(even, h + ob - inner, h), inner)]


def take_near(ob, steps, even, got, u, r, now):
    h = HB * steps
    inner = h - HB
    at = jnp.where(even, h + ob, 0)
    u[pl.ds(at, h)] = got[:h]
    if inner:
        r[pl.ds(jnp.where(even, h + ob, HB), inner)] = got[h:]
    high, low = split(got[:h])
    now[pl.ds(at, h), :16] = high
    now[pl.ds(at, h), 16:] = low


def sent_blocks(steps):
    return HB * (steps - 2)


def put_far(ob, steps, even, u, r, pay):
    h = HB * steps
    pay[: 2 * HB] = u[pl.ds(jnp.where(even, h, h + ob - 2 * HB), 2 * HB)]
    if pay.shape[0] - sent_blocks(steps) > 2 * HB:
        pay[2 * HB : 3 * HB] = r[pl.ds(jnp.where(even, h, h + ob - HB), HB)]


def put_far_ahead(ob, steps, even, u, pay):
    h, n = HB * steps, sent_blocks(steps)
    pay[pay.shape[0] - n :] = u[pl.ds(jnp.where(even, h + HB, h + ob - HB - n), n)]


def take_far(ob, steps, even, got, u, r, now, later):
    h, n = HB * steps, sent_blocks(steps)
    high, low = split(got[: 2 * HB])
    at = jnp.where(even, h - 2 * HB, h + ob)
    now[pl.ds(at, 2 * HB), :16] = high
    now[pl.ds(at, 2 * HB), 16:] = low
    at = jnp.where(even, h - HB, h + ob)
    nearest = got[pl.ds(jnp.where(even, HB, 0), HB)]
    u[pl.ds(at, HB)] = nearest
    r[pl.ds(at, HB)] = got[2 * HB : 3 * HB] if got.shape[0] - n > 2 * HB else nearest * THETA
    if n:
        ahead = got[got.shape[0] - n :]
        at = jnp.where(even, h - HB - n, h + ob + HB)
        u[pl.ds(at, n)] = ahead
        r[pl.ds(at, n)] = ahead * THETA
        high, low = split(ahead)
        later[pl.ds(at, n), :16] = high
        later[pl.ds(at, n), 16:] = low


COUNTS = 4


def begin_of(facts, folds, j):
    total = 0
    for i in range(folds):
        total = total + jnp.where(i < j, facts[COUNTS + i], 0)
    return total


def holder(fold, folds, d, c):
    return lax.rem(fold // 2 + d, folds // 2) * 2 + jnp.where(c, 1 - fold % 2, fold % 2)


def part_of(fold, folds, backwards):
    return jnp.where(backwards == 1, folds - 1 - fold, fold)


def align_kernel(ob, folds, lend, width, facts, indices, blocks, *refs):
    sources, outs, (border, sem) = refs[:2], refs[2:-2], refs[-2:]
    own = indices.shape[1]
    size = blocks.shape[0] // own
    edge = (facts[0] == 0) | (facts[0] == folds - 1)
    first = jnp.where(facts[0] == 0, 0, own - lend)

    def copies():
        for i in range(lend):
            row = blocks.at[pl.ds(pl.multiple_of((first + i) * size, size), size)]
            yield pltpu.make_async_copy(row, border.at[i * size : (i + 1) * size], sem.at[i])

    @pl.when(edge)
    def _():
        for copy in copies():
            copy.start()

    capacity = sources[0].shape[-1]
    lane = lax.broadcasted_iota(jnp.int32, (16, 128), 1)
    spans = []
    for c in (False, True):
        owner = holder(facts[2], folds, 0, c)
        spans.append((begin_of(facts, folds, owner), facts[COUNTS + owner]))
    for d, out in enumerate(outs):
        base = part_of(holder(facts[2], folds, d, False), folds, facts[3]) * (ob * 128)

        def block(e, carry, out=out, base=base):
            row = base + e * 128
            totals = [jnp.zeros((16, 128), F32), jnp.zeros((16, 128), F32)]
            for source, (start, count) in zip(sources, spans):
                at = row - start
                low = at >> 7
                shift = at & 127
                index = at + lane
                valid = (index >= 0) & (index < count)
                for a in range(2):

                    def window(b, a=a, source=source):
                        b = jnp.clip(b, 0, capacity // 128 - 1)
                        return source[a, :, pl.ds(pl.multiple_of(b * 128, 128), 128)]

                    totals[a] = jnp.where(valid, pick_lanes(window, low, shift), totals[a])
            out[0, e] = totals[0]
            out[1, e] = totals[1]
            return carry

        lax.fori_loop(0, ob, block, 0, unroll=4)

    @pl.when(edge)
    def _():
        place = lax.broadcasted_iota(jnp.int32, (8, 128), 1)
        lines = jnp.zeros((8, 128), jnp.int32)
        for i in range(lend):
            for k in range(width):
                lines = jnp.where(place == i * width + k, indices[k, first + i], lines)
        border[lend * size :] = lines.astype(F32)
        for copy in copies():
            copy.wait()


def first_kernel(folds, counts, columns, initial, right_side, facts, held, stacked, live, sem):
    fold = lax.axis_index("fold")
    backwards = lax.rem(lax.axis_index("group"), 2)
    part = part_of(fold, folds, backwards)
    small = [pltpu.make_async_copy(columns, held, sem.at[0]), pltpu.make_async_copy(counts, live, sem.at[1])]
    pair = [pltpu.make_async_copy(array, stacked.at[i], sem.at[2 + i]) for i, array in enumerate((initial, right_side))]
    for copy in pair + small:
        copy.start()
    for copy in small:
        copy.wait()
    for i, fact in enumerate((part, lax.rem(part, 2), fold, backwards)):
        facts[i] = fact
    for i in range(folds):
        facts[COUNTS + i] = live[0, i]
    for copy in pair:
        copy.wait()


def put_row(out, a, raw):
    side = raw.shape[-1]
    for k in range(out.shape[1] // side):
        high, low = split(raw[k * side : (k + 1) * side])
        out[a, k * side : (k + 1) * side, :side] = high.T
        out[a, k * side : (k + 1) * side, side:] = low.T


def prepare_kernel(ob, halo, lend, width, facts, columns, blocks, token, out, offsets, raw, sem):
    del token
    used, size = raw.shape[0], raw.shape[1]
    own = blocks.shape[0] // size
    first = facts[0] * ob - halo
    start = jnp.where(facts[1] == 0, halo - lend, 0)

    def copy(n):
        i = pl.multiple_of(jnp.clip(first + start + n, 0, own - 1) * size, size)
        return pltpu.make_async_copy(blocks.at[pl.ds(i, size)], raw.at[n], sem.at[n])

    for n in range(used):
        copy(n).start()

    def indices(a, carry):
        i = first + a
        for k in range(width):
            offsets[a * width + k] = columns[k, jnp.clip(i, 0, own - 1)] - HB - i
        return carry

    lax.fori_loop(0, ob + 2 * halo, indices, 0)
    group = max(n for n in (1, 2, 3, 4, 5) if used % n == 0)

    def several(g, carry):
        for s in range(group):
            n = g * group + s
            copy(n).wait()
            put_row(out, start + n, raw.at[n])
        return carry

    lax.fori_loop(0, used // group, several, 0)


def border_kernel(ob, folds, halo, lend, width, facts, prepared, raw, before, out, offsets, vector, scalars, sem):
    del prepared, before
    part = facts[0]
    size = out.shape[1]

    @pl.when((part == 0) | (part == folds - 1))
    def _():
        vector[...] = raw[lend * size :].astype(jnp.int32)
        copy = pltpu.make_async_copy(vector, scalars, sem)
        copy.start()
        first = jnp.where(part == 0, halo - lend, halo + ob)
        for a in range(lend):
            put_row(out, first + a, raw.at[a * size : (a + 1) * size])
        copy.wait()
        for i in range(lend):
            local = jnp.where(part == 0, ob * folds - lend + i, i)
            for k in range(width):
                offsets[i * width + k] = jnp.clip(scalars[0, i * width + k] - HB - local, -HB, HB)


def apply_rows(t, steps, starts, count, first, last, pair, offset, operator, x, u, r, pieces):
    now, later = pieces[t % 2], pieces[(t + 1) % 2]
    width = operator.shape[1] // 128
    old, new = pair
    final = last and t == steps - 1

    def row(n, carry):
        e = starts + n
        a = e - HB
        left = jnp.concatenate([now[e + offset(a, k)] for k in range(width)], axis=1)
        product = jnp.dot(left, operator[a], preferred_element_type=F32)
        product = product[:16] + product[16:]
        resid = r[e] - (product[:, :128] + product[:, 128:])
        before = u[e]
        update = new * resid if old == 0.0 else old * before + new * resid
        total = before if first and t == 0 else x[e] + before
        x[e] = total + update if final else total
        if not final:
            r[e] = resid
            u[e] = update
            high, low = split(update)
            later[e, :16] = high
            later[e, 16:] = low
        return carry

    lax.fori_loop(0, count, row, 0, unroll=True)


def look_up(offsets, width):
    return lambda a, k: offsets[a * width + k]


def ahead(ob, steps, even, first, pair, offset, operator, x, u, r, pieces):
    h, n = HB * steps, sent_blocks(steps)
    starts = jnp.where(even, h + HB, h + ob - HB - n)
    apply_rows(0, steps, starts, n, first, False, pair, offset, operator, x, u, r, pieces)


def begin_kernel(ob, steps, pair, facts, offsets, operator, *refs):
    partial, (x, u, r, *pieces), (pay_a, pay_b) = refs[:-7], refs[-7:-2], refs[-2:]
    h = HB * steps
    total = partial[0][...]
    for other in partial[1:]:
        total = total + other[...]
    u[h : h + ob] = total[0]
    r[h : h + ob] = total[1]
    high, low = split(total[0])
    pieces[0][h : h + ob, :16] = high
    pieces[0][h : h + ob, 16:] = low
    even = facts[1] == 0
    put_near(ob, steps, even, u, r, pay_a)
    put_far(ob, steps, even, u, r, pay_b)
    if sent_blocks(steps):
        ahead(ob, steps, even, True, pair, look_up(offsets, operator.shape[1] // 128), operator, x, u, r, pieces)
        put_far_ahead(ob, steps, even, u, pay_b)


def inner_kernel(ob, folds, steps, first, last, pairs, facts, offsets, operator, *refs):
    got_a, (x, u, r, *pieces) = refs[5], refs[6:]
    h = HB * steps
    even = facts[1] == 0
    offset = look_up(offsets, operator.shape[1] // 128)
    take_near(ob, steps, even, got_a, u, r, pieces[0])
    for t in range(steps):
        done = HB + (HB * t if t else sent_blocks(steps))
        starts = jnp.where(even, h + done, HB + HB * t)
        count = ob + h - HB - HB * t - done
        apply_rows(t, steps, starts, count, first, last, pairs[t], offset, operator, x, u, r, pieces)


def outer_kernel(ob, folds, steps, first, last, pairs, facts, offsets, lent, operator, *refs):
    got_b, (x, u, r, *pieces), outs = refs[5], refs[6:11], refs[11:]
    h = HB * steps
    inner = h - HB
    width = operator.shape[1] // 128
    lend = lent.shape[0] // width
    even = facts[1] == 0
    edge = (facts[0] == 0) | (facts[0] == folds - 1)
    take_far(ob, steps, even, got_b, u, r, *pieces)

    def offset(a, k):
        i = a - jnp.where(even, inner - lend, inner + ob)
        outside = edge & (i >= 0) & (i < lend)
        return jnp.where(outside, lent[jnp.clip(i, 0, lend - 1) * width + k], offsets[a * width + k])

    for t in range(steps):
        count = h if t else 2 * HB
        starts = jnp.where(even, HB + HB * t + h - count if not t else HB + HB * t, h + ob - HB - HB * t)
        apply_rows(t, steps, starts, count, first, last, pairs[t], offset, operator, x, u, r, pieces)
    if last:
        outs[0][...] = x[h : h + ob]
        return
    put_near(ob, steps, even, u, r, outs[0])
    put_far(ob, steps, even, u, r, outs[1])
    if sent_blocks(steps):
        pieces = pieces[::-1] if steps % 2 else pieces
        ahead(ob, steps, even, False, pairs[steps], look_up(offsets, width), operator, x, u, r, pieces)
        put_far_ahead(ob, steps, even, u, outs[1])


def finish_kernel(ob, keys, facts, *refs):
    parts, (out, whole) = refs[:-2], refs[-2:]
    total = whole.shape[0]
    for (d, c), part in zip(keys, parts):
        theirs = part_of(holder(facts[2], len(keys), d, c), len(keys), facts[3])
        whole[pl.ds(theirs * ob, ob)] = part[...]
    start, count = begin_of(facts, len(keys), facts[2]), facts[COUNTS + facts[2]]
    lane = lax.broadcasted_iota(jnp.int32, (16, 128), 1)
    low, shift = start >> 7, start & 127

    def block(b, carry):
        piece = pick_lanes(lambda i: whole[jnp.minimum(i, total - 1)], low + b, shift)
        piece = jnp.where(b * 128 + lane < count, piece, 0.0)
        out[:, pl.ds(pl.multiple_of(b * 128, 128), 128)] = piece
        return carry

    lax.fori_loop(0, out.shape[1] // 128, block, 0, unroll=8)


def over_chips(array, d, folds):
    return lax.ppermute(array, "fold", [((i + 2 * d) % folds, i) for i in range(folds)])


def other_core(array, folds):
    return lax.ppermute(array, "fold", [(i, i ^ 1) for i in range(folds)])


def on_device(right_side, initial, counts, columns, blocks):
    groups, folds = lax.axis_size("group"), lax.axis_size("fold")
    vectors, capacity = right_side.shape
    own, width, side = blocks.shape[0], blocks.shape[1], blocks.shape[2]
    size = width * side
    ob = own // folds
    steps = 3 if ob >= 9 else 2
    halo = HB * (steps - 1)
    lend = max(HB, sent_blocks(steps))
    rows = ob + 2 * halo
    pairs = coefficients()
    devices = groups * folds
    operator_shape = pltpu.VMEM((rows, size, 2 * side), BF16)


    payload_a = jax.ShapeDtypeStruct((2 * HB * steps - HB, vectors, side), F32)

    def payload_b(done):
        blocks = (2 if done and pairs[done - 1][0] == 0.0 else 3) * HB + sent_blocks(steps)
        return jax.ShapeDtypeStruct((blocks, vectors, side), F32)


    line = [g * folds + (folds - 1 - p if g % 2 else p) for g in range(groups) for p in range(folds)]

    def swap(first, distance):
        ends = [(line[i], line[i + 1]) for i in range(first, devices - 1, distance)]
        return ends + [(j, i) for i, j in ends]

    swap_a, swap_b, swap_border = swap(0, 2), swap(1, 2), swap(folds - 1, folds)

    def fixed(array, space=pltpu.HBM):
        return pltpu.with_memory_space_constraint(array, space)

    flat = fixed(blocks.reshape(own * size, side))
    facts, indices, stacked = pl.pallas_call(
        functools.partial(first_kernel, folds),
        out_shape=(
            pltpu.SMEM((COUNTS + folds,), jnp.int32),
            pltpu.SMEM((width, own), jnp.int32),
            pltpu.VMEM((2, vectors, capacity), F32),
        ),
        in_specs=[HBM] * 4,
        out_specs=(SMEM, SMEM, VMEM),
        scratch_shapes=[pltpu.SMEM((1, folds), jnp.int32), pltpu.SemaphoreType.DMA((4,))],
        compiler_params=params(),
    )(fixed(counts), fixed(columns.T), fixed(initial), fixed(right_side))
    facts, indices = fixed(facts, pltpu.SMEM), fixed(indices, pltpu.SMEM)
    mate = other_core(stacked, folds)

    rows_of = jax.ShapeDtypeStruct((2, ob, vectors, side), F32)
    *partial, border = pl.pallas_call(
        functools.partial(align_kernel, ob, folds, lend, width),
        out_shape=(rows_of,) * (folds // 2) + (pltpu.VMEM((lend * size + 8, side), F32),),
        in_specs=[SMEM, SMEM, HBM, VMEM, VMEM],
        out_specs=(VMEM,) * (1 + folds // 2),
        scratch_shapes=[pltpu.SemaphoreType.DMA((lend,))],
        compiler_params=params(),
    )(facts, indices, flat, fixed(stacked, pltpu.VMEM), fixed(mate, pltpu.VMEM))
    sent = [over_chips(partial[d], folds // 2 - d, folds) for d in range(1, folds // 2)]
    border = lax.ppermute(border, AXES, swap_border)

    used = ob + halo + lend
    operator, offsets = pl.pallas_call(
        functools.partial(prepare_kernel, ob, halo, lend, width),
        out_shape=(operator_shape, pltpu.SMEM((rows * width,), jnp.int32)),
        in_specs=[SMEM, SMEM, HBM, pl.BlockSpec(memory_space=pl.ANY)],
        out_specs=(VMEM, SMEM),
        scratch_shapes=[pltpu.VMEM((used, size, side), F32), pltpu.SemaphoreType.DMA((used,))],
        compiler_params=params(32),
        cost_estimate=pl.CostEstimate(flops=10**7, bytes_accessed=2 * rows * size * side * 4, transcendentals=0),
    )(facts, indices, flat, partial[0])
    offsets = fixed(offsets, pltpu.SMEM)

    extent = ob + 2 * HB * steps
    state = (pltpu.VMEM((extent, vectors, side), F32),) * 3 + (pltpu.VMEM((extent, 2 * vectors, side), BF16),) * 2
    *held, pay_a, pay_b = pl.pallas_call(
        functools.partial(begin_kernel, ob, steps, pairs[0]),
        out_shape=(*state, payload_a, payload_b(0)),
        in_specs=[SMEM, SMEM] + [VMEM] * (1 + folds // 2),
        out_specs=(VMEM,) * 7,
        compiler_params=params(),
    )(facts, offsets, fixed(operator, pltpu.VMEM), partial[0], *sent)

    def part_of_phase(kernel, operator, indices, held, got, outs):
        held = [pltpu.with_memory_space_constraint(array, pltpu.VMEM) for array in held]
        n = len(indices)
        results = pl.pallas_call(
            functools.partial(kernel, ob, folds, steps, done == 0, done + steps == APPLIES, pairs[done : done + steps + 1]),
            out_shape=(*state, *outs),
            in_specs=[SMEM] * (1 + n) + [VMEM] * 7,
            out_specs=(VMEM,) * (5 + len(outs)),
            input_output_aliases={2 + n + i: i for i in range(5)},
            compiler_params=params(),
        )(facts, *indices, pltpu.with_memory_space_constraint(operator, pltpu.VMEM), *held, got)
        return results[:5], results[5:]

    for done in range(0, APPLIES, steps):
        got_b = lax.ppermute(pay_b, AXES, swap_b)
        got_a = lax.ppermute(pay_a, AXES, swap_a)
        held, _ = part_of_phase(inner_kernel, operator, [offsets], held, got_a, ())
        if done == 0:
            operator, lent = pl.pallas_call(
                functools.partial(border_kernel, ob, folds, halo, lend, width),
                out_shape=(operator_shape, pltpu.SMEM((lend * width,), jnp.int32)),
                in_specs=[SMEM, VMEM, VMEM, pl.BlockSpec(memory_space=pl.ANY)],
                out_specs=(VMEM, SMEM),
                input_output_aliases={1: 0},
                scratch_shapes=[
                    pltpu.VMEM((8, 128), jnp.int32),
                    pltpu.SMEM((8, 128), jnp.int32),
                    pltpu.SemaphoreType.DMA(()),
                ],
                compiler_params=params(),
            )(facts, pltpu.with_memory_space_constraint(operator, pltpu.VMEM), border, held[0])
            lent = fixed(lent, pltpu.SMEM)
        if done + steps < APPLIES:
            held, (pay_a, pay_b) = part_of_phase(
                outer_kernel, operator, [offsets, lent], held, got_b, (payload_a, payload_b(done + steps))
            )
        else:
            result = jax.ShapeDtypeStruct((ob, vectors, side), F32)
            held, (x,) = part_of_phase(outer_kernel, operator, [offsets, lent], held, got_b, (result,))
        if steps % 2:
            held = [*held[:3], held[4], held[3]]

    parts = []
    keys = [(d, c) for d in range(folds // 2) for c in (False, True)]
    for d in range(folds // 2):
        piece = over_chips(x, d, folds) if d else x
        parts += [piece, other_core(piece, folds)]
    return pl.pallas_call(
        functools.partial(finish_kernel, ob, keys),
        out_shape=jax.ShapeDtypeStruct((vectors, capacity), F32),
        in_specs=[SMEM] + [VMEM] * folds,
        out_specs=VMEM,
        scratch_shapes=[pltpu.VMEM((own, vectors, side), F32)],
        compiler_params=params(),
    )(facts, *parts)


def solution(mesh):
    placed = (
        P(None, AXES),
        P(None, AXES),
        P("group", None),
        P("group", None),
        P("group", None, None, None),
    )
    return jax.shard_map(on_device, mesh=mesh, in_specs=placed, out_specs=P(None, AXES), check_vma=False)
```

```python
import functools

import jax
import jax.numpy as jnp
from jax import lax
from jax.experimental import pallas as pl
from jax.experimental.pallas import tpu as pltpu
from jax.sharding import PartitionSpec as P

HB = 3
SWEEPS = 3
DEGREE = 4
APPLIES = SWEEPS * DEGREE

upper_bound = 4.5
lower_bound = 1.35
THETA = (upper_bound + lower_bound) / 2.0

AXES = ("group", "fold")
F32 = jnp.float32
BF16 = jnp.bfloat16
VMEM = pl.BlockSpec(memory_space=pltpu.VMEM)
SMEM = pl.BlockSpec(memory_space=pltpu.SMEM)
HBM = pl.BlockSpec(memory_space=pltpu.HBM)


def coefficients():
    theta = THETA
    delta = (upper_bound - lower_bound) / 2.0
    pairs = []
    for sweep in range(SWEEPS):
        pairs.append((0.0, 1.0 / theta))
        ratio = delta / theta
        for step in range(1, DEGREE):
            ratio_next = 1.0 / (2.0 * theta / delta - ratio)
            pairs.append((ratio_next * ratio, 2.0 * ratio_next / delta))
            ratio = ratio_next
    return pairs


def params(limit=16):
    return pltpu.CompilerParams(vmem_limit_bytes=limit * 2**20)


def split(value):
    high = value.astype(BF16)
    return high, (value - high.astype(F32)).astype(BF16)


def pick_lanes(window, low, shift):
    lane = lax.broadcasted_iota(jnp.int32, (16, 128), 1)
    turn = (128 - shift) % 128
    first = pltpu.roll(window(low), turn, 1)
    second = pltpu.roll(window(low + 1), turn, 1)
    return jnp.where(lane < 128 - shift, first, second)


def choose(even, left, right):
    if isinstance(even, bool):
        return left if even else right
    return jnp.where(even, left, right)


def put_near(ob, steps, even, u, r, pay):
    h = HB * steps
    inner = h - HB
    pay[:h] = u[pl.ds(choose(even, ob, h), h)]
    if inner:
        pay[h:] = r[pl.ds(choose(even, h + ob - inner, h), inner)]


def take_near(ob, steps, even, got, u, r, now):
    h = HB * steps
    inner = h - HB
    at = choose(even, h + ob, 0)
    u[pl.ds(at, h)] = got[:h]
    if inner:
        r[pl.ds(choose(even, h + ob, HB), inner)] = got[h:]
    high, low = split(got[:h])
    now[pl.ds(at, h), :16] = high
    now[pl.ds(at, h), 16:] = low


def sent_blocks(steps):
    return HB * (steps - 2)


def put_far(ob, steps, even, u, r, pay):
    h = HB * steps
    pay[: 2 * HB] = u[pl.ds(choose(even, h, h + ob - 2 * HB), 2 * HB)]
    if pay.shape[0] - sent_blocks(steps) > 2 * HB:
        pay[2 * HB : 3 * HB] = r[pl.ds(choose(even, h, h + ob - HB), HB)]


def put_far_ahead(ob, steps, even, u, pay):
    h, n = HB * steps, sent_blocks(steps)
    pay[pay.shape[0] - n :] = u[pl.ds(choose(even, h + HB, h + ob - HB - n), n)]


def take_far(ob, steps, even, got, u, r, now, later):
    h, n = HB * steps, sent_blocks(steps)
    high, low = split(got[: 2 * HB])
    at = choose(even, h - 2 * HB, h + ob)
    now[pl.ds(at, 2 * HB), :16] = high
    now[pl.ds(at, 2 * HB), 16:] = low
    at = choose(even, h - HB, h + ob)
    nearest = got[pl.ds(choose(even, HB, 0), HB)]
    u[pl.ds(at, HB)] = nearest
    r[pl.ds(at, HB)] = got[2 * HB : 3 * HB] if got.shape[0] - n > 2 * HB else nearest * THETA
    if n:
        ahead = got[got.shape[0] - n :]
        at = choose(even, h - HB - n, h + ob + HB)
        u[pl.ds(at, n)] = ahead
        r[pl.ds(at, n)] = ahead * THETA
        high, low = split(ahead)
        later[pl.ds(at, n), :16] = high
        later[pl.ds(at, n), 16:] = low


COUNTS = 4


def begin_of(facts, folds, j):
    total = 0
    for i in range(folds):
        total = total + jnp.where(i < j, facts[COUNTS + i], 0)
    return total


def holder(fold, folds, d, c):
    return lax.rem(fold // 2 + d, folds // 2) * 2 + jnp.where(c, 1 - fold % 2, fold % 2)


def part_of(fold, folds, backwards):
    return jnp.where(backwards == 1, folds - 1 - fold, fold)


def align_kernel(ob, folds, lend, width, facts, indices, blocks, *refs):
    sources, outs, (border, sem) = refs[:2], refs[2:-2], refs[-2:]
    own = indices.shape[1]
    size = blocks.shape[0] // own
    edge = (facts[0] == 0) | (facts[0] == folds - 1)
    first = jnp.where(facts[0] == 0, 0, own - lend)

    def copies():
        for i in range(lend):
            row = blocks.at[pl.ds(pl.multiple_of((first + i) * size, size), size)]
            yield pltpu.make_async_copy(row, border.at[i * size : (i + 1) * size], sem.at[i])

    @pl.when(edge)
    def _():
        for copy in copies():
            copy.start()

    capacity = sources[0].shape[-1]
    lane = lax.broadcasted_iota(jnp.int32, (16, 128), 1)
    spans = []
    for c in (False, True):
        owner = holder(facts[2], folds, 0, c)
        spans.append((begin_of(facts, folds, owner), facts[COUNTS + owner]))
    for d, out in enumerate(outs):
        base = part_of(holder(facts[2], folds, d, False), folds, facts[3]) * (ob * 128)

        def block(e, carry, out=out, base=base):
            row = base + e * 128
            totals = [jnp.zeros((16, 128), F32), jnp.zeros((16, 128), F32)]
            for source, (start, count) in zip(sources, spans):
                at = row - start
                low = at >> 7
                shift = at & 127
                index = at + lane
                valid = (index >= 0) & (index < count)
                for a in range(2):

                    def window(b, a=a, source=source):
                        b = jnp.clip(b, 0, capacity // 128 - 1)
                        return source[a, :, pl.ds(pl.multiple_of(b * 128, 128), 128)]

                    totals[a] = jnp.where(valid, pick_lanes(window, low, shift), totals[a])
            out[0, e] = totals[0]
            out[1, e] = totals[1]
            return carry

        lax.fori_loop(0, ob, block, 0, unroll=4)

    @pl.when(edge)
    def _():
        place = lax.broadcasted_iota(jnp.int32, (8, 128), 1)
        lines = jnp.zeros((8, 128), jnp.int32)
        for i in range(lend):
            for k in range(width):
                lines = jnp.where(place == i * width + k, indices[k, first + i], lines)
        border[lend * size :] = lines.astype(F32)
        for copy in copies():
            copy.wait()


def first_kernel(folds, counts, columns, initial, right_side, facts, held, stacked, live, sem):
    fold = lax.axis_index("fold")
    backwards = lax.rem(lax.axis_index("group"), 2)
    part = part_of(fold, folds, backwards)
    small = [pltpu.make_async_copy(columns, held, sem.at[0]), pltpu.make_async_copy(counts, live, sem.at[1])]
    pair = [pltpu.make_async_copy(array, stacked.at[i], sem.at[2 + i]) for i, array in enumerate((initial, right_side))]
    for copy in pair + small:
        copy.start()
    for copy in small:
        copy.wait()
    for i, fact in enumerate((part, lax.rem(part, 2), fold, backwards)):
        facts[i] = fact
    for i in range(folds):
        facts[COUNTS + i] = live[0, i]
    for copy in pair:
        copy.wait()


def put_row(out, a, raw):
    side = raw.shape[-1]
    for k in range(out.shape[1] // side):
        high, low = split(raw[k * side : (k + 1) * side])
        out[a, k * side : (k + 1) * side, :side] = high.T
        out[a, k * side : (k + 1) * side, side:] = low.T


def prepare_kernel(ob, halo, lend, width, facts, columns, blocks, token, out, offsets, raw, sem):
    del token
    used, size = raw.shape[0], raw.shape[1]
    own = blocks.shape[0] // size
    first = facts[0] * ob - halo
    start = jnp.where(facts[1] == 0, halo - lend, 0)

    def copy(n):
        i = pl.multiple_of(jnp.clip(first + start + n, 0, own - 1) * size, size)
        return pltpu.make_async_copy(blocks.at[pl.ds(i, size)], raw.at[n], sem.at[n])

    for n in range(used):
        copy(n).start()

    def indices(a, carry):
        i = first + a
        for k in range(width):
            offsets[a * width + k] = columns[k, jnp.clip(i, 0, own - 1)] - HB - i
        return carry

    lax.fori_loop(0, ob + 2 * halo, indices, 0)
    group = max(n for n in (1, 2, 3, 4, 5) if used % n == 0)

    def several(g, carry):
        for s in range(group):
            n = g * group + s
            copy(n).wait()
            put_row(out, start + n, raw.at[n])
        return carry

    lax.fori_loop(0, used // group, several, 0)


def border_kernel(ob, folds, halo, lend, width, facts, prepared, raw, before, out, offsets, vector, scalars, sem):
    del prepared, before
    part = facts[0]
    size = out.shape[1]

    @pl.when((part == 0) | (part == folds - 1))
    def _():
        vector[...] = raw[lend * size :].astype(jnp.int32)
        copy = pltpu.make_async_copy(vector, scalars, sem)
        copy.start()
        first = jnp.where(part == 0, halo - lend, halo + ob)
        for a in range(lend):
            put_row(out, first + a, raw.at[a * size : (a + 1) * size])
        copy.wait()
        for i in range(lend):
            local = jnp.where(part == 0, ob * folds - lend + i, i)
            for k in range(width):
                offsets[i * width + k] = jnp.clip(scalars[0, i * width + k] - HB - local, -HB, HB)


def apply_rows(t, steps, starts, count, first, last, pair, offset, operator, x, u, r, pieces):
    now, later = pieces[t % 2], pieces[(t + 1) % 2]
    width = operator.shape[1] // 128
    old, new = pair
    final = last and t == steps - 1

    def row(n, carry):
        e = starts + n
        a = e - HB
        if isinstance(starts, int):
            near = [now[e + j] for j in range(-HB, HB + 1)]
            parts = []
            for k in range(width):
                place = offset(a, k)
                part = near[0]
                for j in range(1, 2 * HB + 1):
                    part = jnp.where(place == j - HB, near[j], part)
                parts.append(part)
            left = jnp.concatenate(parts, axis=1)
        else:
            left = jnp.concatenate([now[e + offset(a, k)] for k in range(width)], axis=1)
        product = jnp.dot(left, operator[a], preferred_element_type=F32)
        product = product[:16] + product[16:]
        resid = r[e] - (product[:, :128] + product[:, 128:])
        before = u[e]
        update = new * resid if old == 0.0 else old * before + new * resid
        total = before if first and t == 0 else x[e] + before
        x[e] = total + update if final else total
        if not final:
            r[e] = resid
            u[e] = update
            high, low = split(update)
            later[e, :16] = high
            later[e, 16:] = low
        return carry

    if isinstance(starts, int):
        for n in range(count):
            row(n, 0)
    else:
        lax.fori_loop(0, count, row, 0, unroll=True)


def look_up(offsets, width):
    return lambda a, k: offsets[a * width + k]


def ahead(ob, steps, even, first, pair, offset, operator, x, u, r, pieces):
    h, n = HB * steps, sent_blocks(steps)
    starts = choose(even, h + HB, h + ob - HB - n)
    apply_rows(0, steps, starts, n, first, False, pair, offset, operator, x, u, r, pieces)


def begin_kernel(ob, steps, pair, facts, offsets, operator, *refs):
    partial, (x, u, r, *pieces), (pay_a, pay_b) = refs[:-7], refs[-7:-2], refs[-2:]
    h = HB * steps
    total = partial[0][...]
    for other in partial[1:]:
        total = total + other[...]
    u[h : h + ob] = total[0]
    r[h : h + ob] = total[1]
    high, low = split(total[0])
    pieces[0][h : h + ob, :16] = high
    pieces[0][h : h + ob, 16:] = low
    for left in (True, False):

        @pl.when((facts[1] == 0) == left)
        def _():
            put_near(ob, steps, left, u, r, pay_a)
            put_far(ob, steps, left, u, r, pay_b)
            if sent_blocks(steps):
                offset = look_up(offsets, operator.shape[1] // 128)
                ahead(ob, steps, left, True, pair, offset, operator, x, u, r, pieces)
                put_far_ahead(ob, steps, left, u, pay_b)


def inner_kernel(ob, folds, steps, first, last, pairs, facts, offsets, operator, *refs):
    got_a, (x, u, r, *pieces) = refs[5], refs[6:]
    h = HB * steps
    even = facts[1] == 0
    offset = look_up(offsets, operator.shape[1] // 128)
    take_near(ob, steps, even, got_a, u, r, pieces[0])
    for left in (True, False):

        @pl.when(even == left)
        def _():
            for t in range(steps):
                done = HB + (HB * t if t else sent_blocks(steps))
                starts = h + done if left else HB + HB * t
                count = ob + h - HB - HB * t - done
                apply_rows(t, steps, starts, count, first, last, pairs[t], offset, operator, x, u, r, pieces)


def outer_kernel(ob, folds, steps, first, last, pairs, facts, offsets, lent, operator, *refs):
    got_b, (x, u, r, *pieces), outs = refs[5], refs[6:11], refs[11:]
    h = HB * steps
    inner = h - HB
    width = operator.shape[1] // 128
    lend = lent.shape[0] // width
    even = facts[1] == 0
    edge = (facts[0] == 0) | (facts[0] == folds - 1)
    take_far(ob, steps, even, got_b, u, r, *pieces)

    def offset(a, k):
        i = a - choose(left, inner - lend, inner + ob)
        if not 0 <= i < lend:
            return offsets[a * width + k]
        return jnp.where(edge, lent[i * width + k], offsets[a * width + k])

    for left in (True, False):

        @pl.when(even == left)
        def _():
            for t in range(steps):
                count = h if t else 2 * HB
                starts = (HB + HB * t if t else h - HB) if left else h + ob - HB - HB * t
                apply_rows(t, steps, starts, count, first, last, pairs[t], offset, operator, x, u, r, pieces)
            if last:
                outs[0][...] = x[h : h + ob]
                return
            put_near(ob, steps, left, u, r, outs[0])
            put_far(ob, steps, left, u, r, outs[1])
            if sent_blocks(steps):
                turned = pieces[::-1] if steps % 2 else pieces
                ahead(ob, steps, left, False, pairs[steps], look_up(offsets, width), operator, x, u, r, turned)
                put_far_ahead(ob, steps, left, u, outs[1])


def finish_kernel(ob, keys, facts, *refs):
    parts, (out, whole) = refs[:-2], refs[-2:]
    total = whole.shape[0]
    for (d, c), part in zip(keys, parts):
        theirs = part_of(holder(facts[2], len(keys), d, c), len(keys), facts[3])
        whole[pl.ds(theirs * ob, ob)] = part[...]
    start, count = begin_of(facts, len(keys), facts[2]), facts[COUNTS + facts[2]]
    lane = lax.broadcasted_iota(jnp.int32, (16, 128), 1)
    low, shift = start >> 7, start & 127

    def block(b, carry):
        piece = pick_lanes(lambda i: whole[jnp.minimum(i, total - 1)], low + b, shift)
        piece = jnp.where(b * 128 + lane < count, piece, 0.0)
        out[:, pl.ds(pl.multiple_of(b * 128, 128), 128)] = piece
        return carry

    lax.fori_loop(0, out.shape[1] // 128, block, 0, unroll=8)


def over_chips(array, d, folds):
    return lax.ppermute(array, "fold", [((i + 2 * d) % folds, i) for i in range(folds)])


def other_core(array, folds):
    return lax.ppermute(array, "fold", [(i, i ^ 1) for i in range(folds)])


def on_device(right_side, initial, counts, columns, blocks):
    groups, folds = lax.axis_size("group"), lax.axis_size("fold")
    vectors, capacity = right_side.shape
    own, width, side = blocks.shape[0], blocks.shape[1], blocks.shape[2]
    size = width * side
    ob = own // folds
    steps = 3 if ob >= 9 else 2
    halo = HB * (steps - 1)
    lend = max(HB, sent_blocks(steps))
    rows = ob + 2 * halo
    pairs = coefficients()
    devices = groups * folds
    operator_shape = pltpu.VMEM((rows, size, 2 * side), BF16)


    payload_a = jax.ShapeDtypeStruct((2 * HB * steps - HB, vectors, side), F32)

    def payload_b(done):
        blocks = (2 if done and pairs[done - 1][0] == 0.0 else 3) * HB + sent_blocks(steps)
        return jax.ShapeDtypeStruct((blocks, vectors, side), F32)


    line = [g * folds + (folds - 1 - p if g % 2 else p) for g in range(groups) for p in range(folds)]

    def swap(first, distance):
        ends = [(line[i], line[i + 1]) for i in range(first, devices - 1, distance)]
        return ends + [(j, i) for i, j in ends]

    swap_a, swap_b, swap_border = swap(0, 2), swap(1, 2), swap(folds - 1, folds)

    def fixed(array, space=pltpu.HBM):
        return pltpu.with_memory_space_constraint(array, space)

    flat = fixed(blocks.reshape(own * size, side))
    facts, indices, stacked = pl.pallas_call(
        functools.partial(first_kernel, folds),
        out_shape=(
            pltpu.SMEM((COUNTS + folds,), jnp.int32),
            pltpu.SMEM((width, own), jnp.int32),
            pltpu.VMEM((2, vectors, capacity), F32),
        ),
        in_specs=[HBM] * 4,
        out_specs=(SMEM, SMEM, VMEM),
        scratch_shapes=[pltpu.SMEM((1, folds), jnp.int32), pltpu.SemaphoreType.DMA((4,))],
        compiler_params=params(),
    )(fixed(counts), fixed(columns.T), fixed(initial), fixed(right_side))
    facts, indices = fixed(facts, pltpu.SMEM), fixed(indices, pltpu.SMEM)
    mate = other_core(stacked, folds)

    rows_of = jax.ShapeDtypeStruct((2, ob, vectors, side), F32)
    *partial, border = pl.pallas_call(
        functools.partial(align_kernel, ob, folds, lend, width),
        out_shape=(rows_of,) * (folds // 2) + (pltpu.VMEM((lend * size + 8, side), F32),),
        in_specs=[SMEM, SMEM, HBM, VMEM, VMEM],
        out_specs=(VMEM,) * (1 + folds // 2),
        scratch_shapes=[pltpu.SemaphoreType.DMA((lend,))],
        compiler_params=params(),
    )(facts, indices, flat, fixed(stacked, pltpu.VMEM), fixed(mate, pltpu.VMEM))
    sent = [over_chips(partial[d], folds // 2 - d, folds) for d in range(1, folds // 2)]
    border = lax.ppermute(border, AXES, swap_border)

    used = ob + halo + lend
    operator, offsets = pl.pallas_call(
        functools.partial(prepare_kernel, ob, halo, lend, width),
        out_shape=(operator_shape, pltpu.SMEM((rows * width,), jnp.int32)),
        in_specs=[SMEM, SMEM, HBM, pl.BlockSpec(memory_space=pl.ANY)],
        out_specs=(VMEM, SMEM),
        scratch_shapes=[pltpu.VMEM((used, size, side), F32), pltpu.SemaphoreType.DMA((used,))],
        compiler_params=params(32),
        cost_estimate=pl.CostEstimate(flops=10**7, bytes_accessed=2 * rows * size * side * 4, transcendentals=0),
    )(facts, indices, flat, partial[0])
    offsets = fixed(offsets, pltpu.SMEM)

    extent = ob + 2 * HB * steps
    state = (pltpu.VMEM((extent, vectors, side), F32),) * 3 + (pltpu.VMEM((extent, 2 * vectors, side), BF16),) * 2
    *held, pay_a, pay_b = pl.pallas_call(
        functools.partial(begin_kernel, ob, steps, pairs[0]),
        out_shape=(*state, payload_a, payload_b(0)),
        in_specs=[SMEM, SMEM] + [VMEM] * (1 + folds // 2),
        out_specs=(VMEM,) * 7,
        compiler_params=params(),
    )(facts, offsets, fixed(operator, pltpu.VMEM), partial[0], *sent)

    def part_of_phase(kernel, operator, indices, held, got, outs):
        held = [pltpu.with_memory_space_constraint(array, pltpu.VMEM) for array in held]
        n = len(indices)
        results = pl.pallas_call(
            functools.partial(kernel, ob, folds, steps, done == 0, done + steps == APPLIES, pairs[done : done + steps + 1]),
            out_shape=(*state, *outs),
            in_specs=[SMEM] * (1 + n) + [VMEM] * 7,
            out_specs=(VMEM,) * (5 + len(outs)),
            input_output_aliases={2 + n + i: i for i in range(5)},
            compiler_params=params(),
        )(facts, *indices, pltpu.with_memory_space_constraint(operator, pltpu.VMEM), *held, got)
        return results[:5], results[5:]

    for done in range(0, APPLIES, steps):
        got_b = lax.ppermute(pay_b, AXES, swap_b)
        got_a = lax.ppermute(pay_a, AXES, swap_a)
        held, _ = part_of_phase(inner_kernel, operator, [offsets], held, got_a, ())
        if done == 0:
            operator, lent = pl.pallas_call(
                functools.partial(border_kernel, ob, folds, halo, lend, width),
                out_shape=(operator_shape, pltpu.SMEM((lend * width,), jnp.int32)),
                in_specs=[SMEM, VMEM, VMEM, pl.BlockSpec(memory_space=pl.ANY)],
                out_specs=(VMEM, SMEM),
                input_output_aliases={1: 0},
                scratch_shapes=[
                    pltpu.VMEM((8, 128), jnp.int32),
                    pltpu.SMEM((8, 128), jnp.int32),
                    pltpu.SemaphoreType.DMA(()),
                ],
                compiler_params=params(),
            )(facts, pltpu.with_memory_space_constraint(operator, pltpu.VMEM), border, held[0])
            lent = fixed(lent, pltpu.SMEM)
        if done + steps < APPLIES:
            held, (pay_a, pay_b) = part_of_phase(
                outer_kernel, operator, [offsets, lent], held, got_b, (payload_a, payload_b(done + steps))
            )
        else:
            result = jax.ShapeDtypeStruct((ob, vectors, side), F32)
            held, (x,) = part_of_phase(outer_kernel, operator, [offsets, lent], held, got_b, (result,))
        if steps % 2:
            held = [*held[:3], held[4], held[3]]

    parts = []
    keys = [(d, c) for d in range(folds // 2) for c in (False, True)]
    for d in range(folds // 2):
        piece = over_chips(x, d, folds) if d else x
        parts += [piece, other_core(piece, folds)]
    return pl.pallas_call(
        functools.partial(finish_kernel, ob, keys),
        out_shape=jax.ShapeDtypeStruct((vectors, capacity), F32),
        in_specs=[SMEM] + [VMEM] * folds,
        out_specs=VMEM,
        scratch_shapes=[pltpu.VMEM((own, vectors, side), F32)],
        compiler_params=params(),
    )(facts, *parts)


def solution(mesh):
    placed = (
        P(None, AXES),
        P(None, AXES),
        P("group", None),
        P("group", None),
        P("group", None, None, None),
    )
    return jax.shard_map(on_device, mesh=mesh, in_specs=placed, out_specs=P(None, AXES), check_vma=False)
```

```python
import functools

import jax
import jax.numpy as jnp
from jax import lax
from jax.experimental import pallas as pl
from jax.experimental.pallas import tpu as pltpu
from jax.sharding import PartitionSpec as P

HB = 3
SWEEPS = 3
DEGREE = 4
APPLIES = SWEEPS * DEGREE

upper_bound = 4.5
lower_bound = 1.35
THETA = (upper_bound + lower_bound) / 2.0

AXES = ("group", "fold")
F32 = jnp.float32
BF16 = jnp.bfloat16
VMEM = pl.BlockSpec(memory_space=pltpu.VMEM)
SMEM = pl.BlockSpec(memory_space=pltpu.SMEM)
HBM = pl.BlockSpec(memory_space=pltpu.HBM)


def coefficients():
    theta = THETA
    delta = (upper_bound - lower_bound) / 2.0
    pairs = []
    for sweep in range(SWEEPS):
        pairs.append((0.0, 1.0 / theta))
        ratio = delta / theta
        for step in range(1, DEGREE):
            ratio_next = 1.0 / (2.0 * theta / delta - ratio)
            pairs.append((ratio_next * ratio, 2.0 * ratio_next / delta))
            ratio = ratio_next
    return pairs


def params(limit=16):
    return pltpu.CompilerParams(vmem_limit_bytes=limit * 2**20)


def split(value):
    high = value.astype(BF16)
    return high, (value - high.astype(F32)).astype(BF16)


def pick_lanes(window, low, shift):
    lane = lax.broadcasted_iota(jnp.int32, (16, 128), 1)
    turn = (128 - shift) % 128
    first = pltpu.roll(window(low), turn, 1)
    second = pltpu.roll(window(low + 1), turn, 1)
    return jnp.where(lane < 128 - shift, first, second)


def choose(even, left, right):
    if isinstance(even, bool):
        return left if even else right
    return jnp.where(even, left, right)


def put_near(ob, steps, even, u, r, pay):
    h = HB * steps
    inner = h - HB
    pay[:h] = u[pl.ds(choose(even, ob, h), h)]
    if inner:
        pay[h:] = r[pl.ds(choose(even, h + ob - inner, h), inner)]


def take_near(ob, steps, even, got, u, r, now):
    h = HB * steps
    inner = h - HB
    at = choose(even, h + ob, 0)
    u[pl.ds(at, h)] = got[:h]
    if inner:
        r[pl.ds(choose(even, h + ob, HB), inner)] = got[h:]
    high, low = split(got[:h])
    now[pl.ds(at, h), :16] = high
    now[pl.ds(at, h), 16:] = low


def sent_blocks(steps):
    return HB * (steps - 2)


def put_far(ob, steps, even, u, r, pay):
    h = HB * steps
    pay[: 2 * HB] = u[pl.ds(choose(even, h, h + ob - 2 * HB), 2 * HB)]
    if pay.shape[0] - sent_blocks(steps) > 2 * HB:
        pay[2 * HB : 3 * HB] = r[pl.ds(choose(even, h, h + ob - HB), HB)]


def put_far_ahead(ob, steps, even, u, pay):
    h, n = HB * steps, sent_blocks(steps)
    pay[pay.shape[0] - n :] = u[pl.ds(choose(even, h + HB, h + ob - HB - n), n)]


def take_far(ob, steps, even, got, u, r, now, later):
    h, n = HB * steps, sent_blocks(steps)
    high, low = split(got[: 2 * HB])
    at = choose(even, h - 2 * HB, h + ob)
    now[pl.ds(at, 2 * HB), :16] = high
    now[pl.ds(at, 2 * HB), 16:] = low
    at = choose(even, h - HB, h + ob)
    nearest = got[pl.ds(choose(even, HB, 0), HB)]
    u[pl.ds(at, HB)] = nearest
    r[pl.ds(at, HB)] = got[2 * HB : 3 * HB] if got.shape[0] - n > 2 * HB else nearest * THETA
    if n:
        ahead = got[got.shape[0] - n :]
        at = choose(even, h - HB - n, h + ob + HB)
        u[pl.ds(at, n)] = ahead
        r[pl.ds(at, n)] = ahead * THETA
        high, low = split(ahead)
        later[pl.ds(at, n), :16] = high
        later[pl.ds(at, n), 16:] = low


COUNTS = 4


def begin_of(facts, folds, j):
    total = 0
    for i in range(folds):
        total = total + jnp.where(i < j, facts[COUNTS + i], 0)
    return total


def holder(fold, folds, d, c):
    return lax.rem(fold // 2 + d, folds // 2) * 2 + jnp.where(c, 1 - fold % 2, fold % 2)


def part_of(fold, folds, backwards):
    return jnp.where(backwards == 1, folds - 1 - fold, fold)


def rows_of_parts(ob, folds, facts, sources, outs):
    capacity = sources[0].shape[-1]
    lane = lax.broadcasted_iota(jnp.int32, (16, 128), 1)
    spans = []
    for c in (False, True):
        owner = holder(facts[2], folds, 0, c)
        spans.append((begin_of(facts, folds, owner), facts[COUNTS + owner]))
    for d, out in outs:
        base = part_of(holder(facts[2], folds, d, False), folds, facts[3]) * (ob * 128)

        def block(e, carry, out=out, base=base):
            row = base + e * 128
            totals = [jnp.zeros((16, 128), F32), jnp.zeros((16, 128), F32)]
            for source, (start, count) in zip(sources, spans):
                at = row - start
                low = at >> 7
                shift = at & 127
                index = at + lane
                valid = (index >= 0) & (index < count)
                for a in range(2):

                    def window(b, a=a, source=source):
                        b = jnp.clip(b, 0, capacity // 128 - 1)
                        return source[a, :, pl.ds(pl.multiple_of(b * 128, 128), 128)]

                    totals[a] = jnp.where(valid, pick_lanes(window, low, shift), totals[a])
            out[0, e] = totals[0]
            out[1, e] = totals[1]
            return carry

        lax.fori_loop(0, ob, block, 0, unroll=True)


def align_kernel(ob, folds, facts, first, second, *outs):
    rows_of_parts(ob, folds, facts, (first, second), list(enumerate(outs, 1)))


def own_rows_kernel(ob, folds, facts, first, second, out):
    rows_of_parts(ob, folds, facts, (first, second), [(0, out)])


def first_kernel(folds, lend, width, counts, columns, initial, right_side, blocks, facts, held, stacked, border, live, sem):
    own = columns.shape[1]
    size = blocks.shape[0] // own
    fold = lax.axis_index("fold")
    backwards = lax.rem(lax.axis_index("group"), 2)
    part = part_of(fold, folds, backwards)
    edge = (part == 0) | (part == folds - 1)
    first = jnp.where(part == 0, 0, own - lend)
    small = [pltpu.make_async_copy(columns, held, sem.at[0]), pltpu.make_async_copy(counts, live, sem.at[1])]
    pair = [pltpu.make_async_copy(array, stacked.at[i], sem.at[2 + i]) for i, array in enumerate((initial, right_side))]
    rows = []
    for i in range(lend):
        row = blocks.at[pl.ds(pl.multiple_of((first + i) * size, size), size)]
        rows.append(pltpu.make_async_copy(row, border.at[i * size : (i + 1) * size], sem.at[4 + i]))
    for copy in small:
        copy.start()

    @pl.when(edge)
    def _():
        for copy in rows:
            copy.start()

    for copy in pair:
        copy.start()
    for copy in small:
        copy.wait()
    for i, fact in enumerate((part, lax.rem(part, 2), fold, backwards)):
        facts[i] = fact
    for i in range(folds):
        facts[COUNTS + i] = live[0, i]

    @pl.when(edge)
    def _():
        lane = lax.broadcasted_iota(jnp.int32, (8, 128), 1)
        indices = jnp.zeros((8, 128), jnp.int32)
        for i in range(lend):
            for k in range(width):
                indices = jnp.where(lane == i * width + k, held[k, first + i], indices)
        border[lend * size :] = indices.astype(F32)
        for copy in rows:
            copy.wait()

    for copy in pair:
        copy.wait()


def gate_kernel(*refs):
    del refs


def put_row(out, a, raw):
    side = raw.shape[-1]
    for k in range(out.shape[1] // side):
        high, low = split(raw[k * side : (k + 1) * side])
        out[a, k * side : (k + 1) * side, :side] = high.T
        out[a, k * side : (k + 1) * side, side:] = low.T


def prepare_kernel(ob, halo, lend, width, facts, columns, blocks, token, out, offsets, raw, sem):
    del token
    used, size = raw.shape[0], raw.shape[1]
    own = blocks.shape[0] // size
    first = facts[0] * ob - halo
    start = jnp.where(facts[1] == 0, halo - lend, 0)

    def copy(n):
        i = pl.multiple_of(jnp.clip(first + start + n, 0, own - 1) * size, size)
        return pltpu.make_async_copy(blocks.at[pl.ds(i, size)], raw.at[n], sem.at[n])

    for n in range(used):
        copy(n).start()

    def indices(a, carry):
        i = first + a
        for k in range(width):
            offsets[a * width + k] = columns[k, jnp.clip(i, 0, own - 1)] - HB - i
        return carry

    lax.fori_loop(0, ob + 2 * halo, indices, 0)
    group = max(n for n in (1, 2, 3, 4, 5) if used % n == 0)

    def several(g, carry):
        for s in range(group):
            n = g * group + s
            copy(n).wait()
            put_row(out, start + n, raw.at[n])
        return carry

    lax.fori_loop(0, used // group, several, 0)


def border_kernel(ob, folds, halo, lend, width, facts, prepared, raw, before, out, offsets, vector, scalars, sem):
    del prepared, before
    part = facts[0]
    size = out.shape[1]

    @pl.when((part == 0) | (part == folds - 1))
    def _():
        vector[...] = raw[lend * size :].astype(jnp.int32)
        copy = pltpu.make_async_copy(vector, scalars, sem)
        copy.start()
        first = jnp.where(part == 0, halo - lend, halo + ob)
        for a in range(lend):
            put_row(out, first + a, raw.at[a * size : (a + 1) * size])
        copy.wait()
        for i in range(lend):
            local = jnp.where(part == 0, ob * folds - lend + i, i)
            for k in range(width):
                offsets[i * width + k] = jnp.clip(scalars[0, i * width + k] - HB - local, -HB, HB)


def apply_rows(t, steps, starts, count, first, last, pair, offset, operator, x, u, r, pieces):
    now, later = pieces[t % 2], pieces[(t + 1) % 2]
    width = operator.shape[1] // 128
    old, new = pair
    final = last and t == steps - 1

    def row(n, carry):
        e = starts + n
        a = e - HB
        if isinstance(starts, int):
            near = [now[e + j] for j in range(-HB, HB + 1)]
            parts = []
            for k in range(width):
                place = offset(a, k)
                part = near[0]
                for j in range(1, 2 * HB + 1):
                    part = jnp.where(place == j - HB, near[j], part)
                parts.append(part)
            left = jnp.concatenate(parts, axis=1)
        else:
            left = jnp.concatenate([now[e + offset(a, k)] for k in range(width)], axis=1)
        product = jnp.dot(left, operator[a], preferred_element_type=F32)
        product = product[:16] + product[16:]
        resid = r[e] - (product[:, :128] + product[:, 128:])
        before = u[e]
        update = new * resid if old == 0.0 else old * before + new * resid
        total = before if first and t == 0 else x[e] + before
        x[e] = total + update if final else total
        if not final:
            r[e] = resid
            u[e] = update
            high, low = split(update)
            later[e, :16] = high
            later[e, 16:] = low
        return carry

    if isinstance(starts, int):
        for n in range(count):
            row(n, 0)
    else:
        lax.fori_loop(0, count, row, 0, unroll=True)


def look_up(offsets, width):
    return lambda a, k: offsets[a * width + k]


def ahead(ob, steps, even, first, pair, offset, operator, x, u, r, pieces):
    h, n = HB * steps, sent_blocks(steps)
    starts = choose(even, h + HB, h + ob - HB - n)
    apply_rows(0, steps, starts, n, first, False, pair, offset, operator, x, u, r, pieces)


def begin_kernel(ob, steps, pair, facts, offsets, operator, *refs):
    partial, (x, u, r, *pieces), (pay_a, pay_b) = refs[:-7], refs[-7:-2], refs[-2:]
    h = HB * steps
    total = partial[0][...]
    for other in partial[1:]:
        total = total + other[...]
    u[h : h + ob] = total[0]
    r[h : h + ob] = total[1]
    high, low = split(total[0])
    pieces[0][h : h + ob, :16] = high
    pieces[0][h : h + ob, 16:] = low
    for left in (True, False):

        @pl.when((facts[1] == 0) == left)
        def _():
            put_near(ob, steps, left, u, r, pay_a)
            put_far(ob, steps, left, u, r, pay_b)
            if sent_blocks(steps):
                offset = look_up(offsets, operator.shape[1] // 128)
                ahead(ob, steps, left, True, pair, offset, operator, x, u, r, pieces)
                put_far_ahead(ob, steps, left, u, pay_b)


def inner_kernel(ob, folds, steps, first, last, pairs, facts, offsets, operator, *refs):
    got_a, (x, u, r, *pieces) = refs[5], refs[6:]
    h = HB * steps
    even = facts[1] == 0
    offset = look_up(offsets, operator.shape[1] // 128)
    take_near(ob, steps, even, got_a, u, r, pieces[0])
    for left in (True, False):

        @pl.when(even == left)
        def _():
            for t in range(steps):
                done = HB + (HB * t if t else sent_blocks(steps))
                starts = h + done if left else HB + HB * t
                count = ob + h - HB - HB * t - done
                apply_rows(t, steps, starts, count, first, last, pairs[t], offset, operator, x, u, r, pieces)


def outer_kernel(ob, folds, steps, first, last, pairs, facts, offsets, lent, operator, *refs):
    got_b, (x, u, r, *pieces), outs = refs[5], refs[6:11], refs[11:]
    h = HB * steps
    inner = h - HB
    width = operator.shape[1] // 128
    lend = lent.shape[0] // width
    even = facts[1] == 0
    edge = (facts[0] == 0) | (facts[0] == folds - 1)
    take_far(ob, steps, even, got_b, u, r, *pieces)

    def offset(a, k):
        i = a - choose(left, inner - lend, inner + ob)
        if not 0 <= i < lend:
            return offsets[a * width + k]
        return jnp.where(edge, lent[i * width + k], offsets[a * width + k])

    for left in (True, False):

        @pl.when(even == left)
        def _():
            for t in range(steps):
                count = h if t else 2 * HB
                starts = (HB + HB * t if t else h - HB) if left else h + ob - HB - HB * t
                apply_rows(t, steps, starts, count, first, last, pairs[t], offset, operator, x, u, r, pieces)
            if last:
                outs[0][...] = x[h : h + ob]
                return
            put_near(ob, steps, left, u, r, outs[0])
            put_far(ob, steps, left, u, r, outs[1])
            if sent_blocks(steps):
                turned = pieces[::-1] if steps % 2 else pieces
                ahead(ob, steps, left, False, pairs[steps], look_up(offsets, width), operator, x, u, r, turned)
                put_far_ahead(ob, steps, left, u, outs[1])


def finish_kernel(ob, keys, facts, *refs):
    parts, (out, whole) = refs[:-2], refs[-2:]
    total = whole.shape[0]
    for (d, c), part in zip(keys, parts):
        theirs = part_of(holder(facts[2], len(keys), d, c), len(keys), facts[3])
        whole[pl.ds(theirs * ob, ob)] = part[...]
    start, count = begin_of(facts, len(keys), facts[2]), facts[COUNTS + facts[2]]
    lane = lax.broadcasted_iota(jnp.int32, (16, 128), 1)
    low, shift = start >> 7, start & 127

    def block(b, carry):
        piece = pick_lanes(lambda i: whole[jnp.minimum(i, total - 1)], low + b, shift)
        piece = jnp.where(b * 128 + lane < count, piece, 0.0)
        out[:, pl.ds(pl.multiple_of(b * 128, 128), 128)] = piece
        return carry

    lax.fori_loop(0, out.shape[1] // 128, block, 0, unroll=True)


def over_chips(array, d, folds):
    return lax.ppermute(array, "fold", [((i + 2 * d) % folds, i) for i in range(folds)])


def other_core(array, folds):
    return lax.ppermute(array, "fold", [(i, i ^ 1) for i in range(folds)])


def on_device(right_side, initial, counts, columns, blocks):
    groups, folds = lax.axis_size("group"), lax.axis_size("fold")
    vectors, capacity = right_side.shape
    own, width, side = blocks.shape[0], blocks.shape[1], blocks.shape[2]
    size = width * side
    ob = own // folds
    steps = 3 if ob >= 9 else 2
    halo = HB * (steps - 1)
    lend = max(HB, sent_blocks(steps))
    rows = ob + 2 * halo
    pairs = coefficients()
    devices = groups * folds
    operator_shape = pltpu.VMEM((rows, size, 2 * side), BF16)


    payload_a = jax.ShapeDtypeStruct((2 * HB * steps - HB, vectors, side), F32)

    def payload_b(done):
        blocks = (2 if done and pairs[done - 1][0] == 0.0 else 3) * HB + sent_blocks(steps)
        return jax.ShapeDtypeStruct((blocks, vectors, side), F32)


    line = [g * folds + (folds - 1 - p if g % 2 else p) for g in range(groups) for p in range(folds)]

    def swap(first, distance):
        ends = [(line[i], line[i + 1]) for i in range(first, devices - 1, distance)]
        return ends + [(j, i) for i, j in ends]

    swap_a, swap_b, swap_border = swap(0, 2), swap(1, 2), swap(folds - 1, folds)

    def fixed(array, space=pltpu.HBM):
        return pltpu.with_memory_space_constraint(array, space)

    flat = fixed(blocks.reshape(own * size, side))
    facts, indices, stacked, border = pl.pallas_call(
        functools.partial(first_kernel, folds, lend, width),
        out_shape=(
            pltpu.SMEM((COUNTS + folds,), jnp.int32),
            pltpu.SMEM((width, own), jnp.int32),
            pltpu.VMEM((2, vectors, capacity), F32),
            pltpu.VMEM((lend * size + 8, side), F32),
        ),
        in_specs=[HBM] * 5,
        out_specs=(SMEM, SMEM, VMEM, VMEM),
        scratch_shapes=[pltpu.SMEM((1, folds), jnp.int32), pltpu.SemaphoreType.DMA((4 + lend,))],
        compiler_params=params(),
    )(fixed(counts), fixed(columns.T), fixed(initial), fixed(right_side), flat)
    facts, indices = fixed(facts, pltpu.SMEM), fixed(indices, pltpu.SMEM)
    mate = other_core(stacked, folds)

    rows_of = jax.ShapeDtypeStruct((2, ob, vectors, side), F32)
    slots = [fixed(stacked, pltpu.VMEM), fixed(mate, pltpu.VMEM)]
    partial = pl.pallas_call(
        functools.partial(align_kernel, ob, folds),
        out_shape=(rows_of,) * (folds // 2 - 1),
        in_specs=[SMEM, VMEM, VMEM],
        out_specs=(VMEM,) * (folds // 2 - 1),
        compiler_params=params(),
    )(facts, *slots)
    sent = [over_chips(array, folds // 2 - d, folds) for d, array in enumerate(partial, 1)]
    border = pl.pallas_call(
        gate_kernel,
        out_shape=pltpu.VMEM(border.shape, F32),
        in_specs=[VMEM, pl.BlockSpec(memory_space=pl.ANY)],
        out_specs=VMEM,
        input_output_aliases={0: 0},
        compiler_params=params(),
    )(fixed(border, pltpu.VMEM), partial[0])
    border = lax.ppermute(border, AXES, swap_border)

    used = ob + halo + lend
    operator, offsets = pl.pallas_call(
        functools.partial(prepare_kernel, ob, halo, lend, width),
        out_shape=(operator_shape, pltpu.SMEM((rows * width,), jnp.int32)),
        in_specs=[SMEM, SMEM, HBM, pl.BlockSpec(memory_space=pl.ANY)],
        out_specs=(VMEM, SMEM),
        scratch_shapes=[pltpu.VMEM((used, size, side), F32), pltpu.SemaphoreType.DMA((used,))],
        compiler_params=params(32),
        cost_estimate=pl.CostEstimate(flops=10**7, bytes_accessed=2 * rows * size * side * 4, transcendentals=0),
    )(facts, indices, flat, partial[0])
    mine = pl.pallas_call(
        functools.partial(own_rows_kernel, ob, folds),
        out_shape=rows_of,
        in_specs=[SMEM, VMEM, VMEM],
        out_specs=VMEM,
        compiler_params=params(),
    )(facts, *slots)
    offsets = fixed(offsets, pltpu.SMEM)

    extent = ob + 2 * HB * steps
    state = (pltpu.VMEM((extent, vectors, side), F32),) * 3 + (pltpu.VMEM((extent, 2 * vectors, side), BF16),) * 2
    *held, pay_a, pay_b = pl.pallas_call(
        functools.partial(begin_kernel, ob, steps, pairs[0]),
        out_shape=(*state, payload_a, payload_b(0)),
        in_specs=[SMEM, SMEM] + [VMEM] * (1 + folds // 2),
        out_specs=(VMEM,) * 7,
        compiler_params=params(),
    )(facts, offsets, fixed(operator, pltpu.VMEM), mine, *sent)

    def part_of_phase(kernel, operator, indices, held, got, outs):
        held = [pltpu.with_memory_space_constraint(array, pltpu.VMEM) for array in held]
        n = len(indices)
        results = pl.pallas_call(
            functools.partial(kernel, ob, folds, steps, done == 0, done + steps == APPLIES, pairs[done : done + steps + 1]),
            out_shape=(*state, *outs),
            in_specs=[SMEM] * (1 + n) + [VMEM] * 7,
            out_specs=(VMEM,) * (5 + len(outs)),
            input_output_aliases={2 + n + i: i for i in range(5)},
            compiler_params=params(),
        )(facts, *indices, pltpu.with_memory_space_constraint(operator, pltpu.VMEM), *held, got)
        return results[:5], results[5:]

    for done in range(0, APPLIES, steps):
        got_b = lax.ppermute(pay_b, AXES, swap_b)
        got_a = lax.ppermute(pay_a, AXES, swap_a)
        held, _ = part_of_phase(inner_kernel, operator, [offsets], held, got_a, ())
        if done == 0:
            operator, lent = pl.pallas_call(
                functools.partial(border_kernel, ob, folds, halo, lend, width),
                out_shape=(operator_shape, pltpu.SMEM((lend * width,), jnp.int32)),
                in_specs=[SMEM, VMEM, VMEM, pl.BlockSpec(memory_space=pl.ANY)],
                out_specs=(VMEM, SMEM),
                input_output_aliases={1: 0},
                scratch_shapes=[
                    pltpu.VMEM((8, 128), jnp.int32),
                    pltpu.SMEM((8, 128), jnp.int32),
                    pltpu.SemaphoreType.DMA(()),
                ],
                compiler_params=params(),
            )(facts, pltpu.with_memory_space_constraint(operator, pltpu.VMEM), border, held[0])
            lent = fixed(lent, pltpu.SMEM)
        if done + steps < APPLIES:
            held, (pay_a, pay_b) = part_of_phase(
                outer_kernel, operator, [offsets, lent], held, got_b, (payload_a, payload_b(done + steps))
            )
        else:
            result = jax.ShapeDtypeStruct((ob, vectors, side), F32)
            held, (x,) = part_of_phase(outer_kernel, operator, [offsets, lent], held, got_b, (result,))
        if steps % 2:
            held = [*held[:3], held[4], held[3]]

    parts = []
    keys = [(d, c) for d in range(folds // 2) for c in (False, True)]
    for d in range(folds // 2):
        piece = over_chips(x, d, folds) if d else x
        parts += [piece, other_core(piece, folds)]
    return pl.pallas_call(
        functools.partial(finish_kernel, ob, keys),
        out_shape=jax.ShapeDtypeStruct((vectors, capacity), F32),
        in_specs=[SMEM] + [VMEM] * folds,
        out_specs=VMEM,
        scratch_shapes=[pltpu.VMEM((own, vectors, side), F32)],
        compiler_params=params(),
    )(facts, *parts)


def solution(mesh):
    placed = (
        P(None, AXES),
        P(None, AXES),
        P("group", None),
        P("group", None),
        P("group", None, None, None),
    )
    return jax.shard_map(on_device, mesh=mesh, in_specs=placed, out_specs=P(None, AXES), check_vma=False)
```

```python
import functools

import jax
import jax.numpy as jnp
from jax import lax
from jax.experimental import pallas as pl
from jax.experimental.pallas import tpu as pltpu
from jax.sharding import PartitionSpec as P

HB = 3
SWEEPS = 3
DEGREE = 4
APPLIES = SWEEPS * DEGREE

upper_bound = 4.5
lower_bound = 1.35
THETA = (upper_bound + lower_bound) / 2.0

AXES = ("group", "fold")
F32 = jnp.float32
BF16 = jnp.bfloat16
VMEM = pl.BlockSpec(memory_space=pltpu.VMEM)
SMEM = pl.BlockSpec(memory_space=pltpu.SMEM)
HBM = pl.BlockSpec(memory_space=pltpu.HBM)


def coefficients():
    theta = THETA
    delta = (upper_bound - lower_bound) / 2.0
    pairs = []
    for sweep in range(SWEEPS):
        pairs.append((0.0, 1.0 / theta))
        ratio = delta / theta
        for step in range(1, DEGREE):
            ratio_next = 1.0 / (2.0 * theta / delta - ratio)
            pairs.append((ratio_next * ratio, 2.0 * ratio_next / delta))
            ratio = ratio_next
    return pairs


def params(limit=16):
    return pltpu.CompilerParams(vmem_limit_bytes=limit * 2**20)


def split(value):
    high = value.astype(BF16)
    return high, (value - high.astype(F32)).astype(BF16)


def pick_lanes(window, low, shift):
    lane = lax.broadcasted_iota(jnp.int32, (16, 128), 1)
    turn = (128 - shift) % 128
    first = pltpu.roll(window(low), turn, 1)
    second = pltpu.roll(window(low + 1), turn, 1)
    return jnp.where(lane < 128 - shift, first, second)


def choose(even, left, right):
    if isinstance(even, bool):
        return left if even else right
    return jnp.where(even, left, right)


def put_near(ob, steps, even, u, r, pay):
    h = HB * steps
    inner = h - HB
    pay[:h] = u[pl.ds(choose(even, ob, h), h)]
    if inner:
        pay[h:] = r[pl.ds(choose(even, h + ob - inner, h), inner)]


def take_near(ob, steps, even, got, u, r, now):
    h = HB * steps
    inner = h - HB
    at = choose(even, h + ob, 0)
    u[pl.ds(at, h)] = got[:h]
    if inner:
        r[pl.ds(choose(even, h + ob, HB), inner)] = got[h:]
    high, low = split(got[:h])
    now[pl.ds(at, h), :16] = high
    now[pl.ds(at, h), 16:] = low


def sent_blocks(steps):
    return HB * (steps - 2)


def put_far(ob, steps, even, u, r, pay):
    h = HB * steps
    pay[: 2 * HB] = u[pl.ds(choose(even, h, h + ob - 2 * HB), 2 * HB)]
    if pay.shape[0] - sent_blocks(steps) > 2 * HB:
        pay[2 * HB : 3 * HB] = r[pl.ds(choose(even, h, h + ob - HB), HB)]


def put_far_ahead(ob, steps, even, u, pay):
    h, n = HB * steps, sent_blocks(steps)
    pay[pay.shape[0] - n :] = u[pl.ds(choose(even, h + HB, h + ob - HB - n), n)]


def take_far(ob, steps, even, got, u, r, now, later):
    h, n = HB * steps, sent_blocks(steps)
    high, low = split(got[: 2 * HB])
    at = choose(even, h - 2 * HB, h + ob)
    now[pl.ds(at, 2 * HB), :16] = high
    now[pl.ds(at, 2 * HB), 16:] = low
    at = choose(even, h - HB, h + ob)
    nearest = got[pl.ds(choose(even, HB, 0), HB)]
    u[pl.ds(at, HB)] = nearest
    r[pl.ds(at, HB)] = got[2 * HB : 3 * HB] if got.shape[0] - n > 2 * HB else nearest * THETA
    if n:
        ahead = got[got.shape[0] - n :]
        at = choose(even, h - HB - n, h + ob + HB)
        u[pl.ds(at, n)] = ahead
        r[pl.ds(at, n)] = ahead * THETA
        high, low = split(ahead)
        later[pl.ds(at, n), :16] = high
        later[pl.ds(at, n), 16:] = low


COUNTS = 4


def begin_of(facts, folds, j):
    total = 0
    for i in range(folds):
        total = total + jnp.where(i < j, facts[COUNTS + i], 0)
    return total


def holder(fold, folds, d, c):
    return lax.rem(fold // 2 + d, folds // 2) * 2 + jnp.where(c, 1 - fold % 2, fold % 2)


def part_of(fold, folds, backwards):
    return jnp.where(backwards == 1, folds - 1 - fold, fold)


def rows_of_parts(ob, folds, facts, sources, outs):
    capacity = sources[0].shape[-1]
    lane = lax.broadcasted_iota(jnp.int32, (16, 128), 1)
    spans = []
    for c in (False, True):
        owner = holder(facts[2], folds, 0, c)
        spans.append((begin_of(facts, folds, owner), facts[COUNTS + owner]))
    for d, out in outs:
        base = part_of(holder(facts[2], folds, d, False), folds, facts[3]) * (ob * 128)

        def block(e, carry, out=out, base=base):
            row = base + e * 128
            totals = [jnp.zeros((16, 128), F32), jnp.zeros((16, 128), F32)]
            for source, (start, count) in zip(sources, spans):
                at = row - start
                low = at >> 7
                shift = at & 127
                index = at + lane
                valid = (index >= 0) & (index < count)
                for a in range(2):

                    def window(b, a=a, source=source):
                        b = jnp.clip(b, 0, capacity // 128 - 1)
                        return source[a, :, pl.ds(pl.multiple_of(b * 128, 128), 128)]

                    totals[a] = jnp.where(valid, pick_lanes(window, low, shift), totals[a])
            out[0, e] = totals[0]
            out[1, e] = totals[1]
            return carry

        lax.fori_loop(0, ob, block, 0, unroll=True)


def align_kernel(ob, folds, facts, first, second, *outs):
    rows_of_parts(ob, folds, facts, (first, second), list(enumerate(outs, 1)))


def own_rows_kernel(ob, folds, facts, first, second, out):
    rows_of_parts(ob, folds, facts, (first, second), [(0, out)])


def first_kernel(folds, counts, columns, initial, right_side, facts, held, stacked, live, sem):
    fold = lax.axis_index("fold")
    backwards = lax.rem(lax.axis_index("group"), 2)
    part = part_of(fold, folds, backwards)
    small = [pltpu.make_async_copy(columns, held, sem.at[0]), pltpu.make_async_copy(counts, live, sem.at[1])]
    pair = [pltpu.make_async_copy(array, stacked.at[i], sem.at[2 + i]) for i, array in enumerate((initial, right_side))]
    for copy in pair + small:
        copy.start()
    for copy in small:
        copy.wait()
    for i, fact in enumerate((part, lax.rem(part, 2), fold, backwards)):
        facts[i] = fact
    for i in range(folds):
        facts[COUNTS + i] = live[0, i]
    for copy in pair:
        copy.wait()


def outward_kernel(folds, lend, width, facts, held, blocks, before, border, sem):
    del before
    own = held.shape[1]
    size = blocks.shape[0] // own
    part = facts[0]
    first = jnp.where(part == 0, 0, own - lend)

    @pl.when((part == 0) | (part == folds - 1))
    def _():
        rows = []
        for i in range(lend):
            row = blocks.at[pl.ds(pl.multiple_of((first + i) * size, size), size)]
            rows.append(pltpu.make_async_copy(row, border.at[i * size : (i + 1) * size], sem.at[i]))
        for copy in rows:
            copy.start()
        lane = lax.broadcasted_iota(jnp.int32, (8, 128), 1)
        indices = jnp.zeros((8, 128), jnp.int32)
        for i in range(lend):
            for k in range(width):
                indices = jnp.where(lane == i * width + k, held[k, first + i], indices)
        border[lend * size :] = indices.astype(F32)
        for copy in rows:
            copy.wait()


def gate_kernel(*refs):
    del refs


def put_row(out, a, raw):
    side = raw.shape[-1]
    for k in range(out.shape[1] // side):
        high, low = split(raw[k * side : (k + 1) * side])
        out[a, k * side : (k + 1) * side, :side] = high.T
        out[a, k * side : (k + 1) * side, side:] = low.T


def prepare_kernel(ob, halo, lend, width, facts, columns, blocks, token, out, offsets, raw, sem):
    del token
    used, size = raw.shape[0], raw.shape[1]
    own = blocks.shape[0] // size
    first = facts[0] * ob - halo
    start = jnp.where(facts[1] == 0, halo - lend, 0)

    def copy(n):
        i = pl.multiple_of(jnp.clip(first + start + n, 0, own - 1) * size, size)
        return pltpu.make_async_copy(blocks.at[pl.ds(i, size)], raw.at[n], sem.at[n])

    for n in range(used):
        copy(n).start()

    def indices(a, carry):
        i = first + a
        for k in range(width):
            offsets[a * width + k] = columns[k, jnp.clip(i, 0, own - 1)] - HB - i
        return carry

    lax.fori_loop(0, ob + 2 * halo, indices, 0)
    group = max(n for n in (1, 2, 3, 4, 5) if used % n == 0)

    def several(g, carry):
        for s in range(group):
            n = g * group + s
            copy(n).wait()
            put_row(out, start + n, raw.at[n])
        return carry

    lax.fori_loop(0, used // group, several, 0)


def border_kernel(ob, folds, halo, lend, width, facts, prepared, raw, before, out, offsets, vector, scalars, sem):
    del prepared, before
    part = facts[0]
    size = out.shape[1]

    @pl.when((part == 0) | (part == folds - 1))
    def _():
        vector[...] = raw[lend * size :].astype(jnp.int32)
        copy = pltpu.make_async_copy(vector, scalars, sem)
        copy.start()
        first = jnp.where(part == 0, halo - lend, halo + ob)
        for a in range(lend):
            put_row(out, first + a, raw.at[a * size : (a + 1) * size])
        copy.wait()
        for i in range(lend):
            local = jnp.where(part == 0, ob * folds - lend + i, i)
            for k in range(width):
                offsets[i * width + k] = jnp.clip(scalars[0, i * width + k] - HB - local, -HB, HB)


def apply_rows(t, steps, starts, count, first, last, pair, offset, operator, x, u, r, pieces):
    now, later = pieces[t % 2], pieces[(t + 1) % 2]
    width = operator.shape[1] // 128
    home = HB * steps
    old, new = pair
    final = last and t == steps - 1

    def row(n, carry):
        e = starts + n
        a = e - HB
        if isinstance(starts, int):
            near = [now[e + j] for j in range(-HB, HB + 1)]
            parts = []
            for k in range(width):
                place = offset(a, k)
                part = near[0]
                for j in range(1, 2 * HB + 1):
                    part = jnp.where(place == j - HB, near[j], part)
                parts.append(part)
            left = jnp.concatenate(parts, axis=1)
        else:
            left = jnp.concatenate([now[e + offset(a, k)] for k in range(width)], axis=1)
        product = jnp.dot(left, operator[a], preferred_element_type=F32)
        product = product[:16] + product[16:]
        resid = r[e] - (product[:, :128] + product[:, 128:])
        before = u[e]
        update = new * resid if old == 0.0 else old * before + new * resid
        if not isinstance(starts, int) or home <= e < x.shape[0] - home:
            total = before if first and t == 0 else x[e] + before
            x[e] = total + update if final else total
        if not final:
            r[e] = resid
            u[e] = update
            high, low = split(update)
            later[e, :16] = high
            later[e, 16:] = low
        return carry

    if isinstance(starts, int):
        for n in range(count):
            row(n, 0)
    else:
        lax.fori_loop(0, count, row, 0, unroll=True)


def look_up(offsets, width):
    return lambda a, k: offsets[a * width + k]


def ahead(ob, steps, even, first, pair, offset, operator, x, u, r, pieces):
    h, n = HB * steps, sent_blocks(steps)
    starts = choose(even, h + HB, h + ob - HB - n)
    apply_rows(0, steps, starts, n, first, False, pair, offset, operator, x, u, r, pieces)


def begin_kernel(ob, steps, pair, facts, offsets, operator, *refs):
    partial, (x, u, r, *pieces), (pay_a, pay_b) = refs[:-7], refs[-7:-2], refs[-2:]
    h = HB * steps
    total = partial[0][...]
    for other in partial[1:]:
        total = total + other[...]
    u[h : h + ob] = total[0]
    r[h : h + ob] = total[1]
    high, low = split(total[0])
    pieces[0][h : h + ob, :16] = high
    pieces[0][h : h + ob, 16:] = low
    for left in (True, False):

        @pl.when((facts[1] == 0) == left)
        def _():
            put_near(ob, steps, left, u, r, pay_a)
            put_far(ob, steps, left, u, r, pay_b)
            if sent_blocks(steps):
                offset = look_up(offsets, operator.shape[1] // 128)
                ahead(ob, steps, left, True, pair, offset, operator, x, u, r, pieces)
                put_far_ahead(ob, steps, left, u, pay_b)


def inner_kernel(ob, folds, steps, first, last, pairs, facts, offsets, operator, *refs):
    got_a, (x, u, r, *pieces) = refs[5], refs[6:]
    h = HB * steps
    even = facts[1] == 0
    offset = look_up(offsets, operator.shape[1] // 128)
    take_near(ob, steps, even, got_a, u, r, pieces[0])
    for left in (True, False):

        @pl.when(even == left)
        def _():
            for t in range(steps):
                done = HB + (HB * t if t else sent_blocks(steps))
                starts = h + done if left else HB + HB * t
                count = ob + h - HB - HB * t - done
                apply_rows(t, steps, starts, count, first, last, pairs[t], offset, operator, x, u, r, pieces)


def outer_kernel(ob, folds, steps, first, last, pairs, facts, offsets, lent, operator, *refs):
    got_b, (x, u, r, *pieces), outs = refs[5], refs[6:11], refs[11:]
    h = HB * steps
    inner = h - HB
    width = operator.shape[1] // 128
    lend = lent.shape[0] // width
    even = facts[1] == 0
    edge = (facts[0] == 0) | (facts[0] == folds - 1)
    take_far(ob, steps, even, got_b, u, r, *pieces)

    def offset(a, k):
        i = a - choose(left, inner - lend, inner + ob)
        if not 0 <= i < lend:
            return offsets[a * width + k]
        return jnp.where(edge, lent[i * width + k], offsets[a * width + k])

    for left in (True, False):

        @pl.when(even == left)
        def _():
            for t in range(steps):
                count = h if t else 2 * HB
                starts = (HB + HB * t if t else h - HB) if left else h + ob - HB - HB * t
                apply_rows(t, steps, starts, count, first, last, pairs[t], offset, operator, x, u, r, pieces)
            if last:
                outs[0][...] = x[h : h + ob]
                return
            put_near(ob, steps, left, u, r, outs[0])
            put_far(ob, steps, left, u, r, outs[1])
            if sent_blocks(steps):
                turned = pieces[::-1] if steps % 2 else pieces
                ahead(ob, steps, left, False, pairs[steps], look_up(offsets, width), operator, x, u, r, turned)
                put_far_ahead(ob, steps, left, u, outs[1])


def finish_kernel(ob, keys, facts, *refs):
    parts, (out, whole) = refs[:-2], refs[-2:]
    total = whole.shape[0]
    for (d, c), part in zip(keys, parts):
        theirs = part_of(holder(facts[2], len(keys), d, c), len(keys), facts[3])
        whole[pl.ds(theirs * ob, ob)] = part[...]
    start, count = begin_of(facts, len(keys), facts[2]), facts[COUNTS + facts[2]]
    lane = lax.broadcasted_iota(jnp.int32, (16, 128), 1)
    low, shift = start >> 7, start & 127

    def block(b, carry):
        piece = pick_lanes(lambda i: whole[jnp.minimum(i, total - 1)], low + b, shift)
        piece = jnp.where(b * 128 + lane < count, piece, 0.0)
        out[:, pl.ds(pl.multiple_of(b * 128, 128), 128)] = piece
        return carry

    lax.fori_loop(0, out.shape[1] // 128, block, 0, unroll=True)


def over_chips(array, d, folds):
    return lax.ppermute(array, "fold", [((i + 2 * d) % folds, i) for i in range(folds)])


def other_core(array, folds):
    return lax.ppermute(array, "fold", [(i, i ^ 1) for i in range(folds)])


def on_device(right_side, initial, counts, columns, blocks):
    groups, folds = lax.axis_size("group"), lax.axis_size("fold")
    vectors, capacity = right_side.shape
    own, width, side = blocks.shape[0], blocks.shape[1], blocks.shape[2]
    size = width * side
    ob = own // folds
    steps = 3 if ob >= 9 else 2
    halo = HB * (steps - 1)
    lend = max(HB, sent_blocks(steps))
    rows = ob + 2 * halo
    pairs = coefficients()
    devices = groups * folds
    operator_shape = pltpu.VMEM((rows, size, 2 * side), BF16)


    payload_a = jax.ShapeDtypeStruct((2 * HB * steps - HB, vectors, side), F32)

    def payload_b(done):
        blocks = (2 if done and pairs[done - 1][0] == 0.0 else 3) * HB + sent_blocks(steps)
        return jax.ShapeDtypeStruct((blocks, vectors, side), F32)


    line = [g * folds + (folds - 1 - p if g % 2 else p) for g in range(groups) for p in range(folds)]

    def swap(first, distance):
        ends = [(line[i], line[i + 1]) for i in range(first, devices - 1, distance)]
        return ends + [(j, i) for i, j in ends]

    swap_a, swap_b, swap_border = swap(0, 2), swap(1, 2), swap(folds - 1, folds)

    def fixed(array, space=pltpu.HBM):
        return pltpu.with_memory_space_constraint(array, space)

    flat = fixed(blocks.reshape(own * size, side))
    facts, indices, stacked = pl.pallas_call(
        functools.partial(first_kernel, folds),
        out_shape=(
            pltpu.SMEM((COUNTS + folds,), jnp.int32),
            pltpu.SMEM((width, own), jnp.int32),
            pltpu.VMEM((2, vectors, capacity), F32),
        ),
        in_specs=[HBM] * 4,
        out_specs=(SMEM, SMEM, VMEM),
        scratch_shapes=[pltpu.SMEM((1, folds), jnp.int32), pltpu.SemaphoreType.DMA((4,))],
        compiler_params=params(),
    )(fixed(counts), fixed(columns.T), fixed(initial), fixed(right_side))
    facts, indices = fixed(facts, pltpu.SMEM), fixed(indices, pltpu.SMEM)
    mate = other_core(stacked, folds)
    border = pl.pallas_call(
        functools.partial(outward_kernel, folds, lend, width),
        out_shape=pltpu.VMEM((lend * size + 8, side), F32),
        in_specs=[SMEM, SMEM, HBM, pl.BlockSpec(memory_space=pl.ANY)],
        out_specs=VMEM,
        scratch_shapes=[pltpu.SemaphoreType.DMA((lend,))],
        compiler_params=params(),
    )(facts, indices, flat, stacked)

    rows_of = jax.ShapeDtypeStruct((2, ob, vectors, side), F32)
    slots = [fixed(stacked, pltpu.VMEM), fixed(mate, pltpu.VMEM)]
    partial = pl.pallas_call(
        functools.partial(align_kernel, ob, folds),
        out_shape=(rows_of,) * (folds // 2 - 1),
        in_specs=[SMEM, VMEM, VMEM],
        out_specs=(VMEM,) * (folds // 2 - 1),
        compiler_params=params(),
    )(facts, *slots)
    sent = [over_chips(array, folds // 2 - d, folds) for d, array in enumerate(partial, 1)]
    border = pl.pallas_call(
        gate_kernel,
        out_shape=pltpu.VMEM(border.shape, F32),
        in_specs=[VMEM, pl.BlockSpec(memory_space=pl.ANY)],
        out_specs=VMEM,
        input_output_aliases={0: 0},
        compiler_params=params(),
    )(fixed(border, pltpu.VMEM), partial[0])
    border = lax.ppermute(border, AXES, swap_border)

    used = ob + halo + lend
    operator, offsets = pl.pallas_call(
        functools.partial(prepare_kernel, ob, halo, lend, width),
        out_shape=(operator_shape, pltpu.SMEM((rows * width,), jnp.int32)),
        in_specs=[SMEM, SMEM, HBM, pl.BlockSpec(memory_space=pl.ANY)],
        out_specs=(VMEM, SMEM),
        scratch_shapes=[pltpu.VMEM((used, size, side), F32), pltpu.SemaphoreType.DMA((used,))],
        compiler_params=params(32),
        cost_estimate=pl.CostEstimate(flops=10**7, bytes_accessed=2 * rows * size * side * 4, transcendentals=0),
    )(facts, indices, flat, partial[0])
    mine = pl.pallas_call(
        functools.partial(own_rows_kernel, ob, folds),
        out_shape=rows_of,
        in_specs=[SMEM, VMEM, VMEM],
        out_specs=VMEM,
        compiler_params=params(),
    )(facts, *slots)
    offsets = fixed(offsets, pltpu.SMEM)

    extent = ob + 2 * HB * steps
    state = (pltpu.VMEM((extent, vectors, side), F32),) * 3 + (pltpu.VMEM((extent, 2 * vectors, side), BF16),) * 2
    *held, pay_a, pay_b = pl.pallas_call(
        functools.partial(begin_kernel, ob, steps, pairs[0]),
        out_shape=(*state, payload_a, payload_b(0)),
        in_specs=[SMEM, SMEM] + [VMEM] * (1 + folds // 2),
        out_specs=(VMEM,) * 7,
        compiler_params=params(),
    )(facts, offsets, fixed(operator, pltpu.VMEM), mine, *sent)

    def part_of_phase(kernel, operator, indices, held, got, outs):
        held = [pltpu.with_memory_space_constraint(array, pltpu.VMEM) for array in held]
        n = len(indices)
        results = pl.pallas_call(
            functools.partial(kernel, ob, folds, steps, done == 0, done + steps == APPLIES, pairs[done : done + steps + 1]),
            out_shape=(*state, *outs),
            in_specs=[SMEM] * (1 + n) + [VMEM] * 7,
            out_specs=(VMEM,) * (5 + len(outs)),
            input_output_aliases={2 + n + i: i for i in range(5)},
            compiler_params=params(),
        )(facts, *indices, pltpu.with_memory_space_constraint(operator, pltpu.VMEM), *held, got)
        return results[:5], results[5:]

    for done in range(0, APPLIES, steps):
        got_b = lax.ppermute(pay_b, AXES, swap_b)
        got_a = lax.ppermute(pay_a, AXES, swap_a)
        held, _ = part_of_phase(inner_kernel, operator, [offsets], held, got_a, ())
        if done == 0:
            operator, lent = pl.pallas_call(
                functools.partial(border_kernel, ob, folds, halo, lend, width),
                out_shape=(operator_shape, pltpu.SMEM((lend * width,), jnp.int32)),
                in_specs=[SMEM, VMEM, VMEM, pl.BlockSpec(memory_space=pl.ANY)],
                out_specs=(VMEM, SMEM),
                input_output_aliases={1: 0},
                scratch_shapes=[
                    pltpu.VMEM((8, 128), jnp.int32),
                    pltpu.SMEM((8, 128), jnp.int32),
                    pltpu.SemaphoreType.DMA(()),
                ],
                compiler_params=params(),
            )(facts, pltpu.with_memory_space_constraint(operator, pltpu.VMEM), border, held[0])
            lent = fixed(lent, pltpu.SMEM)
        if done + steps < APPLIES:
            held, (pay_a, pay_b) = part_of_phase(
                outer_kernel, operator, [offsets, lent], held, got_b, (payload_a, payload_b(done + steps))
            )
        else:
            result = jax.ShapeDtypeStruct((ob, vectors, side), F32)
            held, (x,) = part_of_phase(outer_kernel, operator, [offsets, lent], held, got_b, (result,))
        if steps % 2:
            held = [*held[:3], held[4], held[3]]

    parts = []
    keys = [(d, c) for d in range(folds // 2) for c in (False, True)]
    for d in range(folds // 2):
        piece = over_chips(x, d, folds) if d else x
        parts += [piece, other_core(piece, folds)]
    return pl.pallas_call(
        functools.partial(finish_kernel, ob, keys),
        out_shape=jax.ShapeDtypeStruct((vectors, capacity), F32),
        in_specs=[SMEM] + [VMEM] * folds,
        out_specs=VMEM,
        scratch_shapes=[pltpu.VMEM((own, vectors, side), F32)],
        compiler_params=params(),
    )(facts, *parts)


def solution(mesh):
    placed = (
        P(None, AXES),
        P(None, AXES),
        P("group", None),
        P("group", None),
        P("group", None, None, None),
    )
    return jax.shard_map(on_device, mesh=mesh, in_specs=placed, out_specs=P(None, AXES), check_vma=False)
```
